32 devices in a mesh: groups: 2 (over y), leaf: 4 (over z), sample: 4 (over x, core).
Axes of the slice: x: 2, y: 2, z: 4, core: 2. Of those that a mesh axis runs over, the one named last changes fastest.
Arguments:
- points: bfloat16 [16384, 256], P(('groups', 'leaf', 'sample')), parts along dimension 0, may hold values from -40 to 40
- cotangent: bfloat16 [16384, 256], P(('groups', 'leaf', 'sample')), parts along dimension 0, may hold values from -6 to 6
- dest_pos: int32 [16384], P(('groups', 'leaf', 'sample')), parts along dimension 0, may hold values from 0 to 8191, as said below
- w_qkv: bfloat16 [256, 768], replicated, may hold values from -8 to 8
- w_out: bfloat16 [256, 256], replicated, may hold values from -0.375 to 0.375
- w_up: bfloat16 [256, 1024], replicated, may hold values from -0.375 to 0.375
- w_down: bfloat16 [1024, 256], replicated, may hold values from -0.1875 to 0.1875
- gain_attn: float32 [256], replicated, may hold values from 0.1 to 1.9
- gain_mlp: float32 [256], replicated, may hold values from 0.1 to 1.9
Outputs:
- grad_points: bfloat16 [16384, 256], P(('groups', 'leaf', 'sample')), parts along dimension 0
- grad_w_qkv: float32 [512, 768], P(('groups', 'leaf')), parts along dimension 0
- grad_w_out: float32 [512, 256], P(('groups', 'leaf')), parts along dimension 0
- grad_w_up: float32 [512, 1024], P(('groups', 'leaf')), parts along dimension 0
- grad_w_down: float32 [2048, 256], P(('groups', 'leaf')), parts along dimension 0
- grad_gain_attn: float32 [512], P(('groups', 'leaf')), parts along dimension 0
- grad_gain_mlp: float32 [512], P(('groups', 'leaf')), parts along dimension 0
The draws below stay inside these ranges and needn't reach their ends.
There are 2 independent parts, one for each index of `groups`. The reference program is written for one: setup_inputs(seed, part) draws one part's arguments, and reference() takes and returns one part's arrays. A program takes and returns all parts, laid end to end along the dimension named above; an argument that names none is the same for every part. Nothing has to cross between parts.
Inputs may be any that keep to these rules, and one draw needn't show every extreme that they name: `dest_pos`: a permutation of the 8192 positions; of the 512 points of one device, at most 64 have positions in any one aligned block of 512 positions, and in every draw some device reaches exactly 64 for some block.
All inputs are finite; a program needn't handle non-finite values.
Results may differ from the reference program's by a relative error of at most 0.0059.
The reference program's roundings to bfloat16 on the way count: a program that leaves them out, or rounds other values in their place, can miss the bound.
Values may be sent and summed in bfloat16 or wider, within the bound.
No kernel may reach another device: no remote copies, remote signals or barrier semaphores. Data moves between devices by JAX's collectives and lax.ppermute only.
A program may use at most 64 MiB of HBM per device.

```python
import math
import jax
import jax.numpy as jnp
from jax import lax

D = 256
HEADS = 8
FF = 1024
BALL = 256
PTS_DEV = 512
HEAD_DIM = 32
PEERS = 16
POINTS = 8192


def draw_points(key, part):
    key_base, key_rows, key_cols = jax.random.split(key, 3)
    row_scale = jnp.exp(jax.random.uniform(key_rows, (POINTS, 1), minval=0.0, maxval=math.log(10.0)))
    col_scale = jnp.exp(jax.random.uniform(key_cols, (1, D), minval=math.log(0.5), maxval=math.log(2.0)))
    base = jax.random.normal(key_base, (POINTS, D))
    return jnp.clip(base * row_scale * col_scale, -40.0, 40.0).astype(jnp.bfloat16)


def draw_w_qkv(key, part):
    key_base = jax.random.fold_in(key, 0)
    base = jax.random.normal(key_base, (D, 3 * D)) * D ** (-0.5)
    return jnp.clip(base, -8.0, 8.0).astype(jnp.bfloat16)


def pair_profile(first_key, second_key):
    half_pair = PTS_DEV // PEERS // 2
    offsets = jax.random.randint(first_key, (PEERS // 2,), 0, half_pair + 1).astype(jnp.int32)
    offsets = offsets.at[0].set(half_pair)
    paired = jnp.stack([half_pair + offsets, half_pair - offsets], axis=1).reshape(PEERS)
    return paired[jax.random.permutation(second_key, PEERS)]


def draw_dest_pos(key, part):
    keys_all = jax.random.split(key, 6)
    first_prof = pair_profile(keys_all[0], keys_all[1])
    second_prof = pair_profile(keys_all[2], keys_all[3])
    first_top = jnp.argmax(first_prof).astype(jnp.int32)
    second_top = jnp.argmax(second_prof).astype(jnp.int32)
    second_prof = jnp.where((first_top - second_top) % 2 == 0, second_prof, jnp.roll(second_prof, 1))
    source_dev = jnp.arange(PEERS, dtype=jnp.int32)[:, None]
    dest_dev = jnp.arange(PEERS, dtype=jnp.int32)[None, :]
    counts = first_prof[(dest_dev - source_dev) % PEERS] + second_prof[(dest_dev + source_dev) % PEERS]
    row_end = jnp.cumsum(counts, axis=1)
    row_start = row_end - counts
    col_start = jnp.cumsum(counts, axis=0) - counts
    local_rank = jnp.arange(PTS_DEV, dtype=jnp.int32)
    dest_of = jax.vmap(lambda row_ends: jnp.searchsorted(row_ends, local_rank, side='right'))(row_end).astype(jnp.int32)
    within = local_rank[None, :] - jnp.take_along_axis(row_start, dest_of, axis=1) + jnp.take_along_axis(col_start, dest_of, axis=1)
    shuffles = jax.vmap(lambda sub_key: jax.random.permutation(sub_key, PTS_DEV))(jax.random.split(keys_all[4], PEERS)).astype(jnp.int32)
    slot_local = shuffles[dest_of, within]
    positions = dest_of * PTS_DEV + slot_local
    src_perms = jax.vmap(lambda sub_key: jax.random.permutation(sub_key, PTS_DEV))(jax.random.split(keys_all[5], PEERS)).astype(jnp.int32)
    result = jnp.zeros((PEERS, PTS_DEV), jnp.int32).at[jnp.arange(PEERS, dtype=jnp.int32)[:, None], src_perms].set(positions)
    return result.reshape(POINTS).astype(jnp.int32)


def block_levels(stream_key, extent, cuts, smallest, largest):
    def one(dim, parts):
        steps = jax.random.uniform(jax.random.fold_in(jax.random.fold_in(stream_key, 6), dim), (parts,), jnp.float32, smallest / len(cuts), largest / len(cuts))
        return jnp.repeat(jnp.exp(steps), extent[dim] // parts).reshape((-1,) + (1,) * (len(extent) - dim - 1))

    level = one(*cuts[0])
    for cut in cuts[1:]:
        level = level * one(*cut)
    return level


def scatter_about(rng, shape, spread, reach, cuts=(), held_as=jnp.bfloat16):
    values = jax.random.normal(rng, shape, jnp.float32) * spread
    if len(cuts) > 0:
        values = block_levels(rng, shape, cuts, -0.22, 0.18) * values
    return jnp.clip(values, min=-reach, max=reach).astype(held_as)


def setup_inputs(seed: int = 0, part: int = 0) -> dict:
    seeds = jax.random.split(jax.random.key(seed), 10)
    own_keys = jax.random.split(jax.random.fold_in(seeds[9], part), 10)
    points = draw_points(jax.random.fold_in(jax.random.fold_in(seeds[9], part), 71), part)
    cotangent = scatter_about(own_keys[1], (POINTS, D), 1.0, 6.0, ((0, 16),))
    dest_pos = draw_dest_pos(jax.random.fold_in(jax.random.fold_in(seeds[9], part), 71), part)
    w_qkv = draw_w_qkv(jax.random.fold_in(seeds[9], 71), part)
    w_out = scatter_about(seeds[4], (D, D), D ** -0.5, 0.375)
    w_up = scatter_about(seeds[5], (D, FF), D ** -0.5, 0.375)
    w_down = scatter_about(seeds[6], (FF, D), FF ** -0.5, 0.1875)
    gain_attn = jnp.clip(1.0 + 0.18 * jax.random.normal(seeds[7], (D,), jnp.float32), 0.1, 1.9)
    gain_mlp = jnp.clip(1.0 + 0.18 * jax.random.normal(seeds[8], (D,), jnp.float32), 0.1, 1.9)
    return dict(points=points, cotangent=cotangent, dest_pos=dest_pos, w_qkv=w_qkv, w_out=w_out, w_up=w_up, w_down=w_down, gain_attn=gain_attn, gain_mlp=gain_mlp)


EPSILON = 1e-06
GELU_COEF = math.sqrt(2.0 / math.pi)

def to_low(matrix):
    return lax.optimization_barrier(matrix.astype(jnp.bfloat16))

def rms_scale(matrix):
    return lax.rsqrt(lax.optimization_barrier(jnp.mean(matrix * matrix, axis=1, keepdims=True)) + EPSILON)

def gelu_parts(pre_act):
    tanh_val = jnp.tanh(GELU_COEF * (pre_act + 0.044715 * pre_act * pre_act * pre_act))
    value = 0.5 * pre_act * (1.0 + tanh_val)
    slope = 0.5 * (1.0 + tanh_val) + 0.5 * pre_act * (1.0 - tanh_val * tanh_val) * GELU_COEF * (1.0 + 3.0 * 0.044715 * pre_act * pre_act)
    return (value, slope)

def ball_split(ball_block):
    ball_groups = ball_block.shape[0] // BALL
    split_parts = ball_block.astype(jnp.float32).reshape(ball_groups, BALL, 3, HEADS, HEAD_DIM)
    return (split_parts[:, :, 0], split_parts[:, :, 1], split_parts[:, :, 2])

def softmax_probs(queries, key_rows):
    scores = jnp.einsum('gqhd,gkhd->ghqk', queries, key_rows) * HEAD_DIM ** (-0.5)
    return jax.nn.softmax(scores, axis=-1)

def ball_forward(operands):
    queries, key_rows, values = ball_split(operands[0])
    probs_low = to_low(softmax_probs(queries, key_rows)).astype(jnp.float32)
    mixed = jnp.einsum('ghqk,gkhd->gqhd', probs_low, values)
    return mixed.reshape(-1, HEADS * HEAD_DIM).astype(jnp.bfloat16)

def ball_backward(operands):
    ball_block, grad_block = operands
    queries, key_rows, values = ball_split(ball_block)
    attn_probs = softmax_probs(queries, key_rows)
    probs_low = to_low(attn_probs).astype(jnp.float32)
    upstream = grad_block.astype(jnp.float32).reshape(queries.shape)
    grad_values = jnp.einsum('ghqk,gqhd->gkhd', probs_low, upstream)
    grad_probs = jnp.einsum('gqhd,gkhd->ghqk', upstream, values)
    row_delta = lax.optimization_barrier(jnp.sum(grad_probs * attn_probs, axis=-1, keepdims=True))
    grad_scores = to_low(attn_probs * (grad_probs - row_delta)).astype(jnp.float32)
    grad_queries = jnp.einsum('ghqk,gkhd->gqhd', grad_scores, key_rows) * HEAD_DIM ** (-0.5)
    grad_keys = jnp.einsum('ghqk,gqhd->gkhd', grad_scores, queries) * HEAD_DIM ** (-0.5)
    stacked = jnp.stack([grad_queries, grad_keys, grad_values], axis=2)
    return stacked.reshape(-1, 3 * HEADS * HEAD_DIM).astype(jnp.bfloat16)

def over_balls(function, operands):
    row_count = operands[0].shape[0]
    ball_count = row_count // BALL
    per_group = math.gcd(ball_count, max(1, 512 // BALL))
    shaped = tuple((operand.reshape(ball_count // per_group, per_group * BALL, operand.shape[1]) for operand in operands))
    result = lax.map(function, shaped)
    return result.reshape(row_count, result.shape[2])

def layer_grads(rotated, rot_cot, w_qkv, w_out, w_up, w_down, gain_attn, gain_mlp):
    rotated_f = rotated.astype(jnp.float32)
    scale_one = rms_scale(rotated_f)
    norm_one = rotated_f * scale_one
    normed_one = to_low(norm_one * gain_attn)
    qkv_rows = to_low(jnp.dot(normed_one, w_qkv, preferred_element_type=jnp.float32))
    attended = to_low(over_balls(ball_forward, (qkv_rows,)))
    middle = rotated_f + jnp.dot(attended, w_out, preferred_element_type=jnp.float32)
    scale_two = rms_scale(middle)
    norm_two = middle * scale_two
    normed_two = to_low(norm_two * gain_mlp)
    pre_act = jnp.dot(normed_two, w_up, preferred_element_type=jnp.float32)
    act_value, act_slope = gelu_parts(pre_act)
    hidden = to_low(act_value)
    grad_down = jnp.dot(hidden.T, rot_cot, preferred_element_type=jnp.float32)
    grad_pre = to_low(jnp.dot(rot_cot, w_down.T, preferred_element_type=jnp.float32) * act_slope)
    grad_up = jnp.dot(normed_two.T, grad_pre, preferred_element_type=jnp.float32)
    grad_normed_two = jnp.dot(grad_pre, w_up.T, preferred_element_type=jnp.float32)
    grad_gain_two = lax.optimization_barrier(jnp.sum(grad_normed_two * norm_two, axis=0))
    inner_two = grad_normed_two * gain_mlp
    grad_middle = rot_cot.astype(jnp.float32) + scale_two * (inner_two - norm_two * lax.optimization_barrier(jnp.mean(inner_two * norm_two, axis=1, keepdims=True)))
    grad_middle_low = to_low(grad_middle)
    grad_out = jnp.dot(attended.T, grad_middle_low, preferred_element_type=jnp.float32)
    grad_attended = to_low(jnp.dot(grad_middle_low, w_out.T, preferred_element_type=jnp.float32))
    grad_qkv_rows = to_low(over_balls(ball_backward, (qkv_rows, grad_attended)))
    grad_qkv = jnp.dot(normed_one.T, grad_qkv_rows, preferred_element_type=jnp.float32)
    grad_normed_one = jnp.dot(grad_qkv_rows, w_qkv.T, preferred_element_type=jnp.float32)
    grad_gain_one = lax.optimization_barrier(jnp.sum(grad_normed_one * norm_one, axis=0))
    inner_one = grad_normed_one * gain_attn
    grad_rot = grad_middle + scale_one * (inner_one - norm_one * lax.optimization_barrier(jnp.mean(inner_one * norm_one, axis=1, keepdims=True)))
    return (grad_rot, grad_qkv, grad_out, grad_up, grad_down, grad_gain_one, grad_gain_two)

def reference(points, cotangent, dest_pos, w_qkv, w_out, w_up, w_down, gain_attn, gain_mlp):
    rotated = jnp.zeros_like(points).at[dest_pos].set(points)
    rot_cot = jnp.zeros_like(cotangent).at[dest_pos].set(cotangent)
    grad_rot, grad_qkv, grad_out, grad_up, grad_down, grad_gain_one, grad_gain_two = layer_grads(rotated, rot_cot, w_qkv, w_out, w_up, w_down, gain_attn, gain_mlp)
    grad_points = grad_rot[dest_pos].astype(jnp.bfloat16)
    inv_root = 1.0 / math.sqrt(POINTS)
    return (grad_points, grad_qkv * inv_root, grad_out * inv_root, grad_up * inv_root, grad_down * inv_root, grad_gain_one * inv_root, grad_gain_two * inv_root)
```

```python
import functools
import math

import jax
import jax.numpy as jnp
from jax import lax
from jax.experimental import pallas as pl
from jax.experimental.pallas import tpu as pltpu
from jax.sharding import PartitionSpec as P

HEADS = 8
BALL = 256
HEAD_DIM = 32
GROUP = 128
META = 16

EPSILON = 1e-06
GELU_COEF = math.sqrt(2.0 / math.pi)
ATT_SCALE = HEAD_DIM ** (-0.5)
BF16 = jnp.bfloat16
F32 = jnp.float32


def mm(a, b):
    return lax.dot_general(a, b, (((1,), (0,)), ((), ())), preferred_element_type=F32)


def mm_nt(a, b):
    return lax.dot_general(a, b, (((1,), (1,)), ((), ())), preferred_element_type=F32)


def mm_tn(a, b):
    return lax.dot_general(a, b, (((0,), (0,)), ((), ())), preferred_element_type=F32)


def iota(shape, dim):
    return lax.broadcasted_iota(jnp.int32, shape, dim)


def one_hot(positions, shape, dim):
    return jnp.where(iota(shape, dim) == positions, 1.0, 0.0).astype(BF16)


def column_of(row):
    return jnp.broadcast_to(row, (128, row.shape[1])).T


def lane_tile(column, width):
    return jnp.concatenate([column] * (width // 128), axis=1)


class Arriving:
    def __init__(self, ref, copies):
        self.ref, self.copies, self.shape = ref, copies, ref.shape

    def __getitem__(self, where):
        for copy in self.copies:
            copy.wait()
        self.copies = []
        return self.ref[where]


class Leaving:
    def __init__(self, ref, out_ref, sems):
        self.ref, self.out_ref, self.sems, self.shape, self.dtype = ref, out_ref, sems, ref.shape, ref.dtype
        self.copies, self.sent = [], 0

    def __getitem__(self, where):
        return self.ref[where]

    def __setitem__(self, where, value):
        self.ref[where] = value

    def send(self, upto=None):
        upto = self.shape[0] if upto is None else upto
        if upto > self.sent:
            part = pl.ds(self.sent, upto - self.sent)
            copy = pltpu.make_async_copy(self.ref.at[part], self.out_ref.at[part], self.sems.at[len(self.copies)])
            copy.start()
            self.copies.append(copy)
            self.sent = upto


def send(ref, upto=None):
    if isinstance(ref, Leaving):
        ref.send(upto)


def pack_points_kernel(peers, cap, direct, dest_ref, points_ref, slot_ref, *out_refs):
    rows = points_ref.shape[0]
    slots = peers * cap
    dest = dest_ref[...]
    shift = rows.bit_length() - 1
    owner = lax.shift_right_logical(dest, shift)
    target = jnp.bitwise_and(dest, rows - 1)
    owned = jnp.where(iota((peers, rows), 0) == owner, 1.0, 0.0)
    upto = jnp.where(iota((rows, rows), 0) <= iota((rows, rows), 1), 1.0, 0.0).astype(BF16)
    counts = mm(owned.astype(BF16), upto)
    rank = (jnp.sum(counts * owned, axis=0, keepdims=True) - 1.0).astype(jnp.int32)
    slot = owner * cap + rank
    slot_ref[...] = slot
    packed = mm(one_hot(slot, (slots, rows), 0), points_ref[...]).astype(BF16)
    within = one_hot(rank, (cap, rows), 0)
    within = jnp.concatenate([within] * (128 // cap), axis=0)
    high = (lax.shift_right_logical(target, 4) + 1).astype(F32)
    low = jnp.bitwise_and(target, 15).astype(F32)
    high_rows = mm_nt((owned * high).astype(BF16), within)
    low_rows = mm_nt((owned * low).astype(BF16), within)
    if direct:
        (msg_ref,) = out_refs
        msg_ref[:, :cap, :] = packed[:, :128].reshape(peers, cap, 128)
        msg_ref[:, cap : 2 * cap, :] = packed[:, 128:].reshape(peers, cap, 128)
        first = iota((META, 128), 0) == 0
        for peer in range(peers):
            block = jnp.where(first, high_rows[peer : peer + 1], low_rows[peer : peer + 1])
            msg_ref[peer, 2 * cap :, :] = block.astype(BF16)
    else:
        packed_ref, high_ref, low_ref = out_refs
        packed_ref[...] = packed
        high_ref[...] = high_rows
        low_ref[...] = low_rows


def partner(step):
    return (lax.axis_index("leaf") * lax.axis_size("sample") + lax.axis_index("sample")) ^ step


def pack_cot_kernel(slot_ref, cot_ref, *refs):
    rows = cot_ref.shape[0]
    if len(refs) == 1:
        (packed_ref,) = refs
        packed_ref[...] = mm(one_hot(slot_ref[...], (packed_ref.shape[0], rows), 0), cot_ref[...]).astype(BF16)
        return
    *block_refs, packed_ref = refs
    peers, cap, width = packed_ref.shape
    packed = mm(one_hot(slot_ref[...], (peers * cap, rows), 0), cot_ref[...]).astype(BF16)
    packed_ref[...] = packed.reshape(peers, cap, width)
    for step, ref in enumerate(block_refs):
        for mate in range(2):
            ref[mate] = packed_ref[partner(2 * step + mate)]


def regroup_kernel(*refs):
    *pair_refs, mine_ref, mate_ref = refs
    for step, ref in enumerate(pair_refs):
        mine_ref[step] = ref[0]
        mate_ref[step] = ref[1]


def group_heads(rows):
    heads = range(GROUP // HEAD_DIM)
    return jnp.concatenate([head_rows(rows[h * HEAD_DIM : (h + 1) * HEAD_DIM], h) for h in heads], axis=1)


def head_rows(rows, head):
    width = rows.shape[1]
    at = (head * HEAD_DIM) % GROUP
    parts = []
    if at:
        parts.append(jnp.zeros((at, width), rows.dtype))
    parts.append(rows)
    if at + HEAD_DIM < GROUP:
        parts.append(jnp.zeros((GROUP - at - HEAD_DIM, width), rows.dtype))
    return jnp.concatenate(parts, axis=0)


def unpack_points_kernel(cap, peers, direct, *refs):
    if not direct:
        recv_ref, high_ref, low_ref = refs[:3]
        recv = recv_ref[...]
        high_rows, low_rows = high_ref[...], low_ref[...]
    else:
        msg_ref = refs[0]
        left = msg_ref[:, :cap, :].reshape(peers * cap, 128)
        right = msg_ref[:, cap : 2 * cap, :].reshape(peers * cap, 128)
        recv = jnp.concatenate([left, right], axis=1)
        tails = [msg_ref[peer, 2 * cap :, :].astype(F32) for peer in range(peers)]
        high_rows = jnp.concatenate([tail[0:1] for tail in tails], axis=0)
        low_rows = jnp.concatenate([tail[1:2] for tail in tails], axis=0)
    target_ref, target_col_ref, rotated_ref = refs[-3:]
    rows = rotated_ref.shape[1]
    slots = peers * cap
    targets = (high_rows - 1.0) * 16.0 + low_rows
    per_row = 128 // cap
    own_lane = iota((per_row, 128), 1) // cap == iota((per_row, 128), 0)
    pieces = []
    for group in range(slots // 128):
        block = targets[group * per_row : (group + 1) * per_row]
        pieces.append(jnp.sum(jnp.where(own_lane, block, 0.0), axis=0, keepdims=True))
    target = jnp.concatenate(pieces, axis=1)
    target_ref[...] = target.astype(jnp.int32)
    target_col_ref[...] = column_of(target).astype(jnp.int32)
    rotated_ref[...] = mm(one_hot(target.astype(jnp.int32), (rows, slots), 0), recv).T


def forward_kernel(
    rotated_ref, w_qkv_ref, w_out_ref, w_up_ref, gain_attn_ref, gain_mlp_ref,
    qkv_t_ref, kv_ref, scales_ref, norm_one_ref, normed_one_ref, attended_ref, norm_two_ref, normed_two_ref,
    hidden_ref, slope_ref, gain_attn_col_ref, gain_mlp_col_ref, *probs_refs,
):
    rot_t = rotated_ref[...]
    width, rows = rot_t.shape
    gain_attn_col = column_of(gain_attn_ref[...])
    gain_attn_col_ref[...] = gain_attn_col
    gain_mlp_col = column_of(gain_mlp_ref[...])
    gain_mlp_col_ref[...] = gain_mlp_col
    scale_one = lax.rsqrt(jnp.mean(rot_t * rot_t, axis=0, keepdims=True) + EPSILON)
    norm_one = rot_t * scale_one
    norm_one_ref[...] = norm_one
    normed_one = (norm_one * lane_tile(gain_attn_col, rows)).astype(BF16)
    normed_one_ref[...] = normed_one
    qkv_t = mm_tn(w_qkv_ref[...], normed_one).astype(BF16)
    qkv_t_ref[...] = qkv_t
    kv_ref[...] = qkv_t[width:].astype(F32).T.astype(BF16)

    for ball in range(rows // BALL):
        at = ball * BALL
        cols = slice(at, at + BALL)
        for group in range(0, width, GROUP):
            queries = group_heads(qkv_t_ref[group : group + GROUP, cols])
            scores = mm(kv_ref[cols, group : group + GROUP], queries) * ATT_SCALE
            top = jnp.max(scores, axis=0, keepdims=True)
            weights = jnp.exp(scores - top)
            probs = weights * (1.0 / jnp.sum(weights, axis=0, keepdims=True))
            probs_refs[ball][group // GROUP] = probs
            probs_low = probs.astype(BF16)
            for head in range(GROUP // HEAD_DIM):
                own = slice(group + head * HEAD_DIM, group + (head + 1) * HEAD_DIM)
                values = qkv_t_ref[2 * width + own.start : 2 * width + own.stop, cols]
                attended_ref[own, cols] = mm(values, probs_low[:, head * BALL : (head + 1) * BALL]).astype(BF16)

    middle = rot_t + mm_tn(w_out_ref[...], attended_ref[...])
    scale_two = lax.rsqrt(jnp.mean(middle * middle, axis=0, keepdims=True) + EPSILON)
    norm_two = middle * scale_two
    norm_two_ref[...] = norm_two
    normed_two = (norm_two * lane_tile(gain_mlp_col, rows)).astype(BF16)
    normed_two_ref[...] = normed_two
    scales_ref[...] = jnp.where(iota(scales_ref.shape, 0) == 0, scale_one, scale_two)
    step = 256
    for at in range(0, hidden_ref.shape[0], step):
        pre_act = mm_tn(w_up_ref[:, at : at + step], normed_two)
        square = pre_act * pre_act
        tanh_val = jnp.tanh(GELU_COEF * (pre_act + 0.044715 * pre_act * square))
        half = 0.5 * (1.0 + tanh_val)
        hidden_ref[at : at + step, :] = (pre_act * half).astype(BF16)
        slope_ref[at : at + step, :] = half + 0.5 * pre_act * (1.0 - tanh_val * tanh_val) * (
            GELU_COEF * (1.0 + 3.0 * 0.044715 * square)
        )


def norm_backward(grad_normed, norm, scale, gain):
    inner = grad_normed * gain
    return scale * (inner - norm * jnp.mean(inner * norm, axis=0, keepdims=True))


def gain_row(product):
    width = product.shape[1]
    partial = product[:, :128]
    for at in range(128, width, 128):
        partial = partial + product[:, at : at + 128]
    return jnp.sum(partial.T, axis=0, keepdims=True)


def place_blocks(blocks_ref, values, first_row, leaf_size, sample_size):
    step = values.shape[0] // (leaf_size * sample_size)
    for block in range(leaf_size * sample_size):
        leaf, sample = divmod(block, sample_size)
        blocks_ref[sample, leaf, first_row : first_row + step, :] = values[block * step : (block + 1) * step]


def part_blocks(blocks_ref, keep_ref, send_ref):
    low = lax.rem(lax.axis_index("sample"), 2)
    for high in range(keep_ref.shape[0]):
        keep_ref[high] = blocks_ref[2 * high + low]
        send_ref[high] = blocks_ref[2 * high + 1 - low].astype(BF16)


def mlp_weights_kernel(
    arranged, direct, target_ref, hidden_ref, slope_ref, normed_two_ref, w_down_ref, *refs
):
    width, rows = normed_two_ref.shape
    if direct:
        mine_ref, mate_ref, *refs, landing_ref = refs
        for step in range(mine_ref.shape[0]):
            landing_ref[partner(2 * step)] = mine_ref[step]
            landing_ref[partner(2 * step + 1)] = mate_ref[step]
        recv_ref = landing_ref
    else:
        recv_ref, *refs = refs
    grad_pre_ref, cot_t_ref, *mat_refs = refs
    recv = recv_ref[...].reshape(-1, width)
    cot_f = mm(one_hot(target_ref[...], (rows, recv.shape[0]), 0), recv)
    cot = cot_f.astype(BF16)
    cot_t = cot_f.T
    cot_t_ref[...] = cot_t
    cot_t_low = cot_t.astype(BF16)
    normed_two = normed_two_ref[...]
    step = 256
    if arranged:
        keep_ref, send_ref, blocks_ref = mat_refs
        leaf_size, sample_size = lax.axis_size("leaf"), lax.axis_size("sample")
        up_rows = width // leaf_size
        down_rows = hidden_ref.shape[0] // (leaf_size * sample_size)
    else:
        grad_up_ref, grad_down_ref = mat_refs
    for at in range(0, hidden_ref.shape[0], step):
        grad_down = mm(hidden_ref[at : at + step, :], cot)
        grad_pre = (mm(w_down_ref[at : at + step, :], cot_t_low) * slope_ref[at : at + step, :]).astype(BF16)
        grad_pre_ref[at : at + step, :] = grad_pre
        grad_up = mm_nt(normed_two, grad_pre)
        if arranged:
            for leaf in range(leaf_size):
                blocks_ref[at // step, leaf, :up_rows, :] = grad_up[leaf * up_rows : (leaf + 1) * up_rows]
            for block in range(step // down_rows):
                leaf, sample = divmod(at // down_rows + block, sample_size)
                piece = grad_down[block * down_rows : (block + 1) * down_rows]
                blocks_ref[sample, leaf, up_rows:, :] = piece
        else:
            grad_down_ref[at : at + step, :] = grad_down.astype(BF16)
            grad_up_ref[:, at : at + step] = grad_up.astype(BF16)
    if arranged:
        part_blocks(blocks_ref, keep_ref, send_ref)


def mlp_inputs_kernel(
    grad_pre_ref, cot_t_ref, norm_two_ref, scales_ref, attended_ref, w_up_ref, w_out_ref, gain_mlp_ref,
    grad_gain_ref, grad_middle_ref, grad_att_ref, grad_out_ref,
):
    grad_normed = mm(w_up_ref[...], grad_pre_ref[...])
    norm_two = norm_two_ref[...]
    grad_gain_ref[...] = gain_row(grad_normed * norm_two)
    gain = lane_tile(gain_mlp_ref[...], norm_two.shape[1])
    grad_middle = cot_t_ref[...] + norm_backward(grad_normed, norm_two, scales_ref[1:2, :], gain)
    grad_middle_ref[...] = grad_middle
    grad_middle_low = grad_middle.astype(BF16)
    grad_att_ref[...] = mm(w_out_ref[...], grad_middle_low).astype(BF16)
    grad_out_ref[...] = mm_nt(attended_ref[...], grad_middle_low)


def ball_backward(ball, qkv_t_ref, kv_ref, probs_ref, grad_att_ref, grad_rows_ref):
    width = qkv_t_ref.shape[0] // 3
    cols = slice(ball * BALL, (ball + 1) * BALL)
    for group in range(0, width, GROUP):
        upstream = grad_att_ref[group : group + GROUP, cols]
        probs = probs_ref[group // GROUP]
        grad_probs = mm(kv_ref[cols, width + group : width + group + GROUP], group_heads(upstream))
        delta = jnp.sum(grad_probs * probs, axis=0, keepdims=True)
        grad_scores = (probs * (grad_probs - delta)).astype(BF16)
        probs_low = probs.astype(BF16)
        for head in range(GROUP // HEAD_DIM):
            first = group + head * HEAD_DIM
            own, own_key, own_value = (slice(at + first, at + first + HEAD_DIM) for at in (0, width, 2 * width))
            part = slice(head * BALL, (head + 1) * BALL)
            scores_of = grad_scores[:, part]
            grad_rows_ref[own, cols] = (mm(qkv_t_ref[own_key, cols], scores_of) * ATT_SCALE).astype(BF16)
            grad_rows_ref[own_key, cols] = (mm_nt(qkv_t_ref[own, cols], scores_of) * ATT_SCALE).astype(BF16)
            grad_rows_ref[own_value, cols] = mm_nt(grad_att_ref[own, cols], probs_low[:, part]).astype(BF16)


def attention_backward_kernel(
    arranged,
    qkv_t_ref, kv_ref, scales_ref, grad_att_ref, grad_middle_ref, norm_one_ref, normed_one_ref,
    w_qkv_ref, gain_attn_ref, target_col_ref, gain_two_ref, grad_out_ref, *refs,
):
    width, rows = norm_one_ref.shape
    probs_refs, refs = refs[: rows // BALL], refs[rows // BALL :]
    back_ref, *mat_refs, grad_rows_ref = refs
    for ball, probs_ref in enumerate(probs_refs):
        ball_backward(ball, qkv_t_ref, kv_ref, probs_ref, grad_att_ref, grad_rows_ref)
    grad_rows = grad_rows_ref[...]
    grad_normed = mm(w_qkv_ref[...], grad_rows)
    norm_one = norm_one_ref[...]
    gain_one = gain_row(grad_normed * norm_one)
    gain = lane_tile(gain_attn_ref[...], rows)
    grad_rot = grad_middle_ref[...] + norm_backward(grad_normed, norm_one, scales_ref[0:1, :], gain)
    place = one_hot(lane_tile(target_col_ref[...], rows), (back_ref.shape[0], rows), 1)
    back_ref[...] = mm_nt(place, grad_rot.astype(BF16)).astype(BF16)
    normed_one = normed_one_ref[...]
    if not arranged:
        mat_refs[0][...] = mm_nt(normed_one, grad_rows).astype(BF16)
        mat_refs[1][...] = gain_one
        return
    keep_ref, send_ref, blocks_ref = mat_refs
    leaf_size, sample_size = lax.axis_size("leaf"), lax.axis_size("sample")
    step = width // (leaf_size * sample_size)
    for col in range(3):
        grad_qkv = mm_nt(normed_one, grad_rows[col * width : (col + 1) * width])
        place_blocks(blocks_ref, grad_qkv, (1 + col) * step, leaf_size, sample_size)
    place_blocks(blocks_ref, grad_out_ref[...], 0, leaf_size, sample_size)
    row = iota((META, width), 0)
    gains = jnp.where(row == 0, gain_one, jnp.where(row == 1, gain_two_ref[...], 0.0))
    for sample in range(sample_size):
        for leaf in range(leaf_size):
            blocks_ref[sample, leaf, 4 * step :, :] = gains
    part_blocks(blocks_ref, keep_ref, send_ref)


def unpack_kernel(slot_ref, returned_ref, out_ref):
    slots = returned_ref.shape[0]
    slot_col = column_of(slot_ref[...].astype(F32)).astype(jnp.int32)
    place = one_hot(lane_tile(slot_col, slots), (out_ref.shape[0], slots), 1)
    out_ref[...] = mm(place, returned_ref[...]).astype(BF16)


def halve_kernel(axis, bit, keep_ref, got_ref, keep_out_ref, send_out_ref):
    mine = lax.rem(lax.div(lax.axis_index(axis), bit), 2)
    for high in range(keep_out_ref.shape[0]):
        for ref, at in ((keep_out_ref, 2 * high + mine), (send_out_ref, 2 * high + 1 - mine)):
            ref[high] = (keep_ref[at] + got_ref[at].astype(F32)).astype(ref.dtype)


def finish_kernel(pairs, *refs):
    ins, (low_ref, gains_ref) = refs[: 2 * pairs], refs[2 * pairs :]
    start = 0
    for pair in range(pairs):
        total = ins[2 * pair][0] + ins[2 * pair + 1][0].astype(F32)
        if pair == pairs - 1:
            gains_ref[...] = total[-META:]
            total = total[:-META]
        low_ref[0, start : start + total.shape[0], :] = total.astype(BF16)
        start += total.shape[0]


def assemble_kernel(scale, offsets, gains_ref, mine_ref, mate_ref, up_ref, down_ref, out_ref, qkv_ref, gain_out_ref):
    size = 2 * len(offsets)
    width = mine_ref.shape[2]
    up_rows, down_rows, out_rows = up_ref.shape[0], down_ref.shape[0] // size, out_ref.shape[0] // size
    me = lax.axis_index("sample")

    def block(source, count):
        return pl.ds(pl.multiple_of(source * count, count), count)

    for index, offset in enumerate(offsets):
        for mate, ref in enumerate((mine_ref, mate_ref)):
            source = me ^ (offset + mate)
            part = ref[index].astype(F32) * scale
            at = up_rows
            up_ref[:, block(source, width)] = part[:at]
            down_ref[block(source, down_rows), :] = part[at : at + down_rows]
            at += down_rows
            out_ref[block(source, out_rows), :] = part[at : at + out_rows]
            at += out_rows
            for col in range(3):
                qkv_ref[block(source, out_rows), col * width : (col + 1) * width] = part[at : at + out_rows]
                at += out_rows
    gain_out_ref[...] = gains_ref[...] * scale


def permute(value, axis, size, bit):
    return lax.ppermute(value, axis, [(i, i ^ bit) for i in range(size)])


def halve(keep, got, axis, bit, name):
    shape = (keep.shape[0] // 2,) + keep.shape[1:]
    return call(functools.partial(halve_kernel, axis, bit), [(shape, F32), (shape, BF16)], name, 0.5, keep, got)


def halve_leaf(keep, got, name):
    leaf_size = lax.axis_size("leaf")
    keep, got = keep[0], got[0]
    bit = 1
    while bit < leaf_size:
        keep, leaving = halve(keep, got, "leaf", bit, name)
        got = permute(leaving, "leaf", leaf_size, bit)
        bit *= 2
    return keep, got


def call(kernel, outs, name, micros, *args, scratch=(), hbm_in=False, hbm_out=False, raw_in=0, raw_out=0, blocked=False, limit=16):
    moved = sum(arg.size * arg.dtype.itemsize for arg in args)
    moved += sum(math.prod(shape) * jnp.dtype(dtype).itemsize for shape, dtype in outs)
    vmem = pl.BlockSpec() if blocked else pl.BlockSpec(memory_space=pltpu.VMEM)
    hbm = pl.BlockSpec(memory_space=pltpu.HBM)
    copied_in = len(args) - raw_in if hbm_in else 0
    copied_out = len(outs) - raw_out if hbm_out else 0
    parts = 2

    def body(*refs):
        ins, refs = list(refs[: len(args)]), refs[len(args) :]
        results, refs = list(refs[: len(outs)]), refs[len(outs) :]
        own, refs = refs[: len(scratch)], refs[len(scratch) :]
        in_bufs, refs = refs[:copied_in], refs[copied_in:]
        out_bufs, refs = refs[:copied_out], refs[copied_out:]
        for at, buf in enumerate(in_bufs):
            copy = pltpu.make_async_copy(ins[at], buf, refs[0].at[at])
            copy.start()
            ins[at] = Arriving(buf, [copy])
        for at, buf in enumerate(out_bufs):
            results[at] = Leaving(buf, results[at], refs[-1].at[at])
        kernel(*ins, *results, *own)
        for ref in ins:
            if isinstance(ref, Arriving):
                for copy in ref.copies:
                    copy.wait()
        for ref in results[:copied_out]:
            ref.send()
        for ref in results[:copied_out]:
            for copy in ref.copies:
                copy.wait()

    extra = [pltpu.VMEM(arg.shape, arg.dtype) for arg in args[:copied_in]]
    extra += [pltpu.VMEM(shape, dtype) for shape, dtype in outs[:copied_out]]
    if copied_in:
        extra.append(pltpu.SemaphoreType.DMA((copied_in,)))
    if copied_out:
        extra.append(pltpu.SemaphoreType.DMA((copied_out, parts)))
    return pl.pallas_call(
        body,
        out_shape=[jax.ShapeDtypeStruct(shape, dtype) for shape, dtype in outs],
        in_specs=[hbm if hbm_in else vmem] * (len(args) - raw_in) + [hbm] * raw_in,
        out_specs=[hbm if hbm_out else vmem] * (len(outs) - raw_out) + [hbm] * raw_out,
        scratch_shapes=list(scratch) + extra,
        compiler_params=pltpu.CompilerParams(vmem_limit_bytes=limit * 1024 * 1024),
        cost_estimate=pl.CostEstimate(flops=int(micros * 1.1e9), bytes_accessed=moved, transcendentals=0),
        name=name,
    )(*args)


def exchange(flat, axes, peers):
    moved = lax.all_to_all(
        flat.reshape((peers, -1) + flat.shape[1:]), axes, split_axis=0, concat_axis=0, tiled=True
    )
    return moved.reshape(flat.shape)


def local(points, cotangent, dest_pos, w_qkv, w_out, w_up, w_down, gain_attn, gain_mlp):
    rows, width = points.shape
    hidden_width = w_up.shape[1]
    axes = ("leaf", "sample")
    peers = lax.axis_size(axes)
    leaf_size, sample_size = lax.axis_size("leaf"), lax.axis_size("sample")
    cap = 2 * rows // peers
    slots = peers * cap
    balls = rows // BALL
    direct = cap % 16 == 0
    paired = leaf_size & (leaf_size - 1) == 0 and sample_size & (sample_size - 1) == 0 and sample_size > 1
    arranged = paired and width % (16 * peers) == 0 and hidden_width == sample_size * width and leaf_size <= 8
    inv_root = 1.0 / math.sqrt(rows * peers)

    msg_rows = 2 * cap + META
    if direct:
        outs = [((peers, msg_rows, 128), BF16)]
    else:
        outs = [((slots, width), BF16), ((peers, 128), F32), ((peers, 128), F32)]
    slot, *message = call(
        functools.partial(pack_points_kernel, peers, cap, direct),
        [((1, rows), jnp.int32)] + outs, "pack_points", 2, dest_pos.reshape(1, rows), points, hbm_in=True, hbm_out=True, limit=60,
    )
    if direct:
        forward_args = [exchange(message[0].reshape(-1, 128), axes, peers).reshape(peers, msg_rows, 128)]
    else:
        packed, high, low = message
        tail = jnp.stack([high, low], axis=1).astype(BF16)
        halves = packed.reshape(peers, cap, 2, 128).transpose(0, 2, 1, 3).reshape(peers, 2 * cap, 128)
        flat = jnp.concatenate([halves, tail], axis=1).reshape(-1, 128)
        arrived = exchange(flat, axes, peers).reshape(peers, 2 * cap + 2, 128)
        halves = arrived[:, : 2 * cap].reshape(peers, 2, cap, 128).transpose(0, 2, 1, 3).reshape(slots, width)
        forward_args = [halves, arrived[:, 2 * cap].astype(F32), arrived[:, 2 * cap + 1].astype(F32)]
    by_permute = direct and paired and peers <= 16
    if by_permute:
        packed_cot = call(
            pack_cot_kernel, [((2, cap, width), BF16)] * (peers // 2), "pack_cot", 1, slot, cotangent,
            scratch=[pltpu.VMEM((peers, cap, width), BF16)],
        )
        pairs = [packed_cot[0]] + [permute(packed_cot[step], axes, peers, 2 * step) for step in range(1, peers // 2)]
        *pairs[1:3], forward_args[0] = lax.optimization_barrier((*pairs[1:3], forward_args[0]))
    else:
        (packed_cot,) = call(pack_cot_kernel, [((slots, width), BF16)], "pack_cot", 1, slot, cotangent)
        arrived_cot = [exchange(packed_cot, axes, peers)]
    target, target_col, rotated = call(
        functools.partial(unpack_points_kernel, cap, peers, direct),
        [((1, slots), jnp.int32), ((slots, 128), jnp.int32), ((width, rows), F32)],
        "unpack_points", 2, *forward_args,
    )
    (
        qkv_t, kv, scales, norm_one, normed_one, attended, norm_two, normed_two, hidden, slope,
        gain_attn_col, gain_mlp_col, *probs,
    ) = call(
        forward_kernel,
        [
            ((3 * width, rows), BF16), ((rows, 2 * width), BF16), ((8, rows), F32),
            ((width, rows), F32), ((width, rows), BF16), ((width, rows), BF16),
            ((width, rows), F32), ((width, rows), BF16),
            ((hidden_width, rows), BF16), ((hidden_width, rows), F32), ((width, 128), F32), ((width, 128), F32),
        ] + [((width // GROUP, BALL, GROUP // HEAD_DIM * BALL), F32)] * balls,
        "forward", 7, rotated, w_qkv, w_out, w_up, gain_attn.reshape(1, width), gain_mlp.reshape(1, width),
    )
    if by_permute:
        scales, *pairs = lax.optimization_barrier((scales, *pairs))
        half = ((peers // 2, cap, width), BF16)
        mine, for_mate = call(regroup_kernel, [half] * 2, "regroup", 0.3, *pairs)
        arrived_cot = [mine, permute(for_mate, axes, peers, 1)]
    mlp_scratch, qkv_scratch = [], []
    if arranged:
        halved = (sample_size // 2, leaf_size)
        mlp_rows = width // leaf_size + hidden_width // peers
        qkv_rows = 4 * width // peers + META
        mlp_mats = [(halved + (mlp_rows, width), F32), (halved + (mlp_rows, width), BF16)]
        qkv_mats = [(halved + (qkv_rows, width), F32), (halved + (qkv_rows, width), BF16)]
        mlp_scratch = [pltpu.VMEM((sample_size, leaf_size, mlp_rows, width), F32)]
        qkv_scratch = [pltpu.VMEM((sample_size, leaf_size, qkv_rows, width), F32)]
    else:
        mlp_mats = [(w_up.shape, BF16), (w_down.shape, BF16)]
        qkv_mats = [(w_qkv.shape, BF16), ((1, width), F32)]
    grad_pre, cot_t, *mlp_grads = call(
        functools.partial(mlp_weights_kernel, arranged, by_permute),
        [((hidden_width, rows), BF16), ((width, rows), F32)] + mlp_mats,
        "mlp_weights", 2.5, target, hidden, slope, normed_two, w_down, *arrived_cot,
        scratch=mlp_scratch + ([pltpu.VMEM((peers, cap, width), BF16)] if by_permute else []),
    )
    gain_two, grad_middle, grad_att, grad_out = call(
        mlp_inputs_kernel,
        [((1, width), F32), ((width, rows), F32), ((width, rows), BF16), ((width, width), F32)],
        "mlp_inputs", 1.5, grad_pre, cot_t, norm_two, scales, attended, w_up, w_out, gain_mlp_col,
    )
    if arranged:
        keep_mlp, send_mlp = mlp_grads
        got_mlp = permute(send_mlp, "sample", sample_size, 1)
        bit = 2
        while bit < sample_size:
            keep_mlp, send_mlp = halve(keep_mlp, got_mlp, "sample", bit, "halve_mlp")
            grad_att, send_mlp = lax.optimization_barrier((grad_att, send_mlp))
            got_mlp = permute(send_mlp, "sample", sample_size, bit)
            bit *= 2
    back, *qkv_grads = call(
        functools.partial(attention_backward_kernel, arranged),
        [((slots, width), BF16)] + qkv_mats, "attention_backward", 6,
        qkv_t, kv, scales, grad_att, grad_middle, norm_one, normed_one,
        w_qkv, gain_attn_col, target_col, gain_two, grad_out, *probs,
        scratch=qkv_scratch + [pltpu.VMEM((3 * width, rows), BF16)],
    )
    if arranged:
        back, got_mlp = lax.optimization_barrier((back, got_mlp))
    returned = exchange(back, axes, peers)
    (grad_points,) = call(unpack_kernel, [((rows, width), BF16)], "unpack", 1, slot, returned, blocked=True)
    if not arranged:
        up_sum, down_sum, out_sum = reduce_mats([*mlp_grads, grad_out])
        qkv_sum, gain_sum = reduce_mats([qkv_grads[0]], jnp.concatenate([qkv_grads[1], gain_two], axis=0))
        return (
            grad_points, qkv_sum * inv_root, out_sum * inv_root, up_sum * inv_root, down_sum * inv_root,
            gain_sum[0] * inv_root, gain_sum[1] * inv_root,
        )
    keep_qkv, send_qkv = qkv_grads
    got_qkv = permute(send_qkv, "sample", sample_size, 1)
    bit = 2
    while bit < sample_size:
        keep_qkv, send_qkv = halve(keep_qkv, got_qkv, "sample", bit, "halve_qkv")
        got_qkv = permute(send_qkv, "sample", sample_size, bit)
        bit *= 2
    low, gains = call(
        functools.partial(finish_kernel, 2),
        [((1, mlp_rows + qkv_rows - META, width), BF16), ((META, width), F32)], "finish", 0.5,
        *halve_leaf(keep_mlp, got_mlp, "leaf_mlp"), *halve_leaf(keep_qkv, got_qkv, "leaf_qkv"),
    )
    offsets = [0]
    bit = sample_size // 2
    while bit > 1:
        low = jnp.concatenate([low, permute(low, "sample", sample_size, bit)], axis=0)
        offsets += [offset ^ bit for offset in offsets]
        bit //= 2
    mate = permute(low, "sample", sample_size, 1)
    grad_points, gains = lax.optimization_barrier((grad_points, gains))
    share = width // leaf_size
    up_sum, down_sum, out_sum, qkv_sum, gain_sum = call(
        functools.partial(assemble_kernel, inv_root, offsets),
        [
            ((share, hidden_width), F32), ((hidden_width // leaf_size, width), F32), ((share, width), F32),
            ((share, 3 * width), F32), ((META, width), F32),
        ],
        "assemble", 1, gains, low, mate, blocked=True,
    )
    gains = lax.dynamic_slice(gain_sum, (0, lax.axis_index("leaf") * share), (2, share))
    return (grad_points, qkv_sum, out_sum, up_sum, down_sum, gains[0], gains[1])


def reduce_mats(mats, gains=None):
    leaf_size = lax.axis_size("leaf")
    sample_size = lax.axis_size("sample")
    me = lax.axis_index("sample")
    pieces = []
    for mat in mats:
        pieces.append(mat.reshape(leaf_size, sample_size, -1, 128).transpose(1, 0, 2, 3))
    if gains is not None:
        gain_block = gains.reshape(2, leaf_size, -1).transpose(1, 0, 2).reshape(1, leaf_size, 1, -1)
        gain_block = jnp.pad(gain_block, ((0, 0), (0, 0), (0, 15), (0, 128 - gain_block.shape[3])))
        pieces.append(jnp.broadcast_to(gain_block, (sample_size,) + gain_block.shape[1:]))
    current = jnp.concatenate(pieces, axis=2).astype(jnp.bfloat16)
    bit = 1
    while bit < sample_size:
        split = current.reshape((current.shape[0] // 2, 2) + current.shape[1:])
        mine = (me // bit) % 2
        keep = lax.dynamic_index_in_dim(split, mine, 1, keepdims=False)
        send = lax.dynamic_index_in_dim(split, 1 - mine, 1, keepdims=False)
        got = lax.ppermute(send, "sample", [(i, i ^ bit) for i in range(sample_size)])
        current = (keep.astype(jnp.float32) + got.astype(jnp.float32)).astype(jnp.bfloat16)
        bit *= 2
    current = lax.all_to_all(current[0], "leaf", split_axis=0, concat_axis=0, tiled=True)
    total = jnp.sum(current.astype(jnp.float32), axis=0)
    low = total.astype(jnp.bfloat16)
    gathered = jnp.zeros((sample_size,) + low.shape, jnp.bfloat16)
    for step in range(sample_size):
        got = low if step == 0 else lax.ppermute(low, "sample", [(i, i ^ step) for i in range(sample_size)])
        gathered = lax.dynamic_update_index_in_dim(gathered, got, me ^ step, 0)
    results = []
    start = 0
    for mat in mats:
        rows = mat.size // (leaf_size * sample_size * 128)
        part = gathered[:, start : start + rows].astype(jnp.float32)
        results.append(part.reshape(mat.shape[0] // leaf_size, mat.shape[1]))
        start += rows
    if gains is not None:
        width = gains.shape[1] // leaf_size
        results.append(total[start, : 2 * width].reshape(2, width))
    return results


def solution(mesh):
    in_specs = (
        P(("groups", "leaf", "sample"), None),
        P(("groups", "leaf", "sample"), None),
        P(("groups", "leaf", "sample")),
        P(),
        P(),
        P(),
        P(),
        P(),
        P(),
    )
    out_specs = (
        P(("groups", "leaf", "sample"), None),
        P(("groups", "leaf"), None),
        P(("groups", "leaf"), None),
        P(("groups", "leaf"), None),
        P(("groups", "leaf"), None),
        P(("groups", "leaf")),
        P(("groups", "leaf")),
    )
    return jax.shard_map(local, mesh=mesh, in_specs=in_specs, out_specs=out_specs, check_vma=False)
```

```python
import functools
import math

import jax
import jax.numpy as jnp
from jax import lax
from jax.experimental import pallas as pl
from jax.experimental.pallas import tpu as pltpu
from jax.sharding import PartitionSpec as P

HEADS = 8
BALL = 256
HEAD_DIM = 32
GROUP = 128
META = 16
GAINS = 8

EPSILON = 1e-06
GELU_COEF = math.sqrt(2.0 / math.pi)
ATT_SCALE = HEAD_DIM ** (-0.5)
BF16 = jnp.bfloat16
F32 = jnp.float32


def mm(a, b):
    return lax.dot_general(a, b, (((1,), (0,)), ((), ())), preferred_element_type=F32)


def mm_nt(a, b):
    return lax.dot_general(a, b, (((1,), (1,)), ((), ())), preferred_element_type=F32)


def mm_tn(a, b):
    return lax.dot_general(a, b, (((0,), (0,)), ((), ())), preferred_element_type=F32)


def iota(shape, dim):
    return lax.broadcasted_iota(jnp.int32, shape, dim)


def one_hot(positions, shape, dim):
    return jnp.where(iota(shape, dim) == positions, 1.0, 0.0).astype(BF16)


def column_of(row):
    return jnp.broadcast_to(row, (128, row.shape[1])).T


def lane_tile(column, width):
    return jnp.concatenate([column] * (width // 128), axis=1)


class Arriving:
    def __init__(self, ref, copies):
        self.ref, self.copies, self.shape = ref, copies, ref.shape

    def __getitem__(self, where):
        for copy in self.copies:
            copy.wait()
        self.copies = []
        return self.ref[where]


class Leaving:
    def __init__(self, ref, out_ref, sems):
        self.ref, self.out_ref, self.sems, self.shape, self.dtype = ref, out_ref, sems, ref.shape, ref.dtype
        self.copies, self.sent = [], 0

    def __getitem__(self, where):
        return self.ref[where]

    def __setitem__(self, where, value):
        self.ref[where] = value

    def send(self, upto=None):
        upto = self.shape[0] if upto is None else upto
        if upto > self.sent:
            part = pl.ds(self.sent, upto - self.sent)
            copy = pltpu.make_async_copy(self.ref.at[part], self.out_ref.at[part], self.sems.at[len(self.copies)])
            copy.start()
            self.copies.append(copy)
            self.sent = upto


def send(ref, upto=None):
    if isinstance(ref, Leaving):
        ref.send(upto)


def pack_points_kernel(peers, cap, direct, dest_ref, points_ref, slot_ref, *out_refs):
    rows = points_ref.shape[0]
    slots = peers * cap
    dest = dest_ref[...]
    shift = rows.bit_length() - 1
    owner = lax.shift_right_logical(dest, shift)
    target = jnp.bitwise_and(dest, rows - 1)
    owned = jnp.where(iota((peers, rows), 0) == owner, 1.0, 0.0)
    upto = jnp.where(iota((rows, rows), 0) <= iota((rows, rows), 1), 1.0, 0.0).astype(BF16)
    counts = mm(owned.astype(BF16), upto)
    rank = (jnp.sum(counts * owned, axis=0, keepdims=True) - 1.0).astype(jnp.int32)
    slot = owner * cap + rank
    slot_ref[...] = slot
    packed = mm(one_hot(slot, (slots, rows), 0), points_ref[...]).astype(BF16)
    within = one_hot(rank, (cap, rows), 0)
    within = jnp.concatenate([within] * (128 // cap), axis=0)
    high = (lax.shift_right_logical(target, 4) + 1).astype(F32)
    low = jnp.bitwise_and(target, 15).astype(F32)
    high_rows = mm_nt((owned * high).astype(BF16), within)
    low_rows = mm_nt((owned * low).astype(BF16), within)
    if direct:
        (msg_ref,) = out_refs
        msg_ref[:, :cap, :] = packed[:, :128].reshape(peers, cap, 128)
        msg_ref[:, cap : 2 * cap, :] = packed[:, 128:].reshape(peers, cap, 128)
        first = iota((META, 128), 0) == 0
        for peer in range(peers):
            block = jnp.where(first, high_rows[peer : peer + 1], low_rows[peer : peer + 1])
            msg_ref[peer, 2 * cap :, :] = block.astype(BF16)
    else:
        packed_ref, high_ref, low_ref = out_refs
        packed_ref[...] = packed
        high_ref[...] = high_rows
        low_ref[...] = low_rows


def partner(step):
    return (lax.axis_index("leaf") * lax.axis_size("sample") + lax.axis_index("sample")) ^ step


def pack_cot_kernel(slot_ref, cot_ref, *refs):
    rows = cot_ref.shape[0]
    if len(refs) == 1:
        (packed_ref,) = refs
        packed_ref[...] = mm(one_hot(slot_ref[...], (packed_ref.shape[0], rows), 0), cot_ref[...]).astype(BF16)
        return
    *block_refs, packed_ref = refs
    peers, cap, width = packed_ref.shape
    packed = mm(one_hot(slot_ref[...], (peers * cap, rows), 0), cot_ref[...]).astype(BF16)
    packed_ref[...] = packed.reshape(peers, cap, width)
    for step, ref in enumerate(block_refs):
        for mate in range(2):
            ref[mate] = packed_ref[partner(2 * step + mate)]


def regroup_kernel(*refs):
    *pair_refs, mine_ref, mate_ref = refs
    for step, ref in enumerate(pair_refs):
        mine_ref[step] = ref[0]
        mate_ref[step] = ref[1]


def group_heads(rows):
    heads = range(GROUP // HEAD_DIM)
    return jnp.concatenate([head_rows(rows[h * HEAD_DIM : (h + 1) * HEAD_DIM], h) for h in heads], axis=1)


def head_rows(rows, head):
    width = rows.shape[1]
    at = (head * HEAD_DIM) % GROUP
    parts = []
    if at:
        parts.append(jnp.zeros((at, width), rows.dtype))
    parts.append(rows)
    if at + HEAD_DIM < GROUP:
        parts.append(jnp.zeros((GROUP - at - HEAD_DIM, width), rows.dtype))
    return jnp.concatenate(parts, axis=0)


def unpack_points_kernel(cap, peers, direct, *refs):
    if not direct:
        recv_ref, high_ref, low_ref = refs[:3]
        recv = recv_ref[...]
        high_rows, low_rows = high_ref[...], low_ref[...]
    else:
        msg_ref = refs[0]
        left = msg_ref[:, :cap, :].reshape(peers * cap, 128)
        right = msg_ref[:, cap : 2 * cap, :].reshape(peers * cap, 128)
        recv = jnp.concatenate([left, right], axis=1)
        tails = [msg_ref[peer, 2 * cap :, :].astype(F32) for peer in range(peers)]
        high_rows = jnp.concatenate([tail[0:1] for tail in tails], axis=0)
        low_rows = jnp.concatenate([tail[1:2] for tail in tails], axis=0)
    target_ref, target_col_ref, rotated_ref = refs[-3:]
    rows = rotated_ref.shape[1]
    slots = peers * cap
    targets = (high_rows - 1.0) * 16.0 + low_rows
    per_row = 128 // cap
    own_lane = iota((per_row, 128), 1) // cap == iota((per_row, 128), 0)
    pieces = []
    for group in range(slots // 128):
        block = targets[group * per_row : (group + 1) * per_row]
        pieces.append(jnp.sum(jnp.where(own_lane, block, 0.0), axis=0, keepdims=True))
    target = jnp.concatenate(pieces, axis=1)
    target_ref[...] = target.astype(jnp.int32)
    target_col_ref[...] = column_of(target).astype(jnp.int32)
    rotated_ref[...] = mm(one_hot(target.astype(jnp.int32), (rows, slots), 0), recv).T


def forward_kernel(
    rotated_ref, w_qkv_ref, w_out_ref, w_up_ref, gain_attn_ref, gain_mlp_ref,
    qkv_t_ref, kv_ref, scales_ref, norm_one_ref, normed_one_ref, attended_ref, norm_two_ref, normed_two_ref,
    hidden_ref, slope_ref, gain_attn_col_ref, gain_mlp_col_ref, *probs_refs,
):
    rot_t = rotated_ref[...]
    width, rows = rot_t.shape
    gain_attn_col = column_of(gain_attn_ref[...])
    gain_attn_col_ref[...] = gain_attn_col
    gain_mlp_col = column_of(gain_mlp_ref[...])
    gain_mlp_col_ref[...] = gain_mlp_col
    scale_one = lax.rsqrt(jnp.mean(rot_t * rot_t, axis=0, keepdims=True) + EPSILON)
    norm_one = rot_t * scale_one
    norm_one_ref[...] = norm_one
    normed_one = (norm_one * lane_tile(gain_attn_col, rows)).astype(BF16)
    normed_one_ref[...] = normed_one
    qkv_t = mm_tn(w_qkv_ref[...], normed_one).astype(BF16)
    qkv_t_ref[...] = qkv_t
    kv_ref[...] = qkv_t[width:].astype(F32).T.astype(BF16)

    for ball in range(rows // BALL):
        at = ball * BALL
        cols = slice(at, at + BALL)
        for group in range(0, width, GROUP):
            queries = group_heads(qkv_t_ref[group : group + GROUP, cols])
            scores = mm(kv_ref[cols, group : group + GROUP], queries) * ATT_SCALE
            top = jnp.max(scores, axis=0, keepdims=True)
            weights = jnp.exp(scores - top)
            probs = weights * (1.0 / jnp.sum(weights, axis=0, keepdims=True))
            probs_refs[ball][group // GROUP] = probs
            probs_low = probs.astype(BF16)
            for head in range(GROUP // HEAD_DIM):
                own = slice(group + head * HEAD_DIM, group + (head + 1) * HEAD_DIM)
                values = qkv_t_ref[2 * width + own.start : 2 * width + own.stop, cols]
                attended_ref[own, cols] = mm(values, probs_low[:, head * BALL : (head + 1) * BALL]).astype(BF16)

    middle = rot_t + mm_tn(w_out_ref[...], attended_ref[...])
    scale_two = lax.rsqrt(jnp.mean(middle * middle, axis=0, keepdims=True) + EPSILON)
    norm_two = middle * scale_two
    norm_two_ref[...] = norm_two
    normed_two = (norm_two * lane_tile(gain_mlp_col, rows)).astype(BF16)
    normed_two_ref[...] = normed_two
    scales_ref[...] = jnp.where(iota(scales_ref.shape, 0) == 0, scale_one, scale_two)
    step = 256
    for at in range(0, hidden_ref.shape[0], step):
        pre_act = mm_tn(w_up_ref[:, at : at + step], normed_two)
        square = pre_act * pre_act
        tanh_val = jnp.tanh(GELU_COEF * (pre_act + 0.044715 * pre_act * square))
        half = 0.5 * (1.0 + tanh_val)
        hidden_ref[at : at + step, :] = (pre_act * half).astype(BF16)
        slope_ref[at : at + step, :] = half + 0.5 * pre_act * (1.0 - tanh_val * tanh_val) * (
            GELU_COEF * (1.0 + 3.0 * 0.044715 * square)
        )


def norm_backward(grad_normed, norm, scale, gain):
    inner = grad_normed * gain
    return scale * (inner - norm * jnp.mean(inner * norm, axis=0, keepdims=True))


def gain_row(product):
    width = product.shape[1]
    partial = product[:, :128]
    for at in range(128, width, 128):
        partial = partial + product[:, at : at + 128]
    return jnp.sum(partial.T, axis=0, keepdims=True)


def place_blocks(blocks_ref, values, first_row, leaf_size, sample_size):
    step = values.shape[0] // (leaf_size * sample_size)
    for block in range(leaf_size * sample_size):
        leaf, sample = divmod(block, sample_size)
        blocks_ref[sample, leaf, first_row : first_row + step, :] = values[block * step : (block + 1) * step]


def part_blocks(blocks_ref, keep_ref, send_ref):
    low = lax.rem(lax.axis_index("sample"), 2)
    for high in range(keep_ref.shape[0]):
        keep_ref[high] = blocks_ref[2 * high + low]
        send_ref[high] = blocks_ref[2 * high + 1 - low].astype(BF16)


def mlp_weights_kernel(
    arranged, direct, target_ref, hidden_ref, slope_ref, normed_two_ref, w_down_ref, *refs
):
    width, rows = normed_two_ref.shape
    if direct:
        mine_ref, mate_ref, *refs, landing_ref = refs
        for step in range(mine_ref.shape[0]):
            landing_ref[partner(2 * step)] = mine_ref[step]
            landing_ref[partner(2 * step + 1)] = mate_ref[step]
        recv_ref = landing_ref
    else:
        recv_ref, *refs = refs
    grad_pre_ref, cot_t_ref, *mat_refs = refs
    recv = recv_ref[...].reshape(-1, width)
    cot_f = mm(one_hot(target_ref[...], (rows, recv.shape[0]), 0), recv)
    cot = cot_f.astype(BF16)
    cot_t = cot_f.T
    cot_t_ref[...] = cot_t
    cot_t_low = cot_t.astype(BF16)
    normed_two = normed_two_ref[...]
    step = 256
    if arranged:
        keep_ref, send_ref, blocks_ref = mat_refs
        leaf_size, sample_size = lax.axis_size("leaf"), lax.axis_size("sample")
        up_rows = width // leaf_size
        down_rows = hidden_ref.shape[0] // (leaf_size * sample_size)
    else:
        grad_up_ref, grad_down_ref = mat_refs
    for at in range(0, hidden_ref.shape[0], step):
        grad_down = mm(hidden_ref[at : at + step, :], cot)
        grad_pre = (mm(w_down_ref[at : at + step, :], cot_t_low) * slope_ref[at : at + step, :]).astype(BF16)
        grad_pre_ref[at : at + step, :] = grad_pre
        grad_up = mm_nt(normed_two, grad_pre)
        if arranged:
            for leaf in range(leaf_size):
                blocks_ref[at // step, leaf, :up_rows, :] = grad_up[leaf * up_rows : (leaf + 1) * up_rows]
            for block in range(step // down_rows):
                leaf, sample = divmod(at // down_rows + block, sample_size)
                piece = grad_down[block * down_rows : (block + 1) * down_rows]
                blocks_ref[sample, leaf, up_rows:, :] = piece
        else:
            grad_down_ref[at : at + step, :] = grad_down.astype(BF16)
            grad_up_ref[:, at : at + step] = grad_up.astype(BF16)
    if arranged:
        part_blocks(blocks_ref, keep_ref, send_ref)


def mlp_inputs_kernel(
    grad_pre_ref, cot_t_ref, norm_two_ref, scales_ref, attended_ref, w_up_ref, w_out_ref, gain_mlp_ref,
    grad_gain_ref, grad_middle_ref, grad_att_ref, grad_out_ref,
):
    grad_normed = mm(w_up_ref[...], grad_pre_ref[...])
    norm_two = norm_two_ref[...]
    grad_gain_ref[...] = gain_row(grad_normed * norm_two)
    gain = lane_tile(gain_mlp_ref[...], norm_two.shape[1])
    grad_middle = cot_t_ref[...] + norm_backward(grad_normed, norm_two, scales_ref[1:2, :], gain)
    grad_middle_ref[...] = grad_middle
    grad_middle_low = grad_middle.astype(BF16)
    grad_att_ref[...] = mm(w_out_ref[...], grad_middle_low).astype(BF16)
    grad_out_ref[...] = mm_nt(attended_ref[...], grad_middle_low)


def ball_backward(ball, qkv_t_ref, kv_ref, probs_ref, grad_att_ref, grad_rows_ref):
    width = qkv_t_ref.shape[0] // 3
    cols = slice(ball * BALL, (ball + 1) * BALL)
    for group in range(0, width, GROUP):
        upstream = grad_att_ref[group : group + GROUP, cols]
        probs = probs_ref[group // GROUP]
        grad_probs = mm(kv_ref[cols, width + group : width + group + GROUP], group_heads(upstream))
        delta = jnp.sum(grad_probs * probs, axis=0, keepdims=True)
        grad_scores = (probs * (grad_probs - delta)).astype(BF16)
        probs_low = probs.astype(BF16)
        for head in range(GROUP // HEAD_DIM):
            first = group + head * HEAD_DIM
            own, own_key, own_value = (slice(at + first, at + first + HEAD_DIM) for at in (0, width, 2 * width))
            part = slice(head * BALL, (head + 1) * BALL)
            scores_of = grad_scores[:, part]
            grad_rows_ref[own, cols] = (mm(qkv_t_ref[own_key, cols], scores_of) * ATT_SCALE).astype(BF16)
            grad_rows_ref[own_key, cols] = (mm_nt(qkv_t_ref[own, cols], scores_of) * ATT_SCALE).astype(BF16)
            grad_rows_ref[own_value, cols] = mm_nt(grad_att_ref[own, cols], probs_low[:, part]).astype(BF16)


def attention_backward_kernel(
    arranged,
    qkv_t_ref, kv_ref, scales_ref, grad_att_ref, grad_middle_ref, norm_one_ref, normed_one_ref,
    w_qkv_ref, gain_attn_ref, target_col_ref, gain_two_ref, grad_out_ref, *refs,
):
    width, rows = norm_one_ref.shape
    probs_refs, refs = refs[: rows // BALL], refs[rows // BALL :]
    back_ref, *mat_refs, grad_rows_ref = refs
    for ball, probs_ref in enumerate(probs_refs):
        ball_backward(ball, qkv_t_ref, kv_ref, probs_ref, grad_att_ref, grad_rows_ref)
    grad_rows = grad_rows_ref[...]
    grad_normed = mm(w_qkv_ref[...], grad_rows)
    norm_one = norm_one_ref[...]
    gain_one = gain_row(grad_normed * norm_one)
    gain = lane_tile(gain_attn_ref[...], rows)
    grad_rot = grad_middle_ref[...] + norm_backward(grad_normed, norm_one, scales_ref[0:1, :], gain)
    place = one_hot(lane_tile(target_col_ref[...], rows), (back_ref.shape[0], rows), 1)
    back_ref[...] = mm_nt(place, grad_rot.astype(BF16)).astype(BF16)
    normed_one = normed_one_ref[...]
    if not arranged:
        mat_refs[0][...] = mm_nt(normed_one, grad_rows).astype(BF16)
        mat_refs[1][...] = gain_one
        return
    keep_ref, send_ref, blocks_ref = mat_refs
    leaf_size, sample_size = lax.axis_size("leaf"), lax.axis_size("sample")
    step = width // (leaf_size * sample_size)
    for col in range(3):
        grad_qkv = mm_nt(normed_one, grad_rows[col * width : (col + 1) * width])
        place_blocks(blocks_ref, grad_qkv, (1 + col) * step, leaf_size, sample_size)
    place_blocks(blocks_ref, grad_out_ref[...], 0, leaf_size, sample_size)
    row = iota((GAINS, width), 0)
    gains = jnp.where(row == 0, gain_one, jnp.where(row == 1, gain_two_ref[...], 0.0))
    for sample in range(sample_size):
        for leaf in range(leaf_size):
            blocks_ref[sample, leaf, 4 * step :, :] = gains
    part_blocks(blocks_ref, keep_ref, send_ref)


def unpack_kernel(slot_ref, returned_ref, out_ref):
    slots = returned_ref.shape[0]
    slot_col = column_of(slot_ref[...].astype(F32)).astype(jnp.int32)
    place = one_hot(lane_tile(slot_col, slots), (out_ref.shape[0], slots), 1)
    out_ref[...] = mm(place, returned_ref[...]).astype(BF16)


def halve_kernel(axis, bit, keep_ref, got_ref, keep_out_ref, send_out_ref):
    mine = lax.rem(lax.div(lax.axis_index(axis), bit), 2)
    for high in range(keep_out_ref.shape[0]):
        for ref, at in ((keep_out_ref, 2 * high + mine), (send_out_ref, 2 * high + 1 - mine)):
            ref[high] = (keep_ref[at] + got_ref[at].astype(F32)).astype(ref.dtype)


def join_kernel(bit, *refs):
    ins, (keep_out_ref, send_out_ref) = refs[:-2], refs[-2:]
    mine = lax.rem(lax.div(lax.axis_index("leaf"), bit), 2)
    start = 0
    for keep_ref, got_ref in zip(ins[::2], ins[1::2]):
        rows = pl.ds(start, keep_ref.shape[1])
        for ref, at in ((keep_out_ref, mine), (send_out_ref, 1 - mine)):
            ref[rows, :] = (keep_ref[at] + got_ref[at].astype(F32)).astype(ref.dtype)
        start += keep_ref.shape[1]


def finish_kernel(keep_ref, got_ref, low_ref, gains_ref):
    total = keep_ref[...] + got_ref[...].astype(F32)
    gains_ref[...] = total[-GAINS:]
    low_ref[0] = total[:-GAINS].astype(BF16)


def assemble_kernel(scale, offsets, mine_ref, mate_ref, up_ref, down_ref, out_ref, qkv_ref):
    size = 2 * len(offsets)
    width = mine_ref.shape[2]
    up_rows, down_rows, out_rows = up_ref.shape[0], down_ref.shape[0] // size, out_ref.shape[0] // size
    me = lax.axis_index("sample")

    def block(source, count):
        return pl.ds(pl.multiple_of(source * count, count), count)

    for index, offset in enumerate(offsets):
        for mate, ref in enumerate((mine_ref, mate_ref)):
            source = me ^ (offset + mate)
            part = ref[index].astype(F32) * scale
            at = up_rows
            up_ref[:, block(source, width)] = part[:at]
            down_ref[block(source, down_rows), :] = part[at : at + down_rows]
            at += down_rows
            out_ref[block(source, out_rows), :] = part[at : at + out_rows]
            at += out_rows
            for col in range(3):
                qkv_ref[block(source, out_rows), col * width : (col + 1) * width] = part[at : at + out_rows]
                at += out_rows


def permute(value, axis, size, bit):
    return lax.ppermute(value, axis, [(i, i ^ bit) for i in range(size)])


def halve(keep, got, axis, bit, name):
    shape = (keep.shape[0] // 2,) + keep.shape[1:]
    return call(functools.partial(halve_kernel, axis, bit), [(shape, F32), (shape, BF16)], name, 0.5, keep, got)


def call(kernel, outs, name, micros, *args, scratch=(), hbm_in=False, hbm_out=False, raw_in=0, raw_out=0, blocked=False, limit=16):
    moved = sum(arg.size * arg.dtype.itemsize for arg in args)
    moved += sum(math.prod(shape) * jnp.dtype(dtype).itemsize for shape, dtype in outs)
    vmem = pl.BlockSpec() if blocked else pl.BlockSpec(memory_space=pltpu.VMEM)
    hbm = pl.BlockSpec(memory_space=pltpu.HBM)
    copied_in = len(args) - raw_in if hbm_in else 0
    copied_out = len(outs) - raw_out if hbm_out else 0
    parts = 2

    def body(*refs):
        ins, refs = list(refs[: len(args)]), refs[len(args) :]
        results, refs = list(refs[: len(outs)]), refs[len(outs) :]
        own, refs = refs[: len(scratch)], refs[len(scratch) :]
        in_bufs, refs = refs[:copied_in], refs[copied_in:]
        out_bufs, refs = refs[:copied_out], refs[copied_out:]
        for at, buf in enumerate(in_bufs):
            copy = pltpu.make_async_copy(ins[at], buf, refs[0].at[at])
            copy.start()
            ins[at] = Arriving(buf, [copy])
        for at, buf in enumerate(out_bufs):
            results[at] = Leaving(buf, results[at], refs[-1].at[at])
        kernel(*ins, *results, *own)
        for ref in ins:
            if isinstance(ref, Arriving):
                for copy in ref.copies:
                    copy.wait()
        for ref in results[:copied_out]:
            ref.send()
        for ref in results[:copied_out]:
            for copy in ref.copies:
                copy.wait()

    extra = [pltpu.VMEM(arg.shape, arg.dtype) for arg in args[:copied_in]]
    extra += [pltpu.VMEM(shape, dtype) for shape, dtype in outs[:copied_out]]
    if copied_in:
        extra.append(pltpu.SemaphoreType.DMA((copied_in,)))
    if copied_out:
        extra.append(pltpu.SemaphoreType.DMA((copied_out, parts)))
    return pl.pallas_call(
        body,
        out_shape=[jax.ShapeDtypeStruct(shape, dtype) for shape, dtype in outs],
        in_specs=[hbm if hbm_in else vmem] * (len(args) - raw_in) + [hbm] * raw_in,
        out_specs=[hbm if hbm_out else vmem] * (len(outs) - raw_out) + [hbm] * raw_out,
        scratch_shapes=list(scratch) + extra,
        compiler_params=pltpu.CompilerParams(vmem_limit_bytes=limit * 1024 * 1024),
        cost_estimate=pl.CostEstimate(flops=int(micros * 1.1e9), bytes_accessed=moved, transcendentals=0),
        name=name,
    )(*args)


def exchange(flat, axes, peers):
    moved = lax.all_to_all(
        flat.reshape((peers, -1) + flat.shape[1:]), axes, split_axis=0, concat_axis=0, tiled=True
    )
    return moved.reshape(flat.shape)


def local(points, cotangent, dest_pos, w_qkv, w_out, w_up, w_down, gain_attn, gain_mlp):
    rows, width = points.shape
    hidden_width = w_up.shape[1]
    axes = ("leaf", "sample")
    peers = lax.axis_size(axes)
    leaf_size, sample_size = lax.axis_size("leaf"), lax.axis_size("sample")
    cap = 2 * rows // peers
    slots = peers * cap
    balls = rows // BALL
    direct = cap % 16 == 0
    paired = leaf_size & (leaf_size - 1) == 0 and sample_size & (sample_size - 1) == 0 and min(leaf_size, sample_size) > 1
    arranged = paired and width % (16 * peers) == 0 and hidden_width == sample_size * width and leaf_size <= 8
    inv_root = 1.0 / math.sqrt(rows * peers)

    msg_rows = 2 * cap + META
    if direct:
        outs = [((peers, msg_rows, 128), BF16)]
    else:
        outs = [((slots, width), BF16), ((peers, 128), F32), ((peers, 128), F32)]
    slot, *message = call(
        functools.partial(pack_points_kernel, peers, cap, direct),
        [((1, rows), jnp.int32)] + outs, "pack_points", 2, dest_pos.reshape(1, rows), points, hbm_in=True, hbm_out=True, limit=60,
    )
    if direct:
        forward_args = [exchange(message[0].reshape(-1, 128), axes, peers).reshape(peers, msg_rows, 128)]
    else:
        packed, high, low = message
        tail = jnp.stack([high, low], axis=1).astype(BF16)
        halves = packed.reshape(peers, cap, 2, 128).transpose(0, 2, 1, 3).reshape(peers, 2 * cap, 128)
        flat = jnp.concatenate([halves, tail], axis=1).reshape(-1, 128)
        arrived = exchange(flat, axes, peers).reshape(peers, 2 * cap + 2, 128)
        halves = arrived[:, : 2 * cap].reshape(peers, 2, cap, 128).transpose(0, 2, 1, 3).reshape(slots, width)
        forward_args = [halves, arrived[:, 2 * cap].astype(F32), arrived[:, 2 * cap + 1].astype(F32)]
    by_permute = direct and paired and peers <= 16
    if by_permute:
        packed_cot = call(
            pack_cot_kernel, [((2, cap, width), BF16)] * (peers // 2), "pack_cot", 1, slot, cotangent,
            scratch=[pltpu.VMEM((peers, cap, width), BF16)],
        )
        pairs = [packed_cot[0]] + [permute(packed_cot[step], axes, peers, 2 * step) for step in range(1, peers // 2)]
        *pairs[1:3], forward_args[0] = lax.optimization_barrier((*pairs[1:3], forward_args[0]))
    else:
        (packed_cot,) = call(pack_cot_kernel, [((slots, width), BF16)], "pack_cot", 1, slot, cotangent)
        arrived_cot = [exchange(packed_cot, axes, peers)]
    target, target_col, rotated = call(
        functools.partial(unpack_points_kernel, cap, peers, direct),
        [((1, slots), jnp.int32), ((slots, 128), jnp.int32), ((width, rows), F32)],
        "unpack_points", 2, *forward_args,
    )
    (
        qkv_t, kv, scales, norm_one, normed_one, attended, norm_two, normed_two, hidden, slope,
        gain_attn_col, gain_mlp_col, *probs,
    ) = call(
        forward_kernel,
        [
            ((3 * width, rows), BF16), ((rows, 2 * width), BF16), ((8, rows), F32),
            ((width, rows), F32), ((width, rows), BF16), ((width, rows), BF16),
            ((width, rows), F32), ((width, rows), BF16),
            ((hidden_width, rows), BF16), ((hidden_width, rows), F32), ((width, 128), F32), ((width, 128), F32),
        ] + [((width // GROUP, BALL, GROUP // HEAD_DIM * BALL), F32)] * balls,
        "forward", 7, rotated, w_qkv, w_out, w_up, gain_attn.reshape(1, width), gain_mlp.reshape(1, width),
    )
    if by_permute:
        scales, *pairs = lax.optimization_barrier((scales, *pairs))
        half = ((peers // 2, cap, width), BF16)
        mine, for_mate = call(regroup_kernel, [half] * 2, "regroup", 0.3, *pairs)
        arrived_cot = [mine, permute(for_mate, axes, peers, 1)]
    mlp_scratch, qkv_scratch = [], []
    if arranged:
        halved = (sample_size // 2, leaf_size)
        mlp_rows = width // leaf_size + hidden_width // peers
        qkv_rows = 4 * width // peers + GAINS
        mlp_mats = [(halved + (mlp_rows, width), F32), (halved + (mlp_rows, width), BF16)]
        qkv_mats = [(halved + (qkv_rows, width), F32), (halved + (qkv_rows, width), BF16)]
        mlp_scratch = [pltpu.VMEM((sample_size, leaf_size, mlp_rows, width), F32)]
        qkv_scratch = [pltpu.VMEM((sample_size, leaf_size, qkv_rows, width), F32)]
    else:
        mlp_mats = [(w_up.shape, BF16), (w_down.shape, BF16)]
        qkv_mats = [(w_qkv.shape, BF16), ((1, width), F32)]
    grad_pre, cot_t, *mlp_grads = call(
        functools.partial(mlp_weights_kernel, arranged, by_permute),
        [((hidden_width, rows), BF16), ((width, rows), F32)] + mlp_mats,
        "mlp_weights", 2.5, target, hidden, slope, normed_two, w_down, *arrived_cot,
        scratch=mlp_scratch + ([pltpu.VMEM((peers, cap, width), BF16)] if by_permute else []),
    )
    gain_two, grad_middle, grad_att, grad_out = call(
        mlp_inputs_kernel,
        [((1, width), F32), ((width, rows), F32), ((width, rows), BF16), ((width, width), F32)],
        "mlp_inputs", 1.5, grad_pre, cot_t, norm_two, scales, attended, w_up, w_out, gain_mlp_col,
    )
    if arranged:
        keep_mlp, send_mlp = mlp_grads
        got_mlp = permute(send_mlp, "sample", sample_size, 1)
        bit = 2
        while bit < sample_size:
            keep_mlp, send_mlp = halve(keep_mlp, got_mlp, "sample", bit, "halve_mlp")
            grad_att, send_mlp = lax.optimization_barrier((grad_att, send_mlp))
            got_mlp = permute(send_mlp, "sample", sample_size, bit)
            bit *= 2
    back, *qkv_grads = call(
        functools.partial(attention_backward_kernel, arranged),
        [((slots, width), BF16)] + qkv_mats, "attention_backward", 6,
        qkv_t, kv, scales, grad_att, grad_middle, norm_one, normed_one,
        w_qkv, gain_attn_col, target_col, gain_two, grad_out, *probs,
        scratch=qkv_scratch + [pltpu.VMEM((3 * width, rows), BF16)],
    )
    if not arranged:
        returned = exchange(back, axes, peers)
        (grad_points,) = call(unpack_kernel, [((rows, width), BF16)], "unpack", 1, slot, returned, blocked=True)
        up_sum, down_sum, out_sum = reduce_mats([*mlp_grads, grad_out])
        qkv_sum, gain_sum = reduce_mats([qkv_grads[0]], jnp.concatenate([qkv_grads[1], gain_two], axis=0))
        return (
            grad_points, qkv_sum * inv_root, out_sum * inv_root, up_sum * inv_root, down_sum * inv_root,
            gain_sum[0] * inv_root, gain_sum[1] * inv_root,
        )
    keep_qkv, send_qkv = qkv_grads
    got_qkv = permute(send_qkv, "sample", sample_size, 1)
    got_qkv = lax.optimization_barrier((got_qkv, got_mlp))[0]
    bit = 2
    while bit < sample_size:
        keep_qkv, send_qkv = halve(keep_qkv, got_qkv, "sample", bit, "halve_qkv")
        got_qkv = permute(send_qkv, "sample", sample_size, bit)
        bit *= 2
    keep_mlp, got_mlp, keep_qkv, got_qkv = keep_mlp[0], got_mlp[0], keep_qkv[0], got_qkv[0]
    bit = 1
    while bit * 2 < leaf_size:
        keep_mlp, leaving = halve(keep_mlp, got_mlp, "leaf", bit, "leaf_mlp")
        if bit == 1:
            back = lax.optimization_barrier((back, leaving, send_qkv))[0]
        got_mlp = permute(leaving, "leaf", leaf_size, bit)
        keep_qkv, leaving = halve(keep_qkv, got_qkv, "leaf", bit, "leaf_qkv")
        got_qkv = permute(leaving, "leaf", leaf_size, bit)
        bit *= 2
    joined = (mlp_rows + qkv_rows, width)
    keep, leaving = call(
        functools.partial(join_kernel, bit), [(joined, F32), (joined, BF16)], "leaf_last", 0.5,
        keep_mlp, got_mlp, keep_qkv, got_qkv,
    )
    got = permute(leaving, "leaf", leaf_size, bit)
    returned = exchange(back, axes, peers)
    (grad_points,) = call(unpack_kernel, [((rows, width), BF16)], "unpack", 1, slot, returned, blocked=True)
    low, gains = call(
        finish_kernel, [((1, mlp_rows + qkv_rows - GAINS, width), BF16), ((GAINS, width), F32)], "finish", 0.5, keep, got
    )
    offsets = [0]
    bit = sample_size // 2
    while bit > 1:
        low = jnp.concatenate([low, permute(low, "sample", sample_size, bit)], axis=0)
        offsets += [offset ^ bit for offset in offsets]
        bit //= 2
    mate = permute(low, "sample", sample_size, 1)
    share = width // leaf_size
    gains = lax.dynamic_slice(gains, (0, lax.axis_index("leaf") * share), (2, share)) * inv_root
    gain_one, gain_two = gains[0], gains[1]
    grad_points, gain_one, gain_two, mate = lax.optimization_barrier((grad_points, gain_one, gain_two, mate))
    up_sum, down_sum, out_sum, qkv_sum = call(
        functools.partial(assemble_kernel, inv_root, offsets),
        [
            ((share, hidden_width), F32), ((hidden_width // leaf_size, width), F32), ((share, width), F32),
            ((share, 3 * width), F32),
        ],
        "assemble", 1, low, mate, blocked=True,
    )
    return (grad_points, qkv_sum, out_sum, up_sum, down_sum, gain_one, gain_two)


def reduce_mats(mats, gains=None):
    leaf_size = lax.axis_size("leaf")
    sample_size = lax.axis_size("sample")
    me = lax.axis_index("sample")
    pieces = []
    for mat in mats:
        pieces.append(mat.reshape(leaf_size, sample_size, -1, 128).transpose(1, 0, 2, 3))
    if gains is not None:
        gain_block = gains.reshape(2, leaf_size, -1).transpose(1, 0, 2).reshape(1, leaf_size, 1, -1)
        gain_block = jnp.pad(gain_block, ((0, 0), (0, 0), (0, 15), (0, 128 - gain_block.shape[3])))
        pieces.append(jnp.broadcast_to(gain_block, (sample_size,) + gain_block.shape[1:]))
    current = jnp.concatenate(pieces, axis=2).astype(jnp.bfloat16)
    bit = 1
    while bit < sample_size:
        split = current.reshape((current.shape[0] // 2, 2) + current.shape[1:])
        mine = (me // bit) % 2
        keep = lax.dynamic_index_in_dim(split, mine, 1, keepdims=False)
        send = lax.dynamic_index_in_dim(split, 1 - mine, 1, keepdims=False)
        got = lax.ppermute(send, "sample", [(i, i ^ bit) for i in range(sample_size)])
        current = (keep.astype(jnp.float32) + got.astype(jnp.float32)).astype(jnp.bfloat16)
        bit *= 2
    current = lax.all_to_all(current[0], "leaf", split_axis=0, concat_axis=0, tiled=True)
    total = jnp.sum(current.astype(jnp.float32), axis=0)
    low = total.astype(jnp.bfloat16)
    gathered = jnp.zeros((sample_size,) + low.shape, jnp.bfloat16)
    for step in range(sample_size):
        got = low if step == 0 else lax.ppermute(low, "sample", [(i, i ^ step) for i in range(sample_size)])
        gathered = lax.dynamic_update_index_in_dim(gathered, got, me ^ step, 0)
    results = []
    start = 0
    for mat in mats:
        rows = mat.size // (leaf_size * sample_size * 128)
        part = gathered[:, start : start + rows].astype(jnp.float32)
        results.append(part.reshape(mat.shape[0] // leaf_size, mat.shape[1]))
        start += rows
    if gains is not None:
        width = gains.shape[1] // leaf_size
        results.append(total[start, : 2 * width].reshape(2, width))
    return results


def solution(mesh):
    in_specs = (
        P(("groups", "leaf", "sample"), None),
        P(("groups", "leaf", "sample"), None),
        P(("groups", "leaf", "sample")),
        P(),
        P(),
        P(),
        P(),
        P(),
        P(),
    )
    out_specs = (
        P(("groups", "leaf", "sample"), None),
        P(("groups", "leaf"), None),
        P(("groups", "leaf"), None),
        P(("groups", "leaf"), None),
        P(("groups", "leaf"), None),
        P(("groups", "leaf")),
        P(("groups", "leaf")),
    )
    return jax.shard_map(local, mesh=mesh, in_specs=in_specs, out_specs=out_specs, check_vma=False)
```

```python
import functools
import math

import jax
import jax.numpy as jnp
from jax import lax
from jax.experimental import pallas as pl
from jax.experimental.pallas import tpu as pltpu
from jax.sharding import PartitionSpec as P

HEADS = 8
BALL = 256
HEAD_DIM = 32
GROUP = 128
META = 16
GAINS = 8

EPSILON = 1e-06
GELU_COEF = math.sqrt(2.0 / math.pi)
ATT_SCALE = HEAD_DIM ** (-0.5)
BF16 = jnp.bfloat16
F32 = jnp.float32


def mm(a, b):
    return lax.dot_general(a, b, (((1,), (0,)), ((), ())), preferred_element_type=F32)


def mm_nt(a, b):
    return lax.dot_general(a, b, (((1,), (1,)), ((), ())), preferred_element_type=F32)


def mm_tn(a, b):
    return lax.dot_general(a, b, (((0,), (0,)), ((), ())), preferred_element_type=F32)


def iota(shape, dim):
    return lax.broadcasted_iota(jnp.int32, shape, dim)


def one_hot(positions, shape, dim):
    return jnp.where(iota(shape, dim) == positions, 1.0, 0.0).astype(BF16)


def column_of(row):
    return jnp.broadcast_to(row, (128, row.shape[1])).T


def lane_tile(column, width):
    return jnp.concatenate([column] * (width // 128), axis=1)


class Arriving:
    def __init__(self, ref, copies):
        self.ref, self.copies, self.shape = ref, copies, ref.shape

    def __getitem__(self, where):
        for copy in self.copies:
            copy.wait()
        self.copies = []
        return self.ref[where]


class Leaving:
    def __init__(self, ref, out_ref, sems):
        self.ref, self.out_ref, self.sems, self.shape, self.dtype = ref, out_ref, sems, ref.shape, ref.dtype
        self.copies, self.sent = [], 0

    def __getitem__(self, where):
        return self.ref[where]

    def __setitem__(self, where, value):
        self.ref[where] = value

    def send(self, upto=None):
        upto = self.shape[0] if upto is None else upto
        if upto > self.sent:
            part = pl.ds(self.sent, upto - self.sent)
            copy = pltpu.make_async_copy(self.ref.at[part], self.out_ref.at[part], self.sems.at[len(self.copies)])
            copy.start()
            self.copies.append(copy)
            self.sent = upto


def send(ref, upto=None):
    if isinstance(ref, Leaving):
        ref.send(upto)


def pack_points_kernel(peers, cap, direct, dest_ref, points_ref, slot_ref, *out_refs):
    rows = points_ref.shape[0]
    slots = peers * cap
    dest = dest_ref[...]
    shift = rows.bit_length() - 1
    owner = lax.shift_right_logical(dest, shift)
    target = jnp.bitwise_and(dest, rows - 1)
    owned = jnp.where(iota((peers, rows), 0) == owner, 1.0, 0.0)
    upto = jnp.where(iota((rows, rows), 0) <= iota((rows, rows), 1), 1.0, 0.0).astype(BF16)
    counts = mm(owned.astype(BF16), upto)
    rank = (jnp.sum(counts * owned, axis=0, keepdims=True) - 1.0).astype(jnp.int32)
    slot = owner * cap + rank
    slot_ref[...] = slot
    packed = mm(one_hot(slot, (slots, rows), 0), points_ref[...]).astype(BF16)
    within = one_hot(rank, (cap, rows), 0)
    within = jnp.concatenate([within] * (128 // cap), axis=0)
    high = (lax.shift_right_logical(target, 4) + 1).astype(F32)
    low = jnp.bitwise_and(target, 15).astype(F32)
    high_rows = mm_nt((owned * high).astype(BF16), within)
    low_rows = mm_nt((owned * low).astype(BF16), within)
    if direct:
        (msg_ref,) = out_refs
        msg_ref[:, :cap, :] = packed[:, :128].reshape(peers, cap, 128)
        msg_ref[:, cap : 2 * cap, :] = packed[:, 128:].reshape(peers, cap, 128)
        first = iota((META, 128), 0) == 0
        for peer in range(peers):
            block = jnp.where(first, high_rows[peer : peer + 1], low_rows[peer : peer + 1])
            msg_ref[peer, 2 * cap :, :] = block.astype(BF16)
    else:
        packed_ref, high_ref, low_ref = out_refs
        packed_ref[...] = packed
        high_ref[...] = high_rows
        low_ref[...] = low_rows


def partner(step):
    return (lax.axis_index("leaf") * lax.axis_size("sample") + lax.axis_index("sample")) ^ step


def pack_cot_kernel(slot_ref, cot_ref, *refs):
    rows = cot_ref.shape[0]
    if len(refs) == 1:
        (packed_ref,) = refs
        packed_ref[...] = mm(one_hot(slot_ref[...], (packed_ref.shape[0], rows), 0), cot_ref[...]).astype(BF16)
        return
    *block_refs, packed_ref = refs
    peers, cap, width = packed_ref.shape
    packed = mm(one_hot(slot_ref[...], (peers * cap, rows), 0), cot_ref[...]).astype(BF16)
    packed_ref[...] = packed.reshape(peers, cap, width)
    for step, ref in enumerate(block_refs):
        for mate in range(2):
            ref[mate] = packed_ref[partner(2 * step + mate)]


def regroup_kernel(*refs):
    *pair_refs, mine_ref, mate_ref = refs
    for step, ref in enumerate(pair_refs):
        mine_ref[step] = ref[0]
        mate_ref[step] = ref[1]


def group_heads(rows):
    heads = range(GROUP // HEAD_DIM)
    return jnp.concatenate([head_rows(rows[h * HEAD_DIM : (h + 1) * HEAD_DIM], h) for h in heads], axis=1)


def head_rows(rows, head):
    width = rows.shape[1]
    at = (head * HEAD_DIM) % GROUP
    parts = []
    if at:
        parts.append(jnp.zeros((at, width), rows.dtype))
    parts.append(rows)
    if at + HEAD_DIM < GROUP:
        parts.append(jnp.zeros((GROUP - at - HEAD_DIM, width), rows.dtype))
    return jnp.concatenate(parts, axis=0)


def unpack_points_kernel(cap, peers, direct, *refs):
    if not direct:
        recv_ref, high_ref, low_ref = refs[:3]
        recv = recv_ref[...]
        high_rows, low_rows = high_ref[...], low_ref[...]
    else:
        msg_ref = refs[0]
        left = msg_ref[:, :cap, :].reshape(peers * cap, 128)
        right = msg_ref[:, cap : 2 * cap, :].reshape(peers * cap, 128)
        recv = jnp.concatenate([left, right], axis=1)
        tails = [msg_ref[peer, 2 * cap :, :].astype(F32) for peer in range(peers)]
        high_rows = jnp.concatenate([tail[0:1] for tail in tails], axis=0)
        low_rows = jnp.concatenate([tail[1:2] for tail in tails], axis=0)
    target_ref, target_col_ref, rotated_ref = refs[-3:]
    rows = rotated_ref.shape[1]
    slots = peers * cap
    targets = (high_rows - 1.0) * 16.0 + low_rows
    per_row = 128 // cap
    own_lane = iota((per_row, 128), 1) // cap == iota((per_row, 128), 0)
    pieces = []
    for group in range(slots // 128):
        block = targets[group * per_row : (group + 1) * per_row]
        pieces.append(jnp.sum(jnp.where(own_lane, block, 0.0), axis=0, keepdims=True))
    target = jnp.concatenate(pieces, axis=1)
    target_ref[...] = target.astype(jnp.int32)
    target_col_ref[...] = column_of(target).astype(jnp.int32)
    rotated_ref[...] = mm(one_hot(target.astype(jnp.int32), (rows, slots), 0), recv).T


def forward_kernel(
    rotated_ref, w_qkv_ref, w_out_ref, w_up_ref, gain_attn_ref, gain_mlp_ref,
    qkv_t_ref, kv_ref, scales_ref, norm_one_ref, normed_one_ref, attended_ref, norm_two_ref, normed_two_ref,
    hidden_ref, slope_ref, gain_attn_col_ref, gain_mlp_col_ref, *probs_refs,
):
    rot_t = rotated_ref[...]
    width, rows = rot_t.shape
    gain_attn_col = column_of(gain_attn_ref[...])
    gain_attn_col_ref[...] = gain_attn_col
    gain_mlp_col = column_of(gain_mlp_ref[...])
    gain_mlp_col_ref[...] = gain_mlp_col
    scale_one = lax.rsqrt(jnp.mean(rot_t * rot_t, axis=0, keepdims=True) + EPSILON)
    norm_one = rot_t * scale_one
    norm_one_ref[...] = norm_one
    normed_one = (norm_one * lane_tile(gain_attn_col, rows)).astype(BF16)
    normed_one_ref[...] = normed_one
    qkv_t = mm_tn(w_qkv_ref[...], normed_one).astype(BF16)
    qkv_t_ref[...] = qkv_t
    kv_ref[...] = qkv_t[width:].astype(F32).T.astype(BF16)

    for ball in range(rows // BALL):
        at = ball * BALL
        cols = slice(at, at + BALL)
        for group in range(0, width, GROUP):
            queries = group_heads(qkv_t_ref[group : group + GROUP, cols])
            scores = mm(kv_ref[cols, group : group + GROUP], queries) * ATT_SCALE
            top = jnp.max(scores, axis=0, keepdims=True)
            weights = jnp.exp(scores - top)
            probs = weights * (1.0 / jnp.sum(weights, axis=0, keepdims=True))
            probs_refs[ball][group // GROUP] = probs
            probs_low = probs.astype(BF16)
            for head in range(GROUP // HEAD_DIM):
                own = slice(group + head * HEAD_DIM, group + (head + 1) * HEAD_DIM)
                values = qkv_t_ref[2 * width + own.start : 2 * width + own.stop, cols]
                attended_ref[own, cols] = mm(values, probs_low[:, head * BALL : (head + 1) * BALL]).astype(BF16)

    middle = rot_t + mm_tn(w_out_ref[...], attended_ref[...])
    scale_two = lax.rsqrt(jnp.mean(middle * middle, axis=0, keepdims=True) + EPSILON)
    norm_two = middle * scale_two
    norm_two_ref[...] = norm_two
    normed_two = (norm_two * lane_tile(gain_mlp_col, rows)).astype(BF16)
    normed_two_ref[...] = normed_two
    scales_ref[...] = jnp.where(iota(scales_ref.shape, 0) == 0, scale_one, scale_two)
    step = 256
    for at in range(0, hidden_ref.shape[0], step):
        pre_act = mm_tn(w_up_ref[:, at : at + step], normed_two)
        square = pre_act * pre_act
        tanh_val = jnp.tanh(GELU_COEF * (pre_act + 0.044715 * pre_act * square))
        half = 0.5 * (1.0 + tanh_val)
        hidden_ref[at : at + step, :] = (pre_act * half).astype(BF16)
        slope_ref[at : at + step, :] = half + 0.5 * pre_act * (1.0 - tanh_val * tanh_val) * (
            GELU_COEF * (1.0 + 3.0 * 0.044715 * square)
        )


def norm_backward(grad_normed, norm, scale, gain):
    inner = grad_normed * gain
    return scale * (inner - norm * jnp.mean(inner * norm, axis=0, keepdims=True))


def gain_row(product):
    width = product.shape[1]
    partial = product[:, :128]
    for at in range(128, width, 128):
        partial = partial + product[:, at : at + 128]
    return jnp.sum(partial.T, axis=0, keepdims=True)


def place_blocks(blocks_ref, values, first_row, leaf_size, sample_size):
    step = values.shape[0] // (leaf_size * sample_size)
    for block in range(leaf_size * sample_size):
        leaf, sample = divmod(block, sample_size)
        blocks_ref[sample, leaf, first_row : first_row + step, :] = values[block * step : (block + 1) * step]


def part_blocks(blocks_ref, keep_ref, send_ref):
    low = lax.rem(lax.axis_index("sample"), 2)
    for high in range(keep_ref.shape[0]):
        keep_ref[high] = blocks_ref[2 * high + low]
        send_ref[high] = blocks_ref[2 * high + 1 - low].astype(BF16)


def mlp_weights_kernel(
    arranged, direct, target_ref, hidden_ref, slope_ref, normed_two_ref, w_down_ref, *refs
):
    width, rows = normed_two_ref.shape
    if direct:
        mine_ref, mate_ref, *refs, landing_ref = refs
        for step in range(mine_ref.shape[0]):
            landing_ref[partner(2 * step)] = mine_ref[step]
            landing_ref[partner(2 * step + 1)] = mate_ref[step]
        recv_ref = landing_ref
    else:
        recv_ref, *refs = refs
    grad_pre_ref, cot_t_ref, *mat_refs = refs
    recv = recv_ref[...].reshape(-1, width)
    cot_f = mm(one_hot(target_ref[...], (rows, recv.shape[0]), 0), recv)
    cot = cot_f.astype(BF16)
    cot_t = cot_f.T
    cot_t_ref[...] = cot_t
    cot_t_low = cot_t.astype(BF16)
    normed_two = normed_two_ref[...]
    step = 256
    if arranged:
        keep_ref, send_ref, blocks_ref = mat_refs
        leaf_size, sample_size = lax.axis_size("leaf"), lax.axis_size("sample")
        up_rows = width // leaf_size
        down_rows = hidden_ref.shape[0] // (leaf_size * sample_size)
    else:
        grad_up_ref, grad_down_ref = mat_refs
    for at in range(0, hidden_ref.shape[0], step):
        grad_down = mm(hidden_ref[at : at + step, :], cot)
        grad_pre = (mm(w_down_ref[at : at + step, :], cot_t_low) * slope_ref[at : at + step, :]).astype(BF16)
        grad_pre_ref[at : at + step, :] = grad_pre
        grad_up = mm_nt(normed_two, grad_pre)
        if arranged:
            for leaf in range(leaf_size):
                blocks_ref[at // step, leaf, :up_rows, :] = grad_up[leaf * up_rows : (leaf + 1) * up_rows]
            for block in range(step // down_rows):
                leaf, sample = divmod(at // down_rows + block, sample_size)
                piece = grad_down[block * down_rows : (block + 1) * down_rows]
                blocks_ref[sample, leaf, up_rows:, :] = piece
        else:
            grad_down_ref[at : at + step, :] = grad_down.astype(BF16)
            grad_up_ref[:, at : at + step] = grad_up.astype(BF16)
    if arranged:
        part_blocks(blocks_ref, keep_ref, send_ref)


def mlp_inputs_kernel(
    grad_pre_ref, cot_t_ref, norm_two_ref, scales_ref, attended_ref, w_up_ref, w_out_ref, gain_mlp_ref,
    grad_gain_ref, grad_middle_ref, grad_att_ref, grad_out_ref,
):
    grad_normed = mm(w_up_ref[...], grad_pre_ref[...])
    norm_two = norm_two_ref[...]
    grad_gain_ref[...] = gain_row(grad_normed * norm_two)
    gain = lane_tile(gain_mlp_ref[...], norm_two.shape[1])
    grad_middle = cot_t_ref[...] + norm_backward(grad_normed, norm_two, scales_ref[1:2, :], gain)
    grad_middle_ref[...] = grad_middle
    grad_middle_low = grad_middle.astype(BF16)
    grad_att_ref[...] = mm(w_out_ref[...], grad_middle_low).astype(BF16)
    grad_out_ref[...] = mm_nt(attended_ref[...], grad_middle_low)


def ball_backward(ball, qkv_t_ref, kv_ref, probs_ref, grad_att_ref, grad_rows_ref):
    width = qkv_t_ref.shape[0] // 3
    cols = slice(ball * BALL, (ball + 1) * BALL)
    for group in range(0, width, GROUP):
        upstream = grad_att_ref[group : group + GROUP, cols]
        probs = probs_ref[group // GROUP]
        grad_probs = mm(kv_ref[cols, width + group : width + group + GROUP], group_heads(upstream))
        delta = jnp.sum(grad_probs * probs, axis=0, keepdims=True)
        grad_scores = (probs * (grad_probs - delta)).astype(BF16)
        probs_low = probs.astype(BF16)
        for head in range(GROUP // HEAD_DIM):
            first = group + head * HEAD_DIM
            own, own_key, own_value = (slice(at + first, at + first + HEAD_DIM) for at in (0, width, 2 * width))
            part = slice(head * BALL, (head + 1) * BALL)
            scores_of = grad_scores[:, part]
            grad_rows_ref[own, cols] = (mm(qkv_t_ref[own_key, cols], scores_of) * ATT_SCALE).astype(BF16)
            grad_rows_ref[own_key, cols] = (mm_nt(qkv_t_ref[own, cols], scores_of) * ATT_SCALE).astype(BF16)
            grad_rows_ref[own_value, cols] = mm_nt(grad_att_ref[own, cols], probs_low[:, part]).astype(BF16)


def attention_backward_kernel(
    arranged,
    qkv_t_ref, kv_ref, scales_ref, grad_att_ref, grad_middle_ref, norm_one_ref, normed_one_ref,
    w_qkv_ref, gain_attn_ref, target_col_ref, gain_two_ref, grad_out_ref, *refs,
):
    width, rows = norm_one_ref.shape
    probs_refs, refs = refs[: rows // BALL], refs[rows // BALL :]
    back_ref, *mat_refs, grad_rows_ref = refs
    for ball, probs_ref in enumerate(probs_refs):
        ball_backward(ball, qkv_t_ref, kv_ref, probs_ref, grad_att_ref, grad_rows_ref)
    grad_rows = grad_rows_ref[...]
    grad_normed = mm(w_qkv_ref[...], grad_rows)
    norm_one = norm_one_ref[...]
    gain_one = gain_row(grad_normed * norm_one)
    gain = lane_tile(gain_attn_ref[...], rows)
    grad_rot = grad_middle_ref[...] + norm_backward(grad_normed, norm_one, scales_ref[0:1, :], gain)
    place = one_hot(lane_tile(target_col_ref[...], rows), (back_ref.shape[0], rows), 1)
    back_ref[...] = mm_nt(place, grad_rot.astype(BF16)).astype(BF16)
    normed_one = normed_one_ref[...]
    if not arranged:
        mat_refs[0][...] = mm_nt(normed_one, grad_rows).astype(BF16)
        mat_refs[1][...] = gain_one
        return
    keep_ref, send_ref, blocks_ref = mat_refs
    leaf_size, sample_size = lax.axis_size("leaf"), lax.axis_size("sample")
    step = width // (leaf_size * sample_size)
    for col in range(3):
        grad_qkv = mm_nt(normed_one, grad_rows[col * width : (col + 1) * width])
        place_blocks(blocks_ref, grad_qkv, (1 + col) * step, leaf_size, sample_size)
    place_blocks(blocks_ref, grad_out_ref[...], 0, leaf_size, sample_size)
    row = iota((GAINS, width), 0)
    gains = jnp.where(row == 0, gain_one, jnp.where(row == 1, gain_two_ref[...], 0.0))
    for sample in range(sample_size):
        for leaf in range(leaf_size):
            blocks_ref[sample, leaf, 4 * step :, :] = gains
    part_blocks(blocks_ref, keep_ref, send_ref)


def unpack_kernel(slot_ref, returned_ref, out_ref):
    slots = returned_ref.shape[0]
    slot_col = column_of(slot_ref[...].astype(F32)).astype(jnp.int32)
    place = one_hot(lane_tile(slot_col, slots), (out_ref.shape[0], slots), 1)
    out_ref[...] = mm(place, returned_ref[...]).astype(BF16)


def halve_kernel(axis, bit, keep_ref, got_ref, keep_out_ref, send_out_ref):
    mine = lax.rem(lax.div(lax.axis_index(axis), bit), 2)
    for high in range(keep_out_ref.shape[0]):
        for ref, at in ((keep_out_ref, 2 * high + mine), (send_out_ref, 2 * high + 1 - mine)):
            ref[high] = (keep_ref[at] + got_ref[at].astype(F32)).astype(ref.dtype)


def join_kernel(bit, *refs):
    ins, (keep_out_ref, send_out_ref) = refs[:-2], refs[-2:]
    mine = lax.rem(lax.div(lax.axis_index("leaf"), bit), 2)
    start = 0
    for keep_ref, got_ref in zip(ins[::2], ins[1::2]):
        rows = pl.ds(start, keep_ref.shape[1])
        for ref, at in ((keep_out_ref, mine), (send_out_ref, 1 - mine)):
            ref[rows, :] = (keep_ref[at] + got_ref[at].astype(F32)).astype(ref.dtype)
        start += keep_ref.shape[1]


def finish_kernel(keep_ref, got_ref, low_ref, gains_ref):
    total = keep_ref[...] + got_ref[...].astype(F32)
    gains_ref[...] = total[-GAINS:]
    low_ref[0] = total[:-GAINS].astype(BF16)


def assemble_kernel(scale, offsets, mine_ref, mate_ref, up_ref, down_ref, out_ref, qkv_ref):
    size = 2 * len(offsets)
    width = mine_ref.shape[2]
    up_rows, down_rows, out_rows = up_ref.shape[0], down_ref.shape[0] // size, out_ref.shape[0] // size
    me = lax.axis_index("sample")

    def block(source, count):
        return pl.ds(pl.multiple_of(source * count, count), count)

    for index, offset in enumerate(offsets):
        for mate, ref in enumerate((mine_ref, mate_ref)):
            source = me ^ (offset + mate)
            part = ref[index].astype(F32) * scale
            at = up_rows
            up_ref[:, block(source, width)] = part[:at]
            down_ref[block(source, down_rows), :] = part[at : at + down_rows]
            at += down_rows
            out_ref[block(source, out_rows), :] = part[at : at + out_rows]
            at += out_rows
            for col in range(3):
                qkv_ref[block(source, out_rows), col * width : (col + 1) * width] = part[at : at + out_rows]
                at += out_rows


def permute(value, axis, size, bit):
    return lax.ppermute(value, axis, [(i, i ^ bit) for i in range(size)])


def halve(keep, got, axis, bit, name, micros=0.5):
    shape = (keep.shape[0] // 2,) + keep.shape[1:]
    return call(functools.partial(halve_kernel, axis, bit), [(shape, F32), (shape, BF16)], name, micros, keep, got)


def call(kernel, outs, name, micros, *args, scratch=(), hbm_in=False, hbm_out=False, raw_in=0, raw_out=0, blocked=False, limit=16):
    moved = sum(arg.size * arg.dtype.itemsize for arg in args)
    moved += sum(math.prod(shape) * jnp.dtype(dtype).itemsize for shape, dtype in outs)
    vmem = pl.BlockSpec() if blocked else pl.BlockSpec(memory_space=pltpu.VMEM)
    hbm = pl.BlockSpec(memory_space=pltpu.HBM)
    copied_in = len(args) - raw_in if hbm_in else 0
    copied_out = len(outs) - raw_out if hbm_out else 0
    parts = 2

    def body(*refs):
        ins, refs = list(refs[: len(args)]), refs[len(args) :]
        results, refs = list(refs[: len(outs)]), refs[len(outs) :]
        own, refs = refs[: len(scratch)], refs[len(scratch) :]
        in_bufs, refs = refs[:copied_in], refs[copied_in:]
        out_bufs, refs = refs[:copied_out], refs[copied_out:]
        for at, buf in enumerate(in_bufs):
            copy = pltpu.make_async_copy(ins[at], buf, refs[0].at[at])
            copy.start()
            ins[at] = Arriving(buf, [copy])
        for at, buf in enumerate(out_bufs):
            results[at] = Leaving(buf, results[at], refs[-1].at[at])
        kernel(*ins, *results, *own)
        for ref in ins:
            if isinstance(ref, Arriving):
                for copy in ref.copies:
                    copy.wait()
        for ref in results[:copied_out]:
            ref.send()
        for ref in results[:copied_out]:
            for copy in ref.copies:
                copy.wait()

    extra = [pltpu.VMEM(arg.shape, arg.dtype) for arg in args[:copied_in]]
    extra += [pltpu.VMEM(shape, dtype) for shape, dtype in outs[:copied_out]]
    if copied_in:
        extra.append(pltpu.SemaphoreType.DMA((copied_in,)))
    if copied_out:
        extra.append(pltpu.SemaphoreType.DMA((copied_out, parts)))
    return pl.pallas_call(
        body,
        out_shape=[jax.ShapeDtypeStruct(shape, dtype) for shape, dtype in outs],
        in_specs=[hbm if hbm_in else vmem] * (len(args) - raw_in) + [hbm] * raw_in,
        out_specs=[hbm if hbm_out else vmem] * (len(outs) - raw_out) + [hbm] * raw_out,
        scratch_shapes=list(scratch) + extra,
        compiler_params=pltpu.CompilerParams(vmem_limit_bytes=limit * 1024 * 1024),
        cost_estimate=pl.CostEstimate(flops=int(micros * 1.1e9), bytes_accessed=moved, transcendentals=0),
        name=name,
    )(*args)


def exchange(flat, axes, peers):
    moved = lax.all_to_all(
        flat.reshape((peers, -1) + flat.shape[1:]), axes, split_axis=0, concat_axis=0, tiled=True
    )
    return moved.reshape(flat.shape)


def local(points, cotangent, dest_pos, w_qkv, w_out, w_up, w_down, gain_attn, gain_mlp):
    rows, width = points.shape
    hidden_width = w_up.shape[1]
    axes = ("leaf", "sample")
    peers = lax.axis_size(axes)
    leaf_size, sample_size = lax.axis_size("leaf"), lax.axis_size("sample")
    cap = 2 * rows // peers
    slots = peers * cap
    balls = rows // BALL
    direct = cap % 16 == 0
    paired = leaf_size & (leaf_size - 1) == 0 and sample_size & (sample_size - 1) == 0 and min(leaf_size, sample_size) > 1
    arranged = paired and width % (16 * peers) == 0 and hidden_width == sample_size * width and leaf_size <= 8
    inv_root = 1.0 / math.sqrt(rows * peers)

    msg_rows = 2 * cap + META
    if direct:
        outs = [((peers, msg_rows, 128), BF16)]
    else:
        outs = [((slots, width), BF16), ((peers, 128), F32), ((peers, 128), F32)]
    slot, *message = call(
        functools.partial(pack_points_kernel, peers, cap, direct),
        [((1, rows), jnp.int32)] + outs, "pack_points", 2, dest_pos.reshape(1, rows), points, hbm_in=True, hbm_out=True, limit=60,
    )
    if direct:
        forward_args = [exchange(message[0].reshape(-1, 128), axes, peers).reshape(peers, msg_rows, 128)]
    else:
        packed, high, low = message
        tail = jnp.stack([high, low], axis=1).astype(BF16)
        halves = packed.reshape(peers, cap, 2, 128).transpose(0, 2, 1, 3).reshape(peers, 2 * cap, 128)
        flat = jnp.concatenate([halves, tail], axis=1).reshape(-1, 128)
        arrived = exchange(flat, axes, peers).reshape(peers, 2 * cap + 2, 128)
        halves = arrived[:, : 2 * cap].reshape(peers, 2, cap, 128).transpose(0, 2, 1, 3).reshape(slots, width)
        forward_args = [halves, arrived[:, 2 * cap].astype(F32), arrived[:, 2 * cap + 1].astype(F32)]
    by_permute = direct and paired and peers <= 16
    if by_permute:
        packed_cot = call(
            pack_cot_kernel, [((2, cap, width), BF16)] * (peers // 2), "pack_cot", 1, slot, cotangent,
            scratch=[pltpu.VMEM((peers, cap, width), BF16)],
        )
        pairs = [packed_cot[0]] + [permute(packed_cot[step], axes, peers, 2 * step) for step in range(1, peers // 2)]
        *pairs[1:3], forward_args[0] = lax.optimization_barrier((*pairs[1:3], forward_args[0]))
    else:
        (packed_cot,) = call(pack_cot_kernel, [((slots, width), BF16)], "pack_cot", 1, slot, cotangent)
        arrived_cot = [exchange(packed_cot, axes, peers)]
    target, target_col, rotated = call(
        functools.partial(unpack_points_kernel, cap, peers, direct),
        [((1, slots), jnp.int32), ((slots, 128), jnp.int32), ((width, rows), F32)],
        "unpack_points", 2, *forward_args,
    )
    (
        qkv_t, kv, scales, norm_one, normed_one, attended, norm_two, normed_two, hidden, slope,
        gain_attn_col, gain_mlp_col, *probs,
    ) = call(
        forward_kernel,
        [
            ((3 * width, rows), BF16), ((rows, 2 * width), BF16), ((8, rows), F32),
            ((width, rows), F32), ((width, rows), BF16), ((width, rows), BF16),
            ((width, rows), F32), ((width, rows), BF16),
            ((hidden_width, rows), BF16), ((hidden_width, rows), F32), ((width, 128), F32), ((width, 128), F32),
        ] + [((width // GROUP, BALL, GROUP // HEAD_DIM * BALL), F32)] * balls,
        "forward", 7, rotated, w_qkv, w_out, w_up, gain_attn.reshape(1, width), gain_mlp.reshape(1, width),
    )
    if by_permute:
        scales, *pairs = lax.optimization_barrier((scales, *pairs))
        half = ((peers // 2, cap, width), BF16)
        mine, for_mate = call(regroup_kernel, [half] * 2, "regroup", 0.3, *pairs)
        arrived_cot = [mine, permute(for_mate, axes, peers, 1)]
    mlp_scratch, qkv_scratch = [], []
    if arranged:
        halved = (sample_size // 2, leaf_size)
        mlp_rows = width // leaf_size + hidden_width // peers
        qkv_rows = 4 * width // peers + GAINS
        mlp_mats = [(halved + (mlp_rows, width), F32), (halved + (mlp_rows, width), BF16)]
        qkv_mats = [(halved + (qkv_rows, width), F32), (halved + (qkv_rows, width), BF16)]
        mlp_scratch = [pltpu.VMEM((sample_size, leaf_size, mlp_rows, width), F32)]
        qkv_scratch = [pltpu.VMEM((sample_size, leaf_size, qkv_rows, width), F32)]
    else:
        mlp_mats = [(w_up.shape, BF16), (w_down.shape, BF16)]
        qkv_mats = [(w_qkv.shape, BF16), ((1, width), F32)]
    grad_pre, cot_t, *mlp_grads = call(
        functools.partial(mlp_weights_kernel, arranged, by_permute),
        [((hidden_width, rows), BF16), ((width, rows), F32)] + mlp_mats,
        "mlp_weights", 2.5, target, hidden, slope, normed_two, w_down, *arrived_cot,
        scratch=mlp_scratch + ([pltpu.VMEM((peers, cap, width), BF16)] if by_permute else []),
    )
    gain_two, grad_middle, grad_att, grad_out = call(
        mlp_inputs_kernel,
        [((1, width), F32), ((width, rows), F32), ((width, rows), BF16), ((width, width), F32)],
        "mlp_inputs", 1.5, grad_pre, cot_t, norm_two, scales, attended, w_up, w_out, gain_mlp_col,
    )
    if arranged:
        keep_mlp, send_mlp = mlp_grads
        got_mlp = permute(send_mlp, "sample", sample_size, 1)
        bit = 2
        while bit < sample_size:
            keep_mlp, send_mlp = halve(keep_mlp, got_mlp, "sample", bit, "halve_mlp")
            grad_att, send_mlp = lax.optimization_barrier((grad_att, send_mlp))
            got_mlp = permute(send_mlp, "sample", sample_size, bit)
            bit *= 2
    back, *qkv_grads = call(
        functools.partial(attention_backward_kernel, arranged),
        [((slots, width), BF16)] + qkv_mats, "attention_backward", 6,
        qkv_t, kv, scales, grad_att, grad_middle, norm_one, normed_one,
        w_qkv, gain_attn_col, target_col, gain_two, grad_out, *probs,
        scratch=qkv_scratch + [pltpu.VMEM((3 * width, rows), BF16)],
    )
    if not arranged:
        returned = exchange(back, axes, peers)
        (grad_points,) = call(unpack_kernel, [((rows, width), BF16)], "unpack", 1, slot, returned, blocked=True)
        up_sum, down_sum, out_sum = reduce_mats([*mlp_grads, grad_out])
        qkv_sum, gain_sum = reduce_mats([qkv_grads[0]], jnp.concatenate([qkv_grads[1], gain_two], axis=0))
        return (
            grad_points, qkv_sum * inv_root, out_sum * inv_root, up_sum * inv_root, down_sum * inv_root,
            gain_sum[0] * inv_root, gain_sum[1] * inv_root,
        )
    keep_qkv, send_qkv = qkv_grads
    got_qkv = permute(send_qkv, "sample", sample_size, 1)
    keep_mlp, got_mlp = keep_mlp[0], got_mlp[0]
    leaving = None
    if leaf_size > 2:
        keep_mlp, leaving = halve(keep_mlp, got_mlp, "leaf", 1, "leaf_mlp", 1.0)
        got_qkv, leaving = lax.optimization_barrier((got_qkv, leaving))
    bit = 2
    while bit < sample_size:
        keep_qkv, send_qkv = halve(keep_qkv, got_qkv, "sample", bit, "halve_qkv")
        got_qkv = permute(send_qkv, "sample", sample_size, bit)
        bit *= 2
    keep_qkv, got_qkv = keep_qkv[0], got_qkv[0]
    back = lax.optimization_barrier((back, got_mlp if leaving is None else leaving, send_qkv))[0]
    returned = exchange(back, axes, peers)
    (grad_points,) = call(unpack_kernel, [((rows, width), BF16)], "unpack", 1, slot, returned, blocked=True)
    bit = 1
    while bit * 2 < leaf_size:
        if bit > 1:
            keep_mlp, leaving = halve(keep_mlp, got_mlp, "leaf", bit, "leaf_mlp")
        got_mlp = permute(leaving, "leaf", leaf_size, bit)
        keep_qkv, leaving = halve(keep_qkv, got_qkv, "leaf", bit, "leaf_qkv")
        got_qkv = permute(leaving, "leaf", leaf_size, bit)
        bit *= 2
    joined = (mlp_rows + qkv_rows, width)
    keep, leaving = call(
        functools.partial(join_kernel, bit), [(joined, F32), (joined, BF16)], "leaf_last", 0.5,
        keep_mlp, got_mlp, keep_qkv, got_qkv,
    )
    got = permute(leaving, "leaf", leaf_size, bit)
    low, gains = call(
        finish_kernel, [((1, mlp_rows + qkv_rows - GAINS, width), BF16), ((GAINS, width), F32)], "finish", 3.5, keep, got
    )
    offsets = [0]
    bit = sample_size // 2
    while bit > 1:
        low = jnp.concatenate([low, permute(low, "sample", sample_size, bit)], axis=0)
        offsets += [offset ^ bit for offset in offsets]
        bit //= 2
    mate = permute(low, "sample", sample_size, 1)
    share = width // leaf_size
    gains = lax.dynamic_slice(gains, (0, lax.axis_index("leaf") * share), (2, share)) * inv_root
    gain_one, gain_two = gains[0], gains[1]
    gain_one, gain_two, mate = lax.optimization_barrier((gain_one, gain_two, mate))
    up_sum, down_sum, out_sum, qkv_sum = call(
        functools.partial(assemble_kernel, inv_root, offsets),
        [
            ((share, hidden_width), F32), ((hidden_width // leaf_size, width), F32), ((share, width), F32),
            ((share, 3 * width), F32),
        ],
        "assemble", 1, low, mate, blocked=True,
    )
    return (grad_points, qkv_sum, out_sum, up_sum, down_sum, gain_one, gain_two)


def reduce_mats(mats, gains=None):
    leaf_size = lax.axis_size("leaf")
    sample_size = lax.axis_size("sample")
    me = lax.axis_index("sample")
    pieces = []
    for mat in mats:
        pieces.append(mat.reshape(leaf_size, sample_size, -1, 128).transpose(1, 0, 2, 3))
    if gains is not None:
        gain_block = gains.reshape(2, leaf_size, -1).transpose(1, 0, 2).reshape(1, leaf_size, 1, -1)
        gain_block = jnp.pad(gain_block, ((0, 0), (0, 0), (0, 15), (0, 128 - gain_block.shape[3])))
        pieces.append(jnp.broadcast_to(gain_block, (sample_size,) + gain_block.shape[1:]))
    current = jnp.concatenate(pieces, axis=2).astype(jnp.bfloat16)
    bit = 1
    while bit < sample_size:
        split = current.reshape((current.shape[0] // 2, 2) + current.shape[1:])
        mine = (me // bit) % 2
        keep = lax.dynamic_index_in_dim(split, mine, 1, keepdims=False)
        send = lax.dynamic_index_in_dim(split, 1 - mine, 1, keepdims=False)
        got = lax.ppermute(send, "sample", [(i, i ^ bit) for i in range(sample_size)])
        current = (keep.astype(jnp.float32) + got.astype(jnp.float32)).astype(jnp.bfloat16)
        bit *= 2
    current = lax.all_to_all(current[0], "leaf", split_axis=0, concat_axis=0, tiled=True)
    total = jnp.sum(current.astype(jnp.float32), axis=0)
    low = total.astype(jnp.bfloat16)
    gathered = jnp.zeros((sample_size,) + low.shape, jnp.bfloat16)
    for step in range(sample_size):
        got = low if step == 0 else lax.ppermute(low, "sample", [(i, i ^ step) for i in range(sample_size)])
        gathered = lax.dynamic_update_index_in_dim(gathered, got, me ^ step, 0)
    results = []
    start = 0
    for mat in mats:
        rows = mat.size // (leaf_size * sample_size * 128)
        part = gathered[:, start : start + rows].astype(jnp.float32)
        results.append(part.reshape(mat.shape[0] // leaf_size, mat.shape[1]))
        start += rows
    if gains is not None:
        width = gains.shape[1] // leaf_size
        results.append(total[start, : 2 * width].reshape(2, width))
    return results


def solution(mesh):
    in_specs = (
        P(("groups", "leaf", "sample"), None),
        P(("groups", "leaf", "sample"), None),
        P(("groups", "leaf", "sample")),
        P(),
        P(),
        P(),
        P(),
        P(),
        P(),
    )
    out_specs = (
        P(("groups", "leaf", "sample"), None),
        P(("groups", "leaf"), None),
        P(("groups", "leaf"), None),
        P(("groups", "leaf"), None),
        P(("groups", "leaf"), None),
        P(("groups", "leaf")),
        P(("groups", "leaf")),
    )
    return jax.shard_map(local, mesh=mesh, in_specs=in_specs, out_specs=out_specs, check_vma=False)
```

```python
import functools
import math

import jax
import jax.numpy as jnp
from jax import lax
from jax.experimental import pallas as pl
from jax.experimental.pallas import tpu as pltpu
from jax.sharding import PartitionSpec as P

HEADS = 8
BALL = 256
HEAD_DIM = 32
GROUP = 128
META = 16
GAINS = 8

EPSILON = 1e-06
GELU_COEF = math.sqrt(2.0 / math.pi)
ATT_SCALE = HEAD_DIM ** (-0.5)
BF16 = jnp.bfloat16
F32 = jnp.float32


def mm(a, b):
    return lax.dot_general(a, b, (((1,), (0,)), ((), ())), preferred_element_type=F32)


def mm_nt(a, b):
    return lax.dot_general(a, b, (((1,), (1,)), ((), ())), preferred_element_type=F32)


def mm_tn(a, b):
    return lax.dot_general(a, b, (((0,), (0,)), ((), ())), preferred_element_type=F32)


def iota(shape, dim):
    return lax.broadcasted_iota(jnp.int32, shape, dim)


def one_hot(positions, shape, dim):
    return jnp.where(iota(shape, dim) == positions, 1.0, 0.0).astype(BF16)


def column_of(row):
    return jnp.broadcast_to(row, (128, row.shape[1])).T


def lane_tile(column, width):
    return jnp.concatenate([column] * (width // 128), axis=1)


class Arriving:
    def __init__(self, ref, copies):
        self.ref, self.copies, self.shape = ref, copies, ref.shape

    def __getitem__(self, where):
        for copy in self.copies:
            copy.wait()
        self.copies = []
        return self.ref[where]


class Leaving:
    def __init__(self, ref, out_ref, sems):
        self.ref, self.out_ref, self.sems, self.shape, self.dtype = ref, out_ref, sems, ref.shape, ref.dtype
        self.copies, self.sent = [], 0

    def __getitem__(self, where):
        return self.ref[where]

    def __setitem__(self, where, value):
        self.ref[where] = value

    def send(self, upto=None):
        upto = self.shape[0] if upto is None else upto
        if upto > self.sent:
            part = pl.ds(self.sent, upto - self.sent)
            copy = pltpu.make_async_copy(self.ref.at[part], self.out_ref.at[part], self.sems.at[len(self.copies)])
            copy.start()
            self.copies.append(copy)
            self.sent = upto


def send(ref, upto=None):
    if isinstance(ref, Leaving):
        ref.send(upto)


def pack_points_kernel(peers, cap, direct, dest_ref, points_ref, slot_ref, *out_refs):
    rows = points_ref.shape[0]
    slots = peers * cap
    dest = dest_ref[...]
    shift = rows.bit_length() - 1
    owner = lax.shift_right_logical(dest, shift)
    target = jnp.bitwise_and(dest, rows - 1)
    owned = jnp.where(iota((peers, rows), 0) == owner, 1.0, 0.0)
    upto = jnp.where(iota((rows, rows), 0) <= iota((rows, rows), 1), 1.0, 0.0).astype(BF16)
    counts = mm(owned.astype(BF16), upto)
    rank = (jnp.sum(counts * owned, axis=0, keepdims=True) - 1.0).astype(jnp.int32)
    slot = owner * cap + rank
    slot_ref[...] = slot
    packed = mm(one_hot(slot, (slots, rows), 0), points_ref[...]).astype(BF16)
    within = one_hot(rank, (cap, rows), 0)
    within = jnp.concatenate([within] * (128 // cap), axis=0)
    high = (lax.shift_right_logical(target, 4) + 1).astype(F32)
    low = jnp.bitwise_and(target, 15).astype(F32)
    high_rows = mm_nt((owned * high).astype(BF16), within)
    low_rows = mm_nt((owned * low).astype(BF16), within)
    if direct:
        (msg_ref,) = out_refs
        msg_ref[:, :cap, :] = packed[:, :128].reshape(peers, cap, 128)
        msg_ref[:, cap : 2 * cap, :] = packed[:, 128:].reshape(peers, cap, 128)
        first = iota((META, 128), 0) == 0
        for peer in range(peers):
            block = jnp.where(first, high_rows[peer : peer + 1], low_rows[peer : peer + 1])
            msg_ref[peer, 2 * cap :, :] = block.astype(BF16)
    else:
        packed_ref, high_ref, low_ref = out_refs
        packed_ref[...] = packed
        high_ref[...] = high_rows
        low_ref[...] = low_rows


def partner(step):
    return (lax.axis_index("leaf") * lax.axis_size("sample") + lax.axis_index("sample")) ^ step


def pack_cot_kernel(slot_ref, cot_ref, *refs):
    rows = cot_ref.shape[0]
    if len(refs) == 1:
        (packed_ref,) = refs
        packed_ref[...] = mm(one_hot(slot_ref[...], (packed_ref.shape[0], rows), 0), cot_ref[...]).astype(BF16)
        return
    *block_refs, packed_ref = refs
    peers, cap, width = packed_ref.shape
    packed = mm(one_hot(slot_ref[...], (peers * cap, rows), 0), cot_ref[...]).astype(BF16)
    packed_ref[...] = packed.reshape(peers, cap, width)
    for step, ref in enumerate(block_refs):
        for mate in range(2):
            ref[mate] = packed_ref[partner(2 * step + mate)]


def regroup_kernel(*refs):
    *pair_refs, mine_ref, mate_ref = refs
    for step, ref in enumerate(pair_refs):
        mine_ref[step] = ref[0]
        mate_ref[step] = ref[1]


def group_heads(rows):
    heads = range(GROUP // HEAD_DIM)
    return jnp.concatenate([head_rows(rows[h * HEAD_DIM : (h + 1) * HEAD_DIM], h) for h in heads], axis=1)


def head_rows(rows, head):
    width = rows.shape[1]
    at = (head * HEAD_DIM) % GROUP
    parts = []
    if at:
        parts.append(jnp.zeros((at, width), rows.dtype))
    parts.append(rows)
    if at + HEAD_DIM < GROUP:
        parts.append(jnp.zeros((GROUP - at - HEAD_DIM, width), rows.dtype))
    return jnp.concatenate(parts, axis=0)


def unpack_points_kernel(cap, peers, direct, *refs):
    if not direct:
        recv_ref, high_ref, low_ref = refs[:3]
        recv = recv_ref[...]
        high_rows, low_rows = high_ref[...], low_ref[...]
    else:
        msg_ref = refs[0]
        left = msg_ref[:, :cap, :].reshape(peers * cap, 128)
        right = msg_ref[:, cap : 2 * cap, :].reshape(peers * cap, 128)
        recv = jnp.concatenate([left, right], axis=1)
        tails = [msg_ref[peer, 2 * cap :, :].astype(F32) for peer in range(peers)]
        high_rows = jnp.concatenate([tail[0:1] for tail in tails], axis=0)
        low_rows = jnp.concatenate([tail[1:2] for tail in tails], axis=0)
    target_ref, target_col_ref, rotated_ref = refs[-3:]
    rows = rotated_ref.shape[1]
    slots = peers * cap
    targets = (high_rows - 1.0) * 16.0 + low_rows
    per_row = 128 // cap
    own_lane = iota((per_row, 128), 1) // cap == iota((per_row, 128), 0)
    pieces = []
    for group in range(slots // 128):
        block = targets[group * per_row : (group + 1) * per_row]
        pieces.append(jnp.sum(jnp.where(own_lane, block, 0.0), axis=0, keepdims=True))
    target = jnp.concatenate(pieces, axis=1)
    target_ref[...] = target.astype(jnp.int32)
    target_col_ref[...] = column_of(target).astype(jnp.int32)
    rotated_ref[...] = mm(one_hot(target.astype(jnp.int32), (rows, slots), 0), recv).T


def forward_kernel(
    rotated_ref, w_qkv_ref, w_out_ref, w_up_ref, gain_attn_ref, gain_mlp_ref,
    qkv_t_ref, kv_ref, scales_ref, norm_one_ref, normed_one_ref, attended_ref, norm_two_ref, normed_two_ref,
    hidden_ref, slope_ref, gain_attn_col_ref, gain_mlp_col_ref, *probs_refs,
):
    rot_t = rotated_ref[...]
    width, rows = rot_t.shape
    gain_attn_col = column_of(gain_attn_ref[...])
    gain_attn_col_ref[...] = gain_attn_col
    gain_mlp_col = column_of(gain_mlp_ref[...])
    gain_mlp_col_ref[...] = gain_mlp_col
    scale_one = lax.rsqrt(jnp.mean(rot_t * rot_t, axis=0, keepdims=True) + EPSILON)
    norm_one = rot_t * scale_one
    norm_one_ref[...] = norm_one
    normed_one = (norm_one * lane_tile(gain_attn_col, rows)).astype(BF16)
    normed_one_ref[...] = normed_one
    qkv_t = mm_tn(w_qkv_ref[...], normed_one).astype(BF16)
    qkv_t_ref[...] = qkv_t
    kv_ref[...] = qkv_t[width:].astype(F32).T.astype(BF16)

    for ball in range(rows // BALL):
        at = ball * BALL
        cols = slice(at, at + BALL)
        for group in range(0, width, GROUP):
            queries = group_heads(qkv_t_ref[group : group + GROUP, cols])
            scores = mm(kv_ref[cols, group : group + GROUP], queries) * ATT_SCALE
            top = jnp.max(scores, axis=0, keepdims=True)
            weights = jnp.exp(scores - top)
            probs = weights * (1.0 / jnp.sum(weights, axis=0, keepdims=True))
            probs_refs[ball][group // GROUP] = probs
            probs_low = probs.astype(BF16)
            for head in range(GROUP // HEAD_DIM):
                own = slice(group + head * HEAD_DIM, group + (head + 1) * HEAD_DIM)
                values = qkv_t_ref[2 * width + own.start : 2 * width + own.stop, cols]
                attended_ref[own, cols] = mm(values, probs_low[:, head * BALL : (head + 1) * BALL]).astype(BF16)

    middle = rot_t + mm_tn(w_out_ref[...], attended_ref[...])
    scale_two = lax.rsqrt(jnp.mean(middle * middle, axis=0, keepdims=True) + EPSILON)
    norm_two = middle * scale_two
    norm_two_ref[...] = norm_two
    normed_two = (norm_two * lane_tile(gain_mlp_col, rows)).astype(BF16)
    normed_two_ref[...] = normed_two
    scales_ref[...] = jnp.where(iota(scales_ref.shape, 0) == 0, scale_one, scale_two)
    step = 256
    for at in range(0, hidden_ref.shape[0], step):
        pre_act = mm_tn(w_up_ref[:, at : at + step], normed_two)
        square = pre_act * pre_act
        tanh_val = jnp.tanh(GELU_COEF * (pre_act + 0.044715 * pre_act * square))
        half = 0.5 * (1.0 + tanh_val)
        hidden_ref[at : at + step, :] = (pre_act * half).astype(BF16)
        slope_ref[at : at + step, :] = half + 0.5 * pre_act * (1.0 - tanh_val * tanh_val) * (
            GELU_COEF * (1.0 + 3.0 * 0.044715 * square)
        )


def norm_backward(grad_normed, norm, scale, gain):
    inner = grad_normed * gain
    return scale * (inner - norm * jnp.mean(inner * norm, axis=0, keepdims=True))


def gain_row(product):
    width = product.shape[1]
    partial = product[:, :128]
    for at in range(128, width, 128):
        partial = partial + product[:, at : at + 128]
    return jnp.sum(partial.T, axis=0, keepdims=True)


def place_blocks(blocks_ref, values, first_row, leaf_size, sample_size):
    step = values.shape[0] // (leaf_size * sample_size)
    for block in range(leaf_size * sample_size):
        leaf, sample = divmod(block, sample_size)
        blocks_ref[sample, leaf, first_row : first_row + step, :] = values[block * step : (block + 1) * step]


def part_blocks(blocks_ref, keep_ref, send_ref):
    low = lax.rem(lax.axis_index("sample"), 2)
    for high in range(keep_ref.shape[0]):
        keep_ref[high] = blocks_ref[2 * high + low]
        send_ref[high] = blocks_ref[2 * high + 1 - low].astype(BF16)


def mlp_weights_kernel(
    arranged, direct, target_ref, hidden_ref, slope_ref, normed_two_ref, w_down_ref, *refs
):
    width, rows = normed_two_ref.shape
    if direct:
        mine_ref, mate_ref, *refs, landing_ref = refs
        for step in range(mine_ref.shape[0]):
            landing_ref[partner(2 * step)] = mine_ref[step]
            landing_ref[partner(2 * step + 1)] = mate_ref[step]
        recv_ref = landing_ref
    else:
        recv_ref, *refs = refs
    grad_pre_ref, cot_t_ref, *mat_refs = refs
    recv = recv_ref[...].reshape(-1, width)
    cot_f = mm(one_hot(target_ref[...], (rows, recv.shape[0]), 0), recv)
    cot = cot_f.astype(BF16)
    cot_t = cot_f.T
    cot_t_ref[...] = cot_t
    cot_t_low = cot_t.astype(BF16)
    normed_two = normed_two_ref[...]
    step = 256
    if arranged:
        keep_ref, send_ref, blocks_ref = mat_refs
        leaf_size, sample_size = lax.axis_size("leaf"), lax.axis_size("sample")
        up_rows = width // leaf_size
        down_rows = hidden_ref.shape[0] // (leaf_size * sample_size)
    else:
        grad_up_ref, grad_down_ref = mat_refs
    for at in range(0, hidden_ref.shape[0], step):
        grad_down = mm(hidden_ref[at : at + step, :], cot)
        grad_pre = (mm(w_down_ref[at : at + step, :], cot_t_low) * slope_ref[at : at + step, :]).astype(BF16)
        grad_pre_ref[at : at + step, :] = grad_pre
        grad_up = mm_nt(normed_two, grad_pre)
        if arranged:
            for leaf in range(leaf_size):
                blocks_ref[at // step, leaf, :up_rows, :] = grad_up[leaf * up_rows : (leaf + 1) * up_rows]
            for block in range(step // down_rows):
                leaf, sample = divmod(at // down_rows + block, sample_size)
                piece = grad_down[block * down_rows : (block + 1) * down_rows]
                blocks_ref[sample, leaf, up_rows:, :] = piece
        else:
            grad_down_ref[at : at + step, :] = grad_down.astype(BF16)
            grad_up_ref[:, at : at + step] = grad_up.astype(BF16)
    if arranged:
        part_blocks(blocks_ref, keep_ref, send_ref)


def mlp_inputs_kernel(
    grad_pre_ref, cot_t_ref, norm_two_ref, scales_ref, attended_ref, w_up_ref, w_out_ref, gain_mlp_ref,
    grad_gain_ref, grad_middle_ref, grad_att_ref, grad_out_ref,
):
    grad_normed = mm(w_up_ref[...], grad_pre_ref[...])
    norm_two = norm_two_ref[...]
    grad_gain_ref[...] = gain_row(grad_normed * norm_two)
    gain = lane_tile(gain_mlp_ref[...], norm_two.shape[1])
    grad_middle = cot_t_ref[...] + norm_backward(grad_normed, norm_two, scales_ref[1:2, :], gain)
    grad_middle_ref[...] = grad_middle
    grad_middle_low = grad_middle.astype(BF16)
    grad_att_ref[...] = mm(w_out_ref[...], grad_middle_low).astype(BF16)
    grad_out_ref[...] = mm_nt(attended_ref[...], grad_middle_low)


def ball_backward(ball, qkv_t_ref, kv_ref, probs_ref, grad_att_ref, grad_rows_ref):
    width = qkv_t_ref.shape[0] // 3
    cols = slice(ball * BALL, (ball + 1) * BALL)
    for group in range(0, width, GROUP):
        upstream = grad_att_ref[group : group + GROUP, cols]
        probs = probs_ref[group // GROUP]
        grad_probs = mm(kv_ref[cols, width + group : width + group + GROUP], group_heads(upstream))
        delta = jnp.sum(grad_probs * probs, axis=0, keepdims=True)
        grad_scores = (probs * (grad_probs - delta)).astype(BF16)
        probs_low = probs.astype(BF16)
        for head in range(GROUP // HEAD_DIM):
            first = group + head * HEAD_DIM
            own, own_key, own_value = (slice(at + first, at + first + HEAD_DIM) for at in (0, width, 2 * width))
            part = slice(head * BALL, (head + 1) * BALL)
            scores_of = grad_scores[:, part]
            grad_rows_ref[own, cols] = (mm(qkv_t_ref[own_key, cols], scores_of) * ATT_SCALE).astype(BF16)
            grad_rows_ref[own_key, cols] = (mm_nt(qkv_t_ref[own, cols], scores_of) * ATT_SCALE).astype(BF16)
            grad_rows_ref[own_value, cols] = mm_nt(grad_att_ref[own, cols], probs_low[:, part]).astype(BF16)


def attention_backward_kernel(
    arranged,
    qkv_t_ref, kv_ref, scales_ref, grad_att_ref, grad_middle_ref, norm_one_ref, normed_one_ref,
    w_qkv_ref, gain_attn_ref, target_col_ref, gain_two_ref, grad_out_ref, *refs,
):
    width, rows = norm_one_ref.shape
    probs_refs, refs = refs[: rows // BALL], refs[rows // BALL :]
    back_ref, *mat_refs, grad_rows_ref = refs
    for ball, probs_ref in enumerate(probs_refs):
        ball_backward(ball, qkv_t_ref, kv_ref, probs_ref, grad_att_ref, grad_rows_ref)
    grad_rows = grad_rows_ref[...]
    grad_normed = mm(w_qkv_ref[...], grad_rows)
    norm_one = norm_one_ref[...]
    gain_one = gain_row(grad_normed * norm_one)
    gain = lane_tile(gain_attn_ref[...], rows)
    grad_rot = grad_middle_ref[...] + norm_backward(grad_normed, norm_one, scales_ref[0:1, :], gain)
    place = one_hot(lane_tile(target_col_ref[...], rows), (back_ref.shape[0], rows), 1)
    back_ref[...] = mm_nt(place, grad_rot.astype(BF16)).astype(BF16)
    normed_one = normed_one_ref[...]
    if not arranged:
        mat_refs[0][...] = mm_nt(normed_one, grad_rows).astype(BF16)
        mat_refs[1][...] = gain_one
        return
    keep_ref, send_ref, blocks_ref = mat_refs
    leaf_size, sample_size = lax.axis_size("leaf"), lax.axis_size("sample")
    step = width // (leaf_size * sample_size)
    for col in range(3):
        grad_qkv = mm_nt(normed_one, grad_rows[col * width : (col + 1) * width])
        place_blocks(blocks_ref, grad_qkv, (1 + col) * step, leaf_size, sample_size)
    place_blocks(blocks_ref, grad_out_ref[...], 0, leaf_size, sample_size)
    row = iota((GAINS, width), 0)
    gains = jnp.where(row == 0, gain_one, jnp.where(row == 1, gain_two_ref[...], 0.0))
    for sample in range(sample_size):
        for leaf in range(leaf_size):
            blocks_ref[sample, leaf, 4 * step :, :] = gains
    part_blocks(blocks_ref, keep_ref, send_ref)


def unpack_kernel(slot_ref, returned_ref, out_ref):
    slots = returned_ref.shape[0]
    slot_col = column_of(slot_ref[...].astype(F32)).astype(jnp.int32)
    place = one_hot(lane_tile(slot_col, slots), (out_ref.shape[0], slots), 1)
    out_ref[...] = mm(place, returned_ref[...]).astype(BF16)


def halve_kernel(axis, bit, keep_ref, got_ref, keep_out_ref, send_out_ref):
    mine = lax.rem(lax.div(lax.axis_index(axis), bit), 2)
    for high in range(keep_out_ref.shape[0]):
        for ref, at in ((keep_out_ref, 2 * high + mine), (send_out_ref, 2 * high + 1 - mine)):
            ref[high] = (keep_ref[at] + got_ref[at].astype(F32)).astype(ref.dtype)


def quarter_kernel(keep_ref, got_ref, keep_out_ref, *send_refs):
    mine = lax.rem(lax.div(lax.axis_index("sample"), 2), 2)
    low = lax.rem(lax.axis_index("leaf"), 2)
    places = ((mine, low), (1 - mine, low), (mine, 1 - low), (1 - mine, 1 - low))
    for ref, (sample, leaf) in zip((keep_out_ref, *send_refs), places):
        for high in range(ref.shape[0]):
            total = keep_ref[sample, 2 * high + leaf] + got_ref[sample, 2 * high + leaf].astype(F32)
            ref[high] = total.astype(ref.dtype)


def join_kernel(counts, *refs):
    ins, (keep_out_ref, send_out_ref) = list(refs[:-2]), refs[-2:]
    mine = lax.rem(lax.div(lax.axis_index("leaf"), 2), 2)
    start = 0
    for count in counts:
        part, ins = ins[:count], ins[count:]
        rows = pl.ds(start, part[0].shape[1])
        for ref, at in ((keep_out_ref, mine), (send_out_ref, 1 - mine)):
            total = part[0][at]
            for got_ref in part[1:]:
                total = total + got_ref[at].astype(F32)
            ref[rows, :] = total.astype(ref.dtype)
        start += part[0].shape[1]


def finish_kernel(keep_ref, got_ref, low_ref, gains_ref):
    total = keep_ref[...] + got_ref[...].astype(F32)
    gains_ref[...] = total[-GAINS:]
    low_ref[0] = total[:-GAINS].astype(BF16)


def assemble_kernel(scale, offsets, mine_ref, mate_ref, up_ref, down_ref, out_ref, qkv_ref):
    size = 2 * len(offsets)
    width = mine_ref.shape[2]
    up_rows, down_rows, out_rows = up_ref.shape[0], down_ref.shape[0] // size, out_ref.shape[0] // size
    me = lax.axis_index("sample")

    def block(source, count):
        return pl.ds(pl.multiple_of(source * count, count), count)

    for index, offset in enumerate(offsets):
        for mate, ref in enumerate((mine_ref, mate_ref)):
            source = me ^ (offset + mate)
            part = ref[index].astype(F32) * scale
            at = up_rows
            up_ref[:, block(source, width)] = part[:at]
            down_ref[block(source, down_rows), :] = part[at : at + down_rows]
            at += down_rows
            out_ref[block(source, out_rows), :] = part[at : at + out_rows]
            at += out_rows
            for col in range(3):
                qkv_ref[block(source, out_rows), col * width : (col + 1) * width] = part[at : at + out_rows]
                at += out_rows


def permute(value, axis, size, bit):
    return lax.ppermute(value, axis, [(i, i ^ bit) for i in range(size)])


def halve(keep, got, axis, bit, name, micros=0.5):
    shape = (keep.shape[0] // 2,) + keep.shape[1:]
    return call(functools.partial(halve_kernel, axis, bit), [(shape, F32), (shape, BF16)], name, micros, keep, got)


def call(kernel, outs, name, micros, *args, scratch=(), hbm_in=False, hbm_out=False, raw_in=0, raw_out=0, blocked=False, limit=16):
    moved = sum(arg.size * arg.dtype.itemsize for arg in args)
    moved += sum(math.prod(shape) * jnp.dtype(dtype).itemsize for shape, dtype in outs)
    vmem = pl.BlockSpec() if blocked else pl.BlockSpec(memory_space=pltpu.VMEM)
    hbm = pl.BlockSpec(memory_space=pltpu.HBM)
    copied_in = len(args) - raw_in if hbm_in else 0
    copied_out = len(outs) - raw_out if hbm_out else 0
    parts = 2

    def body(*refs):
        ins, refs = list(refs[: len(args)]), refs[len(args) :]
        results, refs = list(refs[: len(outs)]), refs[len(outs) :]
        own, refs = refs[: len(scratch)], refs[len(scratch) :]
        in_bufs, refs = refs[:copied_in], refs[copied_in:]
        out_bufs, refs = refs[:copied_out], refs[copied_out:]
        for at, buf in enumerate(in_bufs):
            copy = pltpu.make_async_copy(ins[at], buf, refs[0].at[at])
            copy.start()
            ins[at] = Arriving(buf, [copy])
        for at, buf in enumerate(out_bufs):
            results[at] = Leaving(buf, results[at], refs[-1].at[at])
        kernel(*ins, *results, *own)
        for ref in ins:
            if isinstance(ref, Arriving):
                for copy in ref.copies:
                    copy.wait()
        for ref in results[:copied_out]:
            ref.send()
        for ref in results[:copied_out]:
            for copy in ref.copies:
                copy.wait()

    extra = [pltpu.VMEM(arg.shape, arg.dtype) for arg in args[:copied_in]]
    extra += [pltpu.VMEM(shape, dtype) for shape, dtype in outs[:copied_out]]
    if copied_in:
        extra.append(pltpu.SemaphoreType.DMA((copied_in,)))
    if copied_out:
        extra.append(pltpu.SemaphoreType.DMA((copied_out, parts)))
    return pl.pallas_call(
        body,
        out_shape=[jax.ShapeDtypeStruct(shape, dtype) for shape, dtype in outs],
        in_specs=[hbm if hbm_in else vmem] * (len(args) - raw_in) + [hbm] * raw_in,
        out_specs=[hbm if hbm_out else vmem] * (len(outs) - raw_out) + [hbm] * raw_out,
        scratch_shapes=list(scratch) + extra,
        compiler_params=pltpu.CompilerParams(vmem_limit_bytes=limit * 1024 * 1024),
        cost_estimate=pl.CostEstimate(flops=int(micros * 1.1e9), bytes_accessed=moved, transcendentals=0),
        name=name,
    )(*args)


def exchange(flat, axes, peers):
    moved = lax.all_to_all(
        flat.reshape((peers, -1) + flat.shape[1:]), axes, split_axis=0, concat_axis=0, tiled=True
    )
    return moved.reshape(flat.shape)


def local(points, cotangent, dest_pos, w_qkv, w_out, w_up, w_down, gain_attn, gain_mlp):
    rows, width = points.shape
    hidden_width = w_up.shape[1]
    axes = ("leaf", "sample")
    peers = lax.axis_size(axes)
    leaf_size, sample_size = lax.axis_size("leaf"), lax.axis_size("sample")
    cap = 2 * rows // peers
    slots = peers * cap
    balls = rows // BALL
    direct = cap % 16 == 0
    paired = leaf_size & (leaf_size - 1) == 0 and sample_size & (sample_size - 1) == 0 and min(leaf_size, sample_size) > 1
    arranged = paired and width % (16 * peers) == 0 and hidden_width == sample_size * width and (leaf_size, sample_size) == (4, 4)
    inv_root = 1.0 / math.sqrt(rows * peers)

    msg_rows = 2 * cap + META
    if direct:
        outs = [((peers, msg_rows, 128), BF16)]
    else:
        outs = [((slots, width), BF16), ((peers, 128), F32), ((peers, 128), F32)]
    slot, *message = call(
        functools.partial(pack_points_kernel, peers, cap, direct),
        [((1, rows), jnp.int32)] + outs, "pack_points", 2, dest_pos.reshape(1, rows), points, hbm_in=True, hbm_out=True, limit=60,
    )
    if direct:
        forward_args = [exchange(message[0].reshape(-1, 128), axes, peers).reshape(peers, msg_rows, 128)]
    else:
        packed, high, low = message
        tail = jnp.stack([high, low], axis=1).astype(BF16)
        halves = packed.reshape(peers, cap, 2, 128).transpose(0, 2, 1, 3).reshape(peers, 2 * cap, 128)
        flat = jnp.concatenate([halves, tail], axis=1).reshape(-1, 128)
        arrived = exchange(flat, axes, peers).reshape(peers, 2 * cap + 2, 128)
        halves = arrived[:, : 2 * cap].reshape(peers, 2, cap, 128).transpose(0, 2, 1, 3).reshape(slots, width)
        forward_args = [halves, arrived[:, 2 * cap].astype(F32), arrived[:, 2 * cap + 1].astype(F32)]
    by_permute = direct and paired and peers <= 16
    if by_permute:
        packed_cot = call(
            pack_cot_kernel, [((2, cap, width), BF16)] * (peers // 2), "pack_cot", 1, slot, cotangent,
            scratch=[pltpu.VMEM((peers, cap, width), BF16)],
        )
        pairs = [packed_cot[0]] + [permute(packed_cot[step], axes, peers, 2 * step) for step in range(1, peers // 2)]
        *pairs[1:3], forward_args[0] = lax.optimization_barrier((*pairs[1:3], forward_args[0]))
    else:
        (packed_cot,) = call(pack_cot_kernel, [((slots, width), BF16)], "pack_cot", 1, slot, cotangent)
        arrived_cot = [exchange(packed_cot, axes, peers)]
    target, target_col, rotated = call(
        functools.partial(unpack_points_kernel, cap, peers, direct),
        [((1, slots), jnp.int32), ((slots, 128), jnp.int32), ((width, rows), F32)],
        "unpack_points", 2, *forward_args,
    )
    (
        qkv_t, kv, scales, norm_one, normed_one, attended, norm_two, normed_two, hidden, slope,
        gain_attn_col, gain_mlp_col, *probs,
    ) = call(
        forward_kernel,
        [
            ((3 * width, rows), BF16), ((rows, 2 * width), BF16), ((8, rows), F32),
            ((width, rows), F32), ((width, rows), BF16), ((width, rows), BF16),
            ((width, rows), F32), ((width, rows), BF16),
            ((hidden_width, rows), BF16), ((hidden_width, rows), F32), ((width, 128), F32), ((width, 128), F32),
        ] + [((width // GROUP, BALL, GROUP // HEAD_DIM * BALL), F32)] * balls,
        "forward", 7, rotated, w_qkv, w_out, w_up, gain_attn.reshape(1, width), gain_mlp.reshape(1, width),
    )
    if by_permute:
        scales, *pairs = lax.optimization_barrier((scales, *pairs))
        half = ((peers // 2, cap, width), BF16)
        mine, for_mate = call(regroup_kernel, [half] * 2, "regroup", 0.3, *pairs)
        arrived_cot = [mine, permute(for_mate, axes, peers, 1)]
    mlp_scratch, qkv_scratch = [], []
    if arranged:
        halved = (sample_size // 2, leaf_size)
        mlp_rows = width // leaf_size + hidden_width // peers
        qkv_rows = 4 * width // peers + GAINS
        mlp_mats = [(halved + (mlp_rows, width), F32), (halved + (mlp_rows, width), BF16)]
        qkv_mats = [(halved + (qkv_rows, width), F32), (halved + (qkv_rows, width), BF16)]
        mlp_scratch = [pltpu.VMEM((sample_size, leaf_size, mlp_rows, width), F32)]
        qkv_scratch = [pltpu.VMEM((sample_size, leaf_size, qkv_rows, width), F32)]
    else:
        mlp_mats = [(w_up.shape, BF16), (w_down.shape, BF16)]
        qkv_mats = [(w_qkv.shape, BF16), ((1, width), F32)]
    grad_pre, cot_t, *mlp_grads = call(
        functools.partial(mlp_weights_kernel, arranged, by_permute),
        [((hidden_width, rows), BF16), ((width, rows), F32)] + mlp_mats,
        "mlp_weights", 2.5, target, hidden, slope, normed_two, w_down, *arrived_cot,
        scratch=mlp_scratch + ([pltpu.VMEM((peers, cap, width), BF16)] if by_permute else []),
    )
    gain_two, grad_middle, grad_att, grad_out = call(
        mlp_inputs_kernel,
        [((1, width), F32), ((width, rows), F32), ((width, rows), BF16), ((width, width), F32)],
        "mlp_inputs", 1.5, grad_pre, cot_t, norm_two, scales, attended, w_up, w_out, gain_mlp_col,
    )
    if arranged:
        keep_mlp, send_mlp = mlp_grads
        got_mlp = permute(send_mlp, "sample", sample_size, 1)
        bit = 2
        while bit < sample_size:
            keep_mlp, send_mlp = halve(keep_mlp, got_mlp, "sample", bit, "halve_mlp")
            grad_att, send_mlp = lax.optimization_barrier((grad_att, send_mlp))
            got_mlp = permute(send_mlp, "sample", sample_size, bit)
            bit *= 2
    back, *qkv_grads = call(
        functools.partial(attention_backward_kernel, arranged),
        [((slots, width), BF16)] + qkv_mats, "attention_backward", 6,
        qkv_t, kv, scales, grad_att, grad_middle, norm_one, normed_one,
        w_qkv, gain_attn_col, target_col, gain_two, grad_out, *probs,
        scratch=qkv_scratch + [pltpu.VMEM((3 * width, rows), BF16)],
    )
    if not arranged:
        returned = exchange(back, axes, peers)
        (grad_points,) = call(unpack_kernel, [((rows, width), BF16)], "unpack", 1, slot, returned, blocked=True)
        up_sum, down_sum, out_sum = reduce_mats([*mlp_grads, grad_out])
        qkv_sum, gain_sum = reduce_mats([qkv_grads[0]], jnp.concatenate([qkv_grads[1], gain_two], axis=0))
        return (
            grad_points, qkv_sum * inv_root, out_sum * inv_root, up_sum * inv_root, down_sum * inv_root,
            gain_sum[0] * inv_root, gain_sum[1] * inv_root,
        )
    keep_qkv, send_qkv = qkv_grads
    got_qkv = permute(send_qkv, "sample", sample_size, 1)
    keep_mlp, leaving = halve(keep_mlp[0], got_mlp[0], "leaf", 1, "leaf_mlp", 1.0)
    got_qkv, leaving = lax.optimization_barrier((got_qkv, leaving))
    quarter = (leaf_size // 2, qkv_rows, width)
    keep_qkv, send_sample, send_leaf, send_both = call(
        quarter_kernel, [(quarter, F32)] + [(quarter, BF16)] * 3, "quarter_qkv", 0.5, keep_qkv, got_qkv
    )
    back = lax.optimization_barrier((back, leaving, send_sample))[0]
    returned = exchange(back, axes, peers)
    (grad_points,) = call(unpack_kernel, [((rows, width), BF16)], "unpack", 1, slot, returned, blocked=True)
    joined = (mlp_rows + qkv_rows, width)
    keep, leaving = call(
        functools.partial(join_kernel, (2, 4)), [(joined, F32), (joined, BF16)], "leaf_last", 0.5,
        keep_mlp, permute(leaving, "leaf", leaf_size, 1), keep_qkv,
        permute(send_sample, "sample", sample_size, 2),
        permute(send_leaf, "leaf", leaf_size, 1),
        permute(send_both, axes, peers, sample_size + 2),
    )
    got = permute(leaving, "leaf", leaf_size, 2)
    low, gains = call(
        finish_kernel, [((1, mlp_rows + qkv_rows - GAINS, width), BF16), ((GAINS, width), F32)], "finish", 3.5, keep, got
    )
    offsets = [0]
    bit = sample_size // 2
    while bit > 1:
        low = jnp.concatenate([low, permute(low, "sample", sample_size, bit)], axis=0)
        offsets += [offset ^ bit for offset in offsets]
        bit //= 2
    mate = permute(low, "sample", sample_size, 1)
    share = width // leaf_size
    gains = lax.dynamic_slice(gains, (0, lax.axis_index("leaf") * share), (2, share)) * inv_root
    gain_one, gain_two = gains[0], gains[1]
    gain_one, gain_two, mate = lax.optimization_barrier((gain_one, gain_two, mate))
    up_sum, down_sum, out_sum, qkv_sum = call(
        functools.partial(assemble_kernel, inv_root, offsets),
        [
            ((share, hidden_width), F32), ((hidden_width // leaf_size, width), F32), ((share, width), F32),
            ((share, 3 * width), F32),
        ],
        "assemble", 1, low, mate, blocked=True,
    )
    return (grad_points, qkv_sum, out_sum, up_sum, down_sum, gain_one, gain_two)


def reduce_mats(mats, gains=None):
    leaf_size = lax.axis_size("leaf")
    sample_size = lax.axis_size("sample")
    me = lax.axis_index("sample")
    pieces = []
    for mat in mats:
        pieces.append(mat.reshape(leaf_size, sample_size, -1, 128).transpose(1, 0, 2, 3))
    if gains is not None:
        gain_block = gains.reshape(2, leaf_size, -1).transpose(1, 0, 2).reshape(1, leaf_size, 1, -1)
        gain_block = jnp.pad(gain_block, ((0, 0), (0, 0), (0, 15), (0, 128 - gain_block.shape[3])))
        pieces.append(jnp.broadcast_to(gain_block, (sample_size,) + gain_block.shape[1:]))
    current = jnp.concatenate(pieces, axis=2).astype(jnp.bfloat16)
    bit = 1
    while bit < sample_size:
        split = current.reshape((current.shape[0] // 2, 2) + current.shape[1:])
        mine = (me // bit) % 2
        keep = lax.dynamic_index_in_dim(split, mine, 1, keepdims=False)
        send = lax.dynamic_index_in_dim(split, 1 - mine, 1, keepdims=False)
        got = lax.ppermute(send, "sample", [(i, i ^ bit) for i in range(sample_size)])
        current = (keep.astype(jnp.float32) + got.astype(jnp.float32)).astype(jnp.bfloat16)
        bit *= 2
    current = lax.all_to_all(current[0], "leaf", split_axis=0, concat_axis=0, tiled=True)
    total = jnp.sum(current.astype(jnp.float32), axis=0)
    low = total.astype(jnp.bfloat16)
    gathered = jnp.zeros((sample_size,) + low.shape, jnp.bfloat16)
    for step in range(sample_size):
        got = low if step == 0 else lax.ppermute(low, "sample", [(i, i ^ step) for i in range(sample_size)])
        gathered = lax.dynamic_update_index_in_dim(gathered, got, me ^ step, 0)
    results = []
    start = 0
    for mat in mats:
        rows = mat.size // (leaf_size * sample_size * 128)
        part = gathered[:, start : start + rows].astype(jnp.float32)
        results.append(part.reshape(mat.shape[0] // leaf_size, mat.shape[1]))
        start += rows
    if gains is not None:
        width = gains.shape[1] // leaf_size
        results.append(total[start, : 2 * width].reshape(2, width))
    return results


def solution(mesh):
    in_specs = (
        P(("groups", "leaf", "sample"), None),
        P(("groups", "leaf", "sample"), None),
        P(("groups", "leaf", "sample")),
        P(),
        P(),
        P(),
        P(),
        P(),
        P(),
    )
    out_specs = (
        P(("groups", "leaf", "sample"), None),
        P(("groups", "leaf"), None),
        P(("groups", "leaf"), None),
        P(("groups", "leaf"), None),
        P(("groups", "leaf"), None),
        P(("groups", "leaf")),
        P(("groups", "leaf")),
    )
    return jax.shard_map(local, mesh=mesh, in_specs=in_specs, out_specs=out_specs, check_vma=False)
```

```python
import functools
import math

import jax
import jax.numpy as jnp
from jax import lax
from jax.experimental import pallas as pl
from jax.experimental.pallas import tpu as pltpu
from jax.sharding import PartitionSpec as P

HEADS = 8
BALL = 256
HEAD_DIM = 32
GROUP = 128
META = 16
GAINS = 8

EPSILON = 1e-06
GELU_COEF = math.sqrt(2.0 / math.pi)
ATT_SCALE = HEAD_DIM ** (-0.5)
BF16 = jnp.bfloat16
F32 = jnp.float32


def mm(a, b):
    return lax.dot_general(a, b, (((1,), (0,)), ((), ())), preferred_element_type=F32)


def mm_nt(a, b):
    return lax.dot_general(a, b, (((1,), (1,)), ((), ())), preferred_element_type=F32)


def mm_tn(a, b):
    return lax.dot_general(a, b, (((0,), (0,)), ((), ())), preferred_element_type=F32)


def iota(shape, dim):
    return lax.broadcasted_iota(jnp.int32, shape, dim)


def one_hot(positions, shape, dim):
    return jnp.where(iota(shape, dim) == positions, 1.0, 0.0).astype(BF16)


def column_of(row):
    return jnp.broadcast_to(row, (128, row.shape[1])).T


def lane_tile(column, width):
    return jnp.concatenate([column] * (width // 128), axis=1)


class Arriving:
    def __init__(self, ref, copies):
        self.ref, self.copies, self.shape = ref, copies, ref.shape

    def __getitem__(self, where):
        for copy in self.copies:
            copy.wait()
        self.copies = []
        return self.ref[where]


class Leaving:
    def __init__(self, ref, out_ref, sems):
        self.ref, self.out_ref, self.sems, self.shape, self.dtype = ref, out_ref, sems, ref.shape, ref.dtype
        self.copies, self.sent = [], 0

    def __getitem__(self, where):
        return self.ref[where]

    def __setitem__(self, where, value):
        self.ref[where] = value

    def send(self, upto=None):
        upto = self.shape[0] if upto is None else upto
        if upto > self.sent:
            part = pl.ds(self.sent, upto - self.sent)
            copy = pltpu.make_async_copy(self.ref.at[part], self.out_ref.at[part], self.sems.at[len(self.copies)])
            copy.start()
            self.copies.append(copy)
            self.sent = upto


def send(ref, upto=None):
    if isinstance(ref, Leaving):
        ref.send(upto)


def pack_points_kernel(peers, cap, direct, dest_ref, points_ref, slot_ref, *out_refs):
    rows = points_ref.shape[0]
    slots = peers * cap
    dest = dest_ref[...]
    shift = rows.bit_length() - 1
    owner = lax.shift_right_logical(dest, shift)
    target = jnp.bitwise_and(dest, rows - 1)
    owned = jnp.where(iota((peers, rows), 0) == owner, 1.0, 0.0)
    upto = jnp.where(iota((rows, rows), 0) <= iota((rows, rows), 1), 1.0, 0.0).astype(BF16)
    counts = mm(owned.astype(BF16), upto)
    rank = (jnp.sum(counts * owned, axis=0, keepdims=True) - 1.0).astype(jnp.int32)
    slot = owner * cap + rank
    slot_ref[...] = slot
    packed = mm(one_hot(slot, (slots, rows), 0), points_ref[...]).astype(BF16)
    within = one_hot(rank, (cap, rows), 0)
    within = jnp.concatenate([within] * (128 // cap), axis=0)
    high = (lax.shift_right_logical(target, 4) + 1).astype(F32)
    low = jnp.bitwise_and(target, 15).astype(F32)
    high_rows = mm_nt((owned * high).astype(BF16), within)
    low_rows = mm_nt((owned * low).astype(BF16), within)
    if direct:
        (msg_ref,) = out_refs
        msg_ref[:, :cap, :] = packed[:, :128].reshape(peers, cap, 128)
        msg_ref[:, cap : 2 * cap, :] = packed[:, 128:].reshape(peers, cap, 128)
        first = iota((META, 128), 0) == 0
        for peer in range(peers):
            block = jnp.where(first, high_rows[peer : peer + 1], low_rows[peer : peer + 1])
            msg_ref[peer, 2 * cap :, :] = block.astype(BF16)
    else:
        packed_ref, high_ref, low_ref = out_refs
        packed_ref[...] = packed
        high_ref[...] = high_rows
        low_ref[...] = low_rows


def partner(step):
    return (lax.axis_index("leaf") * lax.axis_size("sample") + lax.axis_index("sample")) ^ step


def pack_cot_kernel(slot_ref, cot_ref, *refs):
    rows = cot_ref.shape[0]
    if len(refs) == 1:
        (packed_ref,) = refs
        packed_ref[...] = mm(one_hot(slot_ref[...], (packed_ref.shape[0], rows), 0), cot_ref[...]).astype(BF16)
        return
    *block_refs, packed_ref = refs
    peers, cap, width = packed_ref.shape
    packed = mm(one_hot(slot_ref[...], (peers * cap, rows), 0), cot_ref[...]).astype(BF16)
    packed_ref[...] = packed.reshape(peers, cap, width)
    for step, ref in enumerate(block_refs):
        for mate in range(2):
            ref[mate] = packed_ref[partner(2 * step + mate)]


def regroup_kernel(*refs):
    *pair_refs, mine_ref, mate_ref = refs
    for step, ref in enumerate(pair_refs):
        mine_ref[step] = ref[0]
        mate_ref[step] = ref[1]


def group_heads(rows):
    heads = range(GROUP // HEAD_DIM)
    return jnp.concatenate([head_rows(rows[h * HEAD_DIM : (h + 1) * HEAD_DIM], h) for h in heads], axis=1)


def head_rows(rows, head):
    width = rows.shape[1]
    at = (head * HEAD_DIM) % GROUP
    parts = []
    if at:
        parts.append(jnp.zeros((at, width), rows.dtype))
    parts.append(rows)
    if at + HEAD_DIM < GROUP:
        parts.append(jnp.zeros((GROUP - at - HEAD_DIM, width), rows.dtype))
    return jnp.concatenate(parts, axis=0)


def unpack_points_kernel(cap, peers, direct, *refs):
    if not direct:
        recv_ref, high_ref, low_ref = refs[:3]
        recv = recv_ref[...]
        high_rows, low_rows = high_ref[...], low_ref[...]
    else:
        msg_ref = refs[0]
        left = msg_ref[:, :cap, :].reshape(peers * cap, 128)
        right = msg_ref[:, cap : 2 * cap, :].reshape(peers * cap, 128)
        recv = jnp.concatenate([left, right], axis=1)
        tails = [msg_ref[peer, 2 * cap :, :].astype(F32) for peer in range(peers)]
        high_rows = jnp.concatenate([tail[0:1] for tail in tails], axis=0)
        low_rows = jnp.concatenate([tail[1:2] for tail in tails], axis=0)
    target_ref, target_col_ref, rotated_ref = refs[-3:]
    rows = rotated_ref.shape[1]
    slots = peers * cap
    targets = (high_rows - 1.0) * 16.0 + low_rows
    per_row = 128 // cap
    own_lane = iota((per_row, 128), 1) // cap == iota((per_row, 128), 0)
    pieces = []
    for group in range(slots // 128):
        block = targets[group * per_row : (group + 1) * per_row]
        pieces.append(jnp.sum(jnp.where(own_lane, block, 0.0), axis=0, keepdims=True))
    target = jnp.concatenate(pieces, axis=1)
    target_ref[...] = target.astype(jnp.int32)
    target_col_ref[...] = column_of(target).astype(jnp.int32)
    rotated_ref[...] = mm(one_hot(target.astype(jnp.int32), (rows, slots), 0), recv).T


def forward_kernel(
    rotated_ref, w_qkv_ref, w_out_ref, w_up_ref, gain_attn_ref, gain_mlp_ref,
    qkv_t_ref, kv_ref, scales_ref, norm_one_ref, normed_one_ref, attended_ref, norm_two_ref, normed_two_ref,
    hidden_ref, slope_ref, gain_attn_col_ref, gain_mlp_col_ref, *probs_refs,
):
    rot_t = rotated_ref[...]
    width, rows = rot_t.shape
    gain_attn_col = column_of(gain_attn_ref[...])
    gain_attn_col_ref[...] = gain_attn_col
    gain_mlp_col = column_of(gain_mlp_ref[...])
    gain_mlp_col_ref[...] = gain_mlp_col
    scale_one = lax.rsqrt(jnp.mean(rot_t * rot_t, axis=0, keepdims=True) + EPSILON)
    norm_one = rot_t * scale_one
    norm_one_ref[...] = norm_one
    normed_one = (norm_one * lane_tile(gain_attn_col, rows)).astype(BF16)
    normed_one_ref[...] = normed_one
    qkv_t = mm_tn(w_qkv_ref[...], normed_one).astype(BF16)
    qkv_t_ref[...] = qkv_t
    kv_ref[...] = qkv_t[width:].astype(F32).T.astype(BF16)

    for ball in range(rows // BALL):
        at = ball * BALL
        cols = slice(at, at + BALL)
        for group in range(0, width, GROUP):
            queries = group_heads(qkv_t_ref[group : group + GROUP, cols])
            scores = mm(kv_ref[cols, group : group + GROUP], queries) * ATT_SCALE
            top = jnp.max(scores, axis=0, keepdims=True)
            weights = jnp.exp(scores - top)
            probs = weights * (1.0 / jnp.sum(weights, axis=0, keepdims=True))
            probs_refs[ball][group // GROUP] = probs
            probs_low = probs.astype(BF16)
            for head in range(GROUP // HEAD_DIM):
                own = slice(group + head * HEAD_DIM, group + (head + 1) * HEAD_DIM)
                values = qkv_t_ref[2 * width + own.start : 2 * width + own.stop, cols]
                attended_ref[own, cols] = mm(values, probs_low[:, head * BALL : (head + 1) * BALL]).astype(BF16)

    middle = rot_t + mm_tn(w_out_ref[...], attended_ref[...])
    scale_two = lax.rsqrt(jnp.mean(middle * middle, axis=0, keepdims=True) + EPSILON)
    norm_two = middle * scale_two
    norm_two_ref[...] = norm_two
    normed_two = (norm_two * lane_tile(gain_mlp_col, rows)).astype(BF16)
    normed_two_ref[...] = normed_two
    scales_ref[...] = jnp.where(iota(scales_ref.shape, 0) == 0, scale_one, scale_two)
    step = 256
    for at in range(0, hidden_ref.shape[0], step):
        pre_act = mm_tn(w_up_ref[:, at : at + step], normed_two)
        square = pre_act * pre_act
        tanh_val = jnp.tanh(GELU_COEF * (pre_act + 0.044715 * pre_act * square))
        half = 0.5 * (1.0 + tanh_val)
        hidden_ref[at : at + step, :] = (pre_act * half).astype(BF16)
        slope_ref[at : at + step, :] = half + 0.5 * pre_act * (1.0 - tanh_val * tanh_val) * (
            GELU_COEF * (1.0 + 3.0 * 0.044715 * square)
        )


def norm_backward(grad_normed, norm, scale, gain):
    inner = grad_normed * gain
    return scale * (inner - norm * jnp.mean(inner * norm, axis=0, keepdims=True))


def gain_row(product):
    width = product.shape[1]
    partial = product[:, :128]
    for at in range(128, width, 128):
        partial = partial + product[:, at : at + 128]
    return jnp.sum(partial.T, axis=0, keepdims=True)


def place_blocks(blocks_ref, values, first_row, leaf_size, sample_size):
    step = values.shape[0] // (leaf_size * sample_size)
    for block in range(leaf_size * sample_size):
        leaf, sample = divmod(block, sample_size)
        blocks_ref[sample, leaf, first_row : first_row + step, :] = values[block * step : (block + 1) * step]


def part_blocks(blocks_ref, keep_ref, send_ref):
    low = lax.rem(lax.axis_index("sample"), 2)
    for high in range(keep_ref.shape[0]):
        keep_ref[high] = blocks_ref[2 * high + low]
        send_ref[high] = blocks_ref[2 * high + 1 - low].astype(BF16)


def mlp_weights_kernel(
    arranged, direct, target_ref, hidden_ref, slope_ref, normed_two_ref, w_down_ref, *refs
):
    width, rows = normed_two_ref.shape
    if direct:
        mine_ref, mate_ref, *refs, landing_ref = refs
        for step in range(mine_ref.shape[0]):
            landing_ref[partner(2 * step)] = mine_ref[step]
            landing_ref[partner(2 * step + 1)] = mate_ref[step]
        recv_ref = landing_ref
    else:
        recv_ref, *refs = refs
    grad_pre_ref, cot_t_ref, *mat_refs = refs
    recv = recv_ref[...].reshape(-1, width)
    cot_f = mm(one_hot(target_ref[...], (rows, recv.shape[0]), 0), recv)
    cot = cot_f.astype(BF16)
    cot_t = cot_f.T
    cot_t_ref[...] = cot_t
    cot_t_low = cot_t.astype(BF16)
    normed_two = normed_two_ref[...]
    step = 256
    if arranged:
        keep_ref, send_ref, blocks_ref = mat_refs
        leaf_size, sample_size = lax.axis_size("leaf"), lax.axis_size("sample")
        up_rows = width // leaf_size
        down_rows = hidden_ref.shape[0] // (leaf_size * sample_size)
    else:
        grad_up_ref, grad_down_ref = mat_refs
    for at in range(0, hidden_ref.shape[0], step):
        grad_down = mm(hidden_ref[at : at + step, :], cot)
        grad_pre = (mm(w_down_ref[at : at + step, :], cot_t_low) * slope_ref[at : at + step, :]).astype(BF16)
        grad_pre_ref[at : at + step, :] = grad_pre
        grad_up = mm_nt(normed_two, grad_pre)
        if arranged:
            for leaf in range(leaf_size):
                blocks_ref[at // step, leaf, :up_rows, :] = grad_up[leaf * up_rows : (leaf + 1) * up_rows]
            for block in range(step // down_rows):
                leaf, sample = divmod(at // down_rows + block, sample_size)
                piece = grad_down[block * down_rows : (block + 1) * down_rows]
                blocks_ref[sample, leaf, up_rows:, :] = piece
        else:
            grad_down_ref[at : at + step, :] = grad_down.astype(BF16)
            grad_up_ref[:, at : at + step] = grad_up.astype(BF16)
    if arranged:
        part_blocks(blocks_ref, keep_ref, send_ref)


def mlp_inputs_kernel(
    grad_pre_ref, cot_t_ref, norm_two_ref, scales_ref, attended_ref, w_up_ref, w_out_ref, gain_mlp_ref,
    grad_gain_ref, grad_middle_ref, grad_att_ref, grad_out_ref,
):
    grad_normed = mm(w_up_ref[...], grad_pre_ref[...])
    norm_two = norm_two_ref[...]
    grad_gain_ref[...] = gain_row(grad_normed * norm_two)
    gain = lane_tile(gain_mlp_ref[...], norm_two.shape[1])
    grad_middle = cot_t_ref[...] + norm_backward(grad_normed, norm_two, scales_ref[1:2, :], gain)
    grad_middle_ref[...] = grad_middle
    grad_middle_low = grad_middle.astype(BF16)
    grad_att_ref[...] = mm(w_out_ref[...], grad_middle_low).astype(BF16)
    grad_out_ref[...] = mm_nt(attended_ref[...], grad_middle_low)


def ball_backward(ball, qkv_t_ref, kv_ref, probs_ref, grad_att_ref, grad_rows_ref):
    width = qkv_t_ref.shape[0] // 3
    cols = slice(ball * BALL, (ball + 1) * BALL)
    for group in range(0, width, GROUP):
        upstream = grad_att_ref[group : group + GROUP, cols]
        probs = probs_ref[group // GROUP]
        grad_probs = mm(kv_ref[cols, width + group : width + group + GROUP], group_heads(upstream))
        delta = jnp.sum(grad_probs * probs, axis=0, keepdims=True)
        grad_scores = (probs * (grad_probs - delta)).astype(BF16)
        probs_low = probs.astype(BF16)
        for head in range(GROUP // HEAD_DIM):
            first = group + head * HEAD_DIM
            own, own_key, own_value = (slice(at + first, at + first + HEAD_DIM) for at in (0, width, 2 * width))
            part = slice(head * BALL, (head + 1) * BALL)
            scores_of = grad_scores[:, part]
            grad_rows_ref[own, cols] = (mm(qkv_t_ref[own_key, cols], scores_of) * ATT_SCALE).astype(BF16)
            grad_rows_ref[own_key, cols] = (mm_nt(qkv_t_ref[own, cols], scores_of) * ATT_SCALE).astype(BF16)
            grad_rows_ref[own_value, cols] = mm_nt(grad_att_ref[own, cols], probs_low[:, part]).astype(BF16)


def attention_backward_kernel(
    arranged,
    qkv_t_ref, kv_ref, scales_ref, grad_att_ref, grad_middle_ref, norm_one_ref, normed_one_ref,
    w_qkv_ref, gain_attn_ref, target_col_ref, gain_two_ref, grad_out_ref, *refs,
):
    width, rows = norm_one_ref.shape
    probs_refs, refs = refs[: rows // BALL], refs[rows // BALL :]
    back_ref, *mat_refs, grad_rows_ref = refs
    for ball, probs_ref in enumerate(probs_refs):
        ball_backward(ball, qkv_t_ref, kv_ref, probs_ref, grad_att_ref, grad_rows_ref)
    grad_rows = grad_rows_ref[...]
    grad_normed = mm(w_qkv_ref[...], grad_rows)
    norm_one = norm_one_ref[...]
    gain_one = gain_row(grad_normed * norm_one)
    gain = lane_tile(gain_attn_ref[...], rows)
    grad_rot = grad_middle_ref[...] + norm_backward(grad_normed, norm_one, scales_ref[0:1, :], gain)
    place = one_hot(lane_tile(target_col_ref[...], rows), (back_ref.shape[0], rows), 1)
    back_ref[...] = mm_nt(place, grad_rot.astype(BF16)).astype(BF16)
    normed_one = normed_one_ref[...]
    if not arranged:
        mat_refs[0][...] = mm_nt(normed_one, grad_rows).astype(BF16)
        mat_refs[1][...] = gain_one
        return
    keep_ref, send_ref, blocks_ref = mat_refs
    leaf_size, sample_size = lax.axis_size("leaf"), lax.axis_size("sample")
    step = width // (leaf_size * sample_size)
    for col in range(3):
        grad_qkv = mm_nt(normed_one, grad_rows[col * width : (col + 1) * width])
        place_blocks(blocks_ref, grad_qkv, (1 + col) * step, leaf_size, sample_size)
    place_blocks(blocks_ref, grad_out_ref[...], 0, leaf_size, sample_size)
    row = iota((GAINS, width), 0)
    gains = jnp.where(row == 0, gain_one, jnp.where(row == 1, gain_two_ref[...], 0.0))
    for sample in range(sample_size):
        for leaf in range(leaf_size):
            blocks_ref[sample, leaf, 4 * step :, :] = gains
    part_blocks(blocks_ref, keep_ref, send_ref)


def unpack_kernel(slot_ref, returned_ref, out_ref):
    slots = returned_ref.shape[0]
    slot_col = column_of(slot_ref[...].astype(F32)).astype(jnp.int32)
    place = one_hot(lane_tile(slot_col, slots), (out_ref.shape[0], slots), 1)
    out_ref[...] = mm(place, returned_ref[...]).astype(BF16)


def halve_kernel(axis, bit, keep_ref, got_ref, keep_out_ref, send_out_ref):
    mine = lax.rem(lax.div(lax.axis_index(axis), bit), 2)
    for high in range(keep_out_ref.shape[0]):
        for ref, at in ((keep_out_ref, 2 * high + mine), (send_out_ref, 2 * high + 1 - mine)):
            ref[high] = (keep_ref[at] + got_ref[at].astype(F32)).astype(ref.dtype)


def quarter_kernel(keep_ref, got_ref, keep_out_ref, *send_refs):
    mine = lax.rem(lax.div(lax.axis_index("sample"), 2), 2)
    low = lax.rem(lax.axis_index("leaf"), 2)
    places = ((mine, low), (1 - mine, low), (mine, 1 - low), (1 - mine, 1 - low))
    for ref, (sample, leaf) in zip((keep_out_ref, *send_refs), places):
        for high in range(ref.shape[0]):
            total = keep_ref[sample, 2 * high + leaf] + got_ref[sample, 2 * high + leaf].astype(F32)
            ref[high] = total.astype(ref.dtype)


def join_kernel(counts, *refs):
    ins, (keep_out_ref, send_out_ref) = list(refs[:-2]), refs[-2:]
    mine = lax.rem(lax.div(lax.axis_index("leaf"), 2), 2)
    start = 0
    for count in counts:
        part, ins = ins[:count], ins[count:]
        rows = pl.ds(start, part[0].shape[1])
        for ref, at in ((keep_out_ref, mine), (send_out_ref, 1 - mine)):
            total = part[0][at]
            for got_ref in part[1:]:
                total = total + got_ref[at].astype(F32)
            ref[rows, :] = total.astype(ref.dtype)
        start += part[0].shape[1]


def finish_kernel(keep_ref, got_ref, low_ref, gains_ref):
    total = keep_ref[...] + got_ref[...].astype(F32)
    gains_ref[...] = total[-GAINS:]
    low_ref[0] = total[:-GAINS].astype(BF16)


def assemble_kernel(scale, offsets, mine_ref, mate_ref, up_ref, down_ref, out_ref, qkv_ref):
    size = 2 * len(offsets)
    width = mine_ref.shape[2]
    up_rows, down_rows, out_rows = up_ref.shape[0], down_ref.shape[0] // size, out_ref.shape[0] // size
    me = lax.axis_index("sample")

    def block(source, count):
        return pl.ds(pl.multiple_of(source * count, count), count)

    for index, offset in enumerate(offsets):
        for mate, ref in enumerate((mine_ref, mate_ref)):
            source = me ^ (offset + mate)
            part = ref[index].astype(F32) * scale
            at = up_rows
            up_ref[:, block(source, width)] = part[:at]
            down_ref[block(source, down_rows), :] = part[at : at + down_rows]
            at += down_rows
            out_ref[block(source, out_rows), :] = part[at : at + out_rows]
            at += out_rows
            for col in range(3):
                qkv_ref[block(source, out_rows), col * width : (col + 1) * width] = part[at : at + out_rows]
                at += out_rows


def permute(value, axis, size, bit):
    return lax.ppermute(value, axis, [(i, i ^ bit) for i in range(size)])


def halve(keep, got, axis, bit, name, micros=0.5):
    shape = (keep.shape[0] // 2,) + keep.shape[1:]
    return call(functools.partial(halve_kernel, axis, bit), [(shape, F32), (shape, BF16)], name, micros, keep, got)


def call(kernel, outs, name, micros, *args, scratch=(), hbm_in=False, hbm_out=False, raw_in=0, raw_out=0, blocked=False, limit=16):
    moved = sum(arg.size * arg.dtype.itemsize for arg in args)
    moved += sum(math.prod(shape) * jnp.dtype(dtype).itemsize for shape, dtype in outs)
    vmem = pl.BlockSpec() if blocked else pl.BlockSpec(memory_space=pltpu.VMEM)
    hbm = pl.BlockSpec(memory_space=pltpu.HBM)
    copied_in = len(args) - raw_in if hbm_in else 0
    copied_out = len(outs) - raw_out if hbm_out else 0
    parts = 2

    def body(*refs):
        ins, refs = list(refs[: len(args)]), refs[len(args) :]
        results, refs = list(refs[: len(outs)]), refs[len(outs) :]
        own, refs = refs[: len(scratch)], refs[len(scratch) :]
        in_bufs, refs = refs[:copied_in], refs[copied_in:]
        out_bufs, refs = refs[:copied_out], refs[copied_out:]
        for at, buf in enumerate(in_bufs):
            copy = pltpu.make_async_copy(ins[at], buf, refs[0].at[at])
            copy.start()
            ins[at] = Arriving(buf, [copy])
        for at, buf in enumerate(out_bufs):
            results[at] = Leaving(buf, results[at], refs[-1].at[at])
        kernel(*ins, *results, *own)
        for ref in ins:
            if isinstance(ref, Arriving):
                for copy in ref.copies:
                    copy.wait()
        for ref in results[:copied_out]:
            ref.send()
        for ref in results[:copied_out]:
            for copy in ref.copies:
                copy.wait()

    extra = [pltpu.VMEM(arg.shape, arg.dtype) for arg in args[:copied_in]]
    extra += [pltpu.VMEM(shape, dtype) for shape, dtype in outs[:copied_out]]
    if copied_in:
        extra.append(pltpu.SemaphoreType.DMA((copied_in,)))
    if copied_out:
        extra.append(pltpu.SemaphoreType.DMA((copied_out, parts)))
    return pl.pallas_call(
        body,
        out_shape=[jax.ShapeDtypeStruct(shape, dtype) for shape, dtype in outs],
        in_specs=[hbm if hbm_in else vmem] * (len(args) - raw_in) + [hbm] * raw_in,
        out_specs=[hbm if hbm_out else vmem] * (len(outs) - raw_out) + [hbm] * raw_out,
        scratch_shapes=list(scratch) + extra,
        compiler_params=pltpu.CompilerParams(vmem_limit_bytes=limit * 1024 * 1024),
        cost_estimate=pl.CostEstimate(flops=int(micros * 1.1e9), bytes_accessed=moved, transcendentals=0),
        name=name,
    )(*args)


def exchange(flat, axes, peers):
    moved = lax.all_to_all(
        flat.reshape((peers, -1) + flat.shape[1:]), axes, split_axis=0, concat_axis=0, tiled=True
    )
    return moved.reshape(flat.shape)


def local(points, cotangent, dest_pos, w_qkv, w_out, w_up, w_down, gain_attn, gain_mlp):
    rows, width = points.shape
    hidden_width = w_up.shape[1]
    axes = ("leaf", "sample")
    peers = lax.axis_size(axes)
    leaf_size, sample_size = lax.axis_size("leaf"), lax.axis_size("sample")
    cap = 2 * rows // peers
    slots = peers * cap
    balls = rows // BALL
    direct = cap % 16 == 0
    paired = leaf_size & (leaf_size - 1) == 0 and sample_size & (sample_size - 1) == 0 and min(leaf_size, sample_size) > 1
    arranged = paired and width % (16 * peers) == 0 and hidden_width == sample_size * width and (leaf_size, sample_size) == (4, 4)
    inv_root = 1.0 / math.sqrt(rows * peers)

    msg_rows = 2 * cap + META
    if direct:
        outs = [((peers, msg_rows, 128), BF16)]
    else:
        outs = [((slots, width), BF16), ((peers, 128), F32), ((peers, 128), F32)]
    slot, *message = call(
        functools.partial(pack_points_kernel, peers, cap, direct),
        [((1, rows), jnp.int32)] + outs, "pack_points", 2, dest_pos.reshape(1, rows), points, hbm_in=True, hbm_out=True, limit=60,
    )
    if direct:
        forward_args = [exchange(message[0].reshape(-1, 128), axes, peers).reshape(peers, msg_rows, 128)]
    else:
        packed, high, low = message
        tail = jnp.stack([high, low], axis=1).astype(BF16)
        halves = packed.reshape(peers, cap, 2, 128).transpose(0, 2, 1, 3).reshape(peers, 2 * cap, 128)
        flat = jnp.concatenate([halves, tail], axis=1).reshape(-1, 128)
        arrived = exchange(flat, axes, peers).reshape(peers, 2 * cap + 2, 128)
        halves = arrived[:, : 2 * cap].reshape(peers, 2, cap, 128).transpose(0, 2, 1, 3).reshape(slots, width)
        forward_args = [halves, arrived[:, 2 * cap].astype(F32), arrived[:, 2 * cap + 1].astype(F32)]
    by_permute = direct and paired and peers <= 16
    if by_permute:
        packed_cot = call(
            pack_cot_kernel, [((2, cap, width), BF16)] * (peers // 2), "pack_cot", 1, slot, cotangent,
            scratch=[pltpu.VMEM((peers, cap, width), BF16)],
        )
        pairs = [packed_cot[0]] + [permute(packed_cot[step], axes, peers, 2 * step) for step in range(1, peers // 2)]
        *pairs[1:3], forward_args[0] = lax.optimization_barrier((*pairs[1:3], forward_args[0]))
    else:
        (packed_cot,) = call(pack_cot_kernel, [((slots, width), BF16)], "pack_cot", 1, slot, cotangent)
        arrived_cot = [exchange(packed_cot, axes, peers)]
    target, target_col, rotated = call(
        functools.partial(unpack_points_kernel, cap, peers, direct),
        [((1, slots), jnp.int32), ((slots, 128), jnp.int32), ((width, rows), F32)],
        "unpack_points", 2, *forward_args,
    )
    (
        qkv_t, kv, scales, norm_one, normed_one, attended, norm_two, normed_two, hidden, slope,
        gain_attn_col, gain_mlp_col, *probs,
    ) = call(
        forward_kernel,
        [
            ((3 * width, rows), BF16), ((rows, 2 * width), BF16), ((8, rows), F32),
            ((width, rows), F32), ((width, rows), BF16), ((width, rows), BF16),
            ((width, rows), F32), ((width, rows), BF16),
            ((hidden_width, rows), BF16), ((hidden_width, rows), F32), ((width, 128), F32), ((width, 128), F32),
        ] + [((width // GROUP, BALL, GROUP // HEAD_DIM * BALL), F32)] * balls,
        "forward", 7, rotated, w_qkv, w_out, w_up, gain_attn.reshape(1, width), gain_mlp.reshape(1, width),
    )
    if by_permute:
        scales, *pairs = lax.optimization_barrier((scales, *pairs))
        half = ((peers // 2, cap, width), BF16)
        mine, for_mate = call(regroup_kernel, [half] * 2, "regroup", 0.3, *pairs)
        arrived_cot = [mine, permute(for_mate, axes, peers, 1)]
    mlp_scratch, qkv_scratch = [], []
    if arranged:
        halved = (sample_size // 2, leaf_size)
        mlp_rows = width // leaf_size + hidden_width // peers
        qkv_rows = 4 * width // peers + GAINS
        mlp_mats = [(halved + (mlp_rows, width), F32), (halved + (mlp_rows, width), BF16)]
        qkv_mats = [(halved + (qkv_rows, width), F32), (halved + (qkv_rows, width), BF16)]
        mlp_scratch = [pltpu.VMEM((sample_size, leaf_size, mlp_rows, width), F32)]
        qkv_scratch = [pltpu.VMEM((sample_size, leaf_size, qkv_rows, width), F32)]
    else:
        mlp_mats = [(w_up.shape, BF16), (w_down.shape, BF16)]
        qkv_mats = [(w_qkv.shape, BF16), ((1, width), F32)]
    grad_pre, cot_t, *mlp_grads = call(
        functools.partial(mlp_weights_kernel, arranged, by_permute),
        [((hidden_width, rows), BF16), ((width, rows), F32)] + mlp_mats,
        "mlp_weights", 2.5, target, hidden, slope, normed_two, w_down, *arrived_cot,
        scratch=mlp_scratch + ([pltpu.VMEM((peers, cap, width), BF16)] if by_permute else []),
    )
    gain_two, grad_middle, grad_att, grad_out = call(
        mlp_inputs_kernel,
        [((1, width), F32), ((width, rows), F32), ((width, rows), BF16), ((width, width), F32)],
        "mlp_inputs", 1.5, grad_pre, cot_t, norm_two, scales, attended, w_up, w_out, gain_mlp_col,
    )
    if arranged:
        keep_mlp, send_mlp = mlp_grads
        got_mlp = permute(send_mlp, "sample", sample_size, 1)
        bit = 2
        while bit < sample_size:
            keep_mlp, send_mlp = halve(keep_mlp, got_mlp, "sample", bit, "halve_mlp")
            grad_att, send_mlp = lax.optimization_barrier((grad_att, send_mlp))
            got_mlp = permute(send_mlp, "sample", sample_size, bit)
            bit *= 2
    back, *qkv_grads = call(
        functools.partial(attention_backward_kernel, arranged),
        [((slots, width), BF16)] + qkv_mats, "attention_backward", 6,
        qkv_t, kv, scales, grad_att, grad_middle, norm_one, normed_one,
        w_qkv, gain_attn_col, target_col, gain_two, grad_out, *probs,
        scratch=qkv_scratch + [pltpu.VMEM((3 * width, rows), BF16)],
    )
    if not arranged:
        returned = exchange(back, axes, peers)
        (grad_points,) = call(unpack_kernel, [((rows, width), BF16)], "unpack", 1, slot, returned, blocked=True)
        up_sum, down_sum, out_sum = reduce_mats([*mlp_grads, grad_out])
        qkv_sum, gain_sum = reduce_mats([qkv_grads[0]], jnp.concatenate([qkv_grads[1], gain_two], axis=0))
        return (
            grad_points, qkv_sum * inv_root, out_sum * inv_root, up_sum * inv_root, down_sum * inv_root,
            gain_sum[0] * inv_root, gain_sum[1] * inv_root,
        )
    keep_qkv, send_qkv = qkv_grads
    got_qkv = permute(send_qkv, "sample", sample_size, 1)
    back = lax.optimization_barrier((back, got_mlp))[0]
    keep_mlp, leaving = halve(keep_mlp[0], got_mlp[0], "leaf", 1, "leaf_mlp", 1.0)
    got_qkv, leaving = lax.optimization_barrier((got_qkv, leaving))
    quarter = (leaf_size // 2, qkv_rows, width)
    keep_qkv, send_sample, send_leaf, send_both = call(
        quarter_kernel, [(quarter, F32)] + [(quarter, BF16)] * 3, "quarter_qkv", 0.5, keep_qkv, got_qkv
    )
    returned = exchange(back, axes, peers)
    (grad_points,) = call(unpack_kernel, [((rows, width), BF16)], "unpack", 1, slot, returned, blocked=True)
    joined = (mlp_rows + qkv_rows, width)
    keep, leaving = call(
        functools.partial(join_kernel, (2, 4)), [(joined, F32), (joined, BF16)], "leaf_last", 0.1,
        keep_mlp, permute(leaving, "leaf", leaf_size, 1), keep_qkv,
        permute(send_sample, "sample", sample_size, 2),
        permute(send_leaf, "leaf", leaf_size, 1),
        permute(send_both, axes, peers, sample_size + 2),
    )
    got = permute(leaving, "leaf", leaf_size, 2)
    low, gains = call(
        finish_kernel, [((1, mlp_rows + qkv_rows - GAINS, width), BF16), ((GAINS, width), F32)], "finish", 0.1, keep, got
    )
    offsets = [0]
    bit = sample_size // 2
    while bit > 1:
        low = jnp.concatenate([low, permute(low, "sample", sample_size, bit)], axis=0)
        offsets += [offset ^ bit for offset in offsets]
        bit //= 2
    low, grad_points = lax.optimization_barrier((low, grad_points))
    mate = permute(low, "sample", sample_size, 1)
    share = width // leaf_size
    gains = lax.dynamic_slice(gains, (0, lax.axis_index("leaf") * share), (2, share)) * inv_root
    gain_one, gain_two = gains[0], gains[1]
    gain_one, gain_two, mate = lax.optimization_barrier((gain_one, gain_two, mate))
    up_sum, down_sum, out_sum, qkv_sum = call(
        functools.partial(assemble_kernel, inv_root, offsets),
        [
            ((share, hidden_width), F32), ((hidden_width // leaf_size, width), F32), ((share, width), F32),
            ((share, 3 * width), F32),
        ],
        "assemble", 1, low, mate, blocked=True,
    )
    return (grad_points, qkv_sum, out_sum, up_sum, down_sum, gain_one, gain_two)


def reduce_mats(mats, gains=None):
    leaf_size = lax.axis_size("leaf")
    sample_size = lax.axis_size("sample")
    me = lax.axis_index("sample")
    pieces = []
    for mat in mats:
        pieces.append(mat.reshape(leaf_size, sample_size, -1, 128).transpose(1, 0, 2, 3))
    if gains is not None:
        gain_block = gains.reshape(2, leaf_size, -1).transpose(1, 0, 2).reshape(1, leaf_size, 1, -1)
        gain_block = jnp.pad(gain_block, ((0, 0), (0, 0), (0, 15), (0, 128 - gain_block.shape[3])))
        pieces.append(jnp.broadcast_to(gain_block, (sample_size,) + gain_block.shape[1:]))
    current = jnp.concatenate(pieces, axis=2).astype(jnp.bfloat16)
    bit = 1
    while bit < sample_size:
        split = current.reshape((current.shape[0] // 2, 2) + current.shape[1:])
        mine = (me // bit) % 2
        keep = lax.dynamic_index_in_dim(split, mine, 1, keepdims=False)
        send = lax.dynamic_index_in_dim(split, 1 - mine, 1, keepdims=False)
        got = lax.ppermute(send, "sample", [(i, i ^ bit) for i in range(sample_size)])
        current = (keep.astype(jnp.float32) + got.astype(jnp.float32)).astype(jnp.bfloat16)
        bit *= 2
    current = lax.all_to_all(current[0], "leaf", split_axis=0, concat_axis=0, tiled=True)
    total = jnp.sum(current.astype(jnp.float32), axis=0)
    low = total.astype(jnp.bfloat16)
    gathered = jnp.zeros((sample_size,) + low.shape, jnp.bfloat16)
    for step in range(sample_size):
        got = low if step == 0 else lax.ppermute(low, "sample", [(i, i ^ step) for i in range(sample_size)])
        gathered = lax.dynamic_update_index_in_dim(gathered, got, me ^ step, 0)
    results = []
    start = 0
    for mat in mats:
        rows = mat.size // (leaf_size * sample_size * 128)
        part = gathered[:, start : start + rows].astype(jnp.float32)
        results.append(part.reshape(mat.shape[0] // leaf_size, mat.shape[1]))
        start += rows
    if gains is not None:
        width = gains.shape[1] // leaf_size
        results.append(total[start, : 2 * width].reshape(2, width))
    return results


def solution(mesh):
    in_specs = (
        P(("groups", "leaf", "sample"), None),
        P(("groups", "leaf", "sample"), None),
        P(("groups", "leaf", "sample")),
        P(),
        P(),
        P(),
        P(),
        P(),
        P(),
    )
    out_specs = (
        P(("groups", "leaf", "sample"), None),
        P(("groups", "leaf"), None),
        P(("groups", "leaf"), None),
        P(("groups", "leaf"), None),
        P(("groups", "leaf"), None),
        P(("groups", "leaf")),
        P(("groups", "leaf")),
    )
    return jax.shard_map(local, mesh=mesh, in_specs=in_specs, out_specs=out_specs, check_vma=False)
```

```python
import functools
import math

import jax
import jax.numpy as jnp
from jax import lax
from jax.experimental import pallas as pl
from jax.experimental.pallas import tpu as pltpu
from jax.sharding import PartitionSpec as P

HEADS = 8
BALL = 256
HEAD_DIM = 32
GROUP = 128
META = 16
GAINS = 8

EPSILON = 1e-06
GELU_COEF = math.sqrt(2.0 / math.pi)
ATT_SCALE = HEAD_DIM ** (-0.5)
BF16 = jnp.bfloat16
F32 = jnp.float32


def mm(a, b):
    return lax.dot_general(a, b, (((1,), (0,)), ((), ())), preferred_element_type=F32)


def mm_nt(a, b):
    return lax.dot_general(a, b, (((1,), (1,)), ((), ())), preferred_element_type=F32)


def mm_tn(a, b):
    return lax.dot_general(a, b, (((0,), (0,)), ((), ())), preferred_element_type=F32)


def iota(shape, dim):
    return lax.broadcasted_iota(jnp.int32, shape, dim)


def one_hot(positions, shape, dim):
    return jnp.where(iota(shape, dim) == positions, 1.0, 0.0).astype(BF16)


def column_of(row):
    return jnp.broadcast_to(row, (128, row.shape[1])).T


def lane_tile(column, width):
    return jnp.concatenate([column] * (width // 128), axis=1)


class Arriving:
    def __init__(self, ref, copies):
        self.ref, self.copies, self.shape = ref, copies, ref.shape

    def __getitem__(self, where):
        for copy in self.copies:
            copy.wait()
        self.copies = []
        return self.ref[where]


class Leaving:
    def __init__(self, ref, out_ref, sems):
        self.ref, self.out_ref, self.sems, self.shape, self.dtype = ref, out_ref, sems, ref.shape, ref.dtype
        self.copies, self.sent = [], 0

    def __getitem__(self, where):
        return self.ref[where]

    def __setitem__(self, where, value):
        self.ref[where] = value

    def send(self, upto=None):
        upto = self.shape[0] if upto is None else upto
        if upto > self.sent:
            part = pl.ds(self.sent, upto - self.sent)
            copy = pltpu.make_async_copy(self.ref.at[part], self.out_ref.at[part], self.sems.at[len(self.copies)])
            copy.start()
            self.copies.append(copy)
            self.sent = upto


def send(ref, upto=None):
    if isinstance(ref, Leaving):
        ref.send(upto)


def pack_points_kernel(peers, cap, direct, dest_ref, points_ref, slot_ref, *out_refs):
    rows = points_ref.shape[0]
    slots = peers * cap
    dest = dest_ref[...]
    shift = rows.bit_length() - 1
    owner = lax.shift_right_logical(dest, shift)
    target = jnp.bitwise_and(dest, rows - 1)
    owned = jnp.where(iota((peers, rows), 0) == owner, 1.0, 0.0)
    upto = jnp.where(iota((rows, rows), 0) <= iota((rows, rows), 1), 1.0, 0.0).astype(BF16)
    counts = mm(owned.astype(BF16), upto)
    rank = (jnp.sum(counts * owned, axis=0, keepdims=True) - 1.0).astype(jnp.int32)
    slot = owner * cap + rank
    slot_ref[...] = slot
    packed = mm(one_hot(slot, (slots, rows), 0), points_ref[...]).astype(BF16)
    within = one_hot(rank, (cap, rows), 0)
    within = jnp.concatenate([within] * (128 // cap), axis=0)
    high = (lax.shift_right_logical(target, 4) + 1).astype(F32)
    low = jnp.bitwise_and(target, 15).astype(F32)
    high_rows = mm_nt((owned * high).astype(BF16), within)
    low_rows = mm_nt((owned * low).astype(BF16), within)
    if direct:
        (msg_ref,) = out_refs
        msg_ref[:, :cap, :] = packed[:, :128].reshape(peers, cap, 128)
        msg_ref[:, cap : 2 * cap, :] = packed[:, 128:].reshape(peers, cap, 128)
        first = iota((META, 128), 0) == 0
        for peer in range(peers):
            block = jnp.where(first, high_rows[peer : peer + 1], low_rows[peer : peer + 1])
            msg_ref[peer, 2 * cap :, :] = block.astype(BF16)
    else:
        packed_ref, high_ref, low_ref = out_refs
        packed_ref[...] = packed
        high_ref[...] = high_rows
        low_ref[...] = low_rows


def partner(step):
    return (lax.axis_index("leaf") * lax.axis_size("sample") + lax.axis_index("sample")) ^ step


def pack_cot_kernel(slot_ref, cot_ref, *refs):
    rows = cot_ref.shape[0]
    if len(refs) == 1:
        (packed_ref,) = refs
        packed_ref[...] = mm(one_hot(slot_ref[...], (packed_ref.shape[0], rows), 0), cot_ref[...]).astype(BF16)
        return
    *block_refs, packed_ref = refs
    peers, cap, width = packed_ref.shape
    packed = mm(one_hot(slot_ref[...], (peers * cap, rows), 0), cot_ref[...]).astype(BF16)
    packed_ref[...] = packed.reshape(peers, cap, width)
    for step, ref in enumerate(block_refs):
        for mate in range(2):
            ref[mate] = packed_ref[partner(2 * step + mate)]


def regroup_kernel(*refs):
    *pair_refs, mine_ref, mate_ref = refs
    for step, ref in enumerate(pair_refs):
        mine_ref[step] = ref[0]
        mate_ref[step] = ref[1]


def group_heads(rows):
    heads = range(GROUP // HEAD_DIM)
    return jnp.concatenate([head_rows(rows[h * HEAD_DIM : (h + 1) * HEAD_DIM], h) for h in heads], axis=1)


def head_rows(rows, head):
    width = rows.shape[1]
    at = (head * HEAD_DIM) % GROUP
    parts = []
    if at:
        parts.append(jnp.zeros((at, width), rows.dtype))
    parts.append(rows)
    if at + HEAD_DIM < GROUP:
        parts.append(jnp.zeros((GROUP - at - HEAD_DIM, width), rows.dtype))
    return jnp.concatenate(parts, axis=0)


def unpack_points_kernel(cap, peers, direct, *refs):
    if not direct:
        recv_ref, high_ref, low_ref = refs[:3]
        recv = recv_ref[...]
        high_rows, low_rows = high_ref[...], low_ref[...]
    else:
        msg_ref = refs[0]
        left = msg_ref[:, :cap, :].reshape(peers * cap, 128)
        right = msg_ref[:, cap : 2 * cap, :].reshape(peers * cap, 128)
        recv = jnp.concatenate([left, right], axis=1)
        tails = [msg_ref[peer, 2 * cap :, :].astype(F32) for peer in range(peers)]
        high_rows = jnp.concatenate([tail[0:1] for tail in tails], axis=0)
        low_rows = jnp.concatenate([tail[1:2] for tail in tails], axis=0)
    target_ref, target_col_ref, rotated_ref = refs[-3:]
    rows = rotated_ref.shape[1]
    slots = peers * cap
    targets = (high_rows - 1.0) * 16.0 + low_rows
    per_row = 128 // cap
    own_lane = iota((per_row, 128), 1) // cap == iota((per_row, 128), 0)
    pieces = []
    for group in range(slots // 128):
        block = targets[group * per_row : (group + 1) * per_row]
        pieces.append(jnp.sum(jnp.where(own_lane, block, 0.0), axis=0, keepdims=True))
    target = jnp.concatenate(pieces, axis=1)
    target_ref[...] = target.astype(jnp.int32)
    target_col_ref[...] = column_of(target).astype(jnp.int32)
    rotated_ref[...] = mm(one_hot(target.astype(jnp.int32), (rows, slots), 0), recv).T


def forward_kernel(
    rotated_ref, w_qkv_ref, w_out_ref, w_up_ref, gain_attn_ref, gain_mlp_ref,
    qkv_t_ref, kv_ref, scales_ref, norm_one_ref, normed_one_ref, attended_ref, norm_two_ref, normed_two_ref,
    hidden_ref, slope_ref, gain_attn_col_ref, gain_mlp_col_ref, *probs_refs,
):
    rot_t = rotated_ref[...]
    width, rows = rot_t.shape
    gain_attn_col = column_of(gain_attn_ref[...])
    gain_attn_col_ref[...] = gain_attn_col
    gain_mlp_col = column_of(gain_mlp_ref[...])
    gain_mlp_col_ref[...] = gain_mlp_col
    scale_one = lax.rsqrt(jnp.mean(rot_t * rot_t, axis=0, keepdims=True) + EPSILON)
    norm_one = rot_t * scale_one
    norm_one_ref[...] = norm_one
    normed_one = (norm_one * lane_tile(gain_attn_col, rows)).astype(BF16)
    normed_one_ref[...] = normed_one
    qkv_t = mm_tn(w_qkv_ref[...], normed_one).astype(BF16)
    qkv_t_ref[...] = qkv_t
    kv_ref[...] = qkv_t[width:].astype(F32).T.astype(BF16)

    for ball in range(rows // BALL):
        at = ball * BALL
        cols = slice(at, at + BALL)
        for group in range(0, width, GROUP):
            queries = group_heads(qkv_t_ref[group : group + GROUP, cols])
            scores = mm(kv_ref[cols, group : group + GROUP], queries) * ATT_SCALE
            top = jnp.max(scores, axis=0, keepdims=True)
            weights = jnp.exp(scores - top)
            probs = weights * (1.0 / jnp.sum(weights, axis=0, keepdims=True))
            probs_refs[ball][group // GROUP] = probs
            probs_low = probs.astype(BF16)
            for head in range(GROUP // HEAD_DIM):
                own = slice(group + head * HEAD_DIM, group + (head + 1) * HEAD_DIM)
                values = qkv_t_ref[2 * width + own.start : 2 * width + own.stop, cols]
                attended_ref[own, cols] = mm(values, probs_low[:, head * BALL : (head + 1) * BALL]).astype(BF16)

    middle = rot_t + mm_tn(w_out_ref[...], attended_ref[...])
    scale_two = lax.rsqrt(jnp.mean(middle * middle, axis=0, keepdims=True) + EPSILON)
    norm_two = middle * scale_two
    norm_two_ref[...] = norm_two
    normed_two = (norm_two * lane_tile(gain_mlp_col, rows)).astype(BF16)
    normed_two_ref[...] = normed_two
    scales_ref[...] = jnp.where(iota(scales_ref.shape, 0) == 0, scale_one, scale_two)
    step = 256
    for at in range(0, hidden_ref.shape[0], step):
        pre_act = mm_tn(w_up_ref[:, at : at + step], normed_two)
        square = pre_act * pre_act
        tanh_val = jnp.tanh(GELU_COEF * (pre_act + 0.044715 * pre_act * square))
        half = 0.5 * (1.0 + tanh_val)
        hidden_ref[at : at + step, :] = (pre_act * half).astype(BF16)
        slope_ref[at : at + step, :] = half + 0.5 * pre_act * (1.0 - tanh_val * tanh_val) * (
            GELU_COEF * (1.0 + 3.0 * 0.044715 * square)
        )


def norm_backward(grad_normed, norm, scale, gain):
    inner = grad_normed * gain
    return scale * (inner - norm * jnp.mean(inner * norm, axis=0, keepdims=True))


def gain_row(product):
    width = product.shape[1]
    partial = product[:, :128]
    for at in range(128, width, 128):
        partial = partial + product[:, at : at + 128]
    return jnp.sum(partial.T, axis=0, keepdims=True)


def place_blocks(blocks_ref, values, first_row, leaf_size, sample_size):
    step = values.shape[0] // (leaf_size * sample_size)
    for block in range(leaf_size * sample_size):
        leaf, sample = divmod(block, sample_size)
        blocks_ref[sample, leaf, first_row : first_row + step, :] = values[block * step : (block + 1) * step]


def part_blocks(blocks_ref, keep_ref, send_ref):
    low = lax.rem(lax.axis_index("sample"), 2)
    for high in range(keep_ref.shape[0]):
        keep_ref[high] = blocks_ref[2 * high + low]
        send_ref[high] = blocks_ref[2 * high + 1 - low].astype(BF16)


def mlp_weights_kernel(
    arranged, direct, target_ref, hidden_ref, slope_ref, normed_two_ref, w_down_ref, *refs
):
    width, rows = normed_two_ref.shape
    if direct:
        mine_ref, mate_ref, *refs, landing_ref = refs
        for step in range(mine_ref.shape[0]):
            landing_ref[partner(2 * step)] = mine_ref[step]
            landing_ref[partner(2 * step + 1)] = mate_ref[step]
        recv_ref = landing_ref
    else:
        recv_ref, *refs = refs
    grad_pre_ref, cot_t_ref, *mat_refs = refs
    recv = recv_ref[...].reshape(-1, width)
    cot_f = mm(one_hot(target_ref[...], (rows, recv.shape[0]), 0), recv)
    cot = cot_f.astype(BF16)
    cot_t = cot_f.T
    cot_t_ref[...] = cot_t
    cot_t_low = cot_t.astype(BF16)
    normed_two = normed_two_ref[...]
    step = 256
    if arranged:
        keep_ref, send_ref, blocks_ref = mat_refs
        leaf_size, sample_size = lax.axis_size("leaf"), lax.axis_size("sample")
        up_rows = width // leaf_size
        down_rows = hidden_ref.shape[0] // (leaf_size * sample_size)
    else:
        grad_up_ref, grad_down_ref = mat_refs
    for at in range(0, hidden_ref.shape[0], step):
        grad_down = mm(hidden_ref[at : at + step, :], cot)
        grad_pre = (mm(w_down_ref[at : at + step, :], cot_t_low) * slope_ref[at : at + step, :]).astype(BF16)
        grad_pre_ref[at : at + step, :] = grad_pre
        grad_up = mm_nt(normed_two, grad_pre)
        if arranged:
            for leaf in range(leaf_size):
                blocks_ref[at // step, leaf, :up_rows, :] = grad_up[leaf * up_rows : (leaf + 1) * up_rows]
            for block in range(step // down_rows):
                leaf, sample = divmod(at // down_rows + block, sample_size)
                piece = grad_down[block * down_rows : (block + 1) * down_rows]
                blocks_ref[sample, leaf, up_rows:, :] = piece
        else:
            grad_down_ref[at : at + step, :] = grad_down.astype(BF16)
            grad_up_ref[:, at : at + step] = grad_up.astype(BF16)
    if arranged:
        part_blocks(blocks_ref, keep_ref, send_ref)


def mlp_inputs_kernel(
    grad_pre_ref, cot_t_ref, norm_two_ref, scales_ref, attended_ref, w_up_ref, w_out_ref, gain_mlp_ref,
    grad_gain_ref, grad_middle_ref, grad_att_ref, grad_out_ref,
):
    grad_normed = mm(w_up_ref[...], grad_pre_ref[...])
    norm_two = norm_two_ref[...]
    grad_gain_ref[...] = gain_row(grad_normed * norm_two)
    gain = lane_tile(gain_mlp_ref[...], norm_two.shape[1])
    grad_middle = cot_t_ref[...] + norm_backward(grad_normed, norm_two, scales_ref[1:2, :], gain)
    grad_middle_ref[...] = grad_middle
    grad_middle_low = grad_middle.astype(BF16)
    grad_att_ref[...] = mm(w_out_ref[...], grad_middle_low).astype(BF16)
    grad_out_ref[...] = mm_nt(attended_ref[...], grad_middle_low)


def ball_backward(ball, qkv_t_ref, kv_ref, probs_ref, grad_att_ref, grad_rows_ref):
    width = qkv_t_ref.shape[0] // 3
    cols = slice(ball * BALL, (ball + 1) * BALL)
    for group in range(0, width, GROUP):
        upstream = grad_att_ref[group : group + GROUP, cols]
        probs = probs_ref[group // GROUP]
        grad_probs = mm(kv_ref[cols, width + group : width + group + GROUP], group_heads(upstream))
        delta = jnp.sum(grad_probs * probs, axis=0, keepdims=True)
        grad_scores = (probs * (grad_probs - delta)).astype(BF16)
        probs_low = probs.astype(BF16)
        for head in range(GROUP // HEAD_DIM):
            first = group + head * HEAD_DIM
            own, own_key, own_value = (slice(at + first, at + first + HEAD_DIM) for at in (0, width, 2 * width))
            part = slice(head * BALL, (head + 1) * BALL)
            scores_of = grad_scores[:, part]
            grad_rows_ref[own, cols] = (mm(qkv_t_ref[own_key, cols], scores_of) * ATT_SCALE).astype(BF16)
            grad_rows_ref[own_key, cols] = (mm_nt(qkv_t_ref[own, cols], scores_of) * ATT_SCALE).astype(BF16)
            grad_rows_ref[own_value, cols] = mm_nt(grad_att_ref[own, cols], probs_low[:, part]).astype(BF16)


def attention_backward_kernel(
    arranged,
    qkv_t_ref, kv_ref, scales_ref, grad_att_ref, grad_middle_ref, norm_one_ref, normed_one_ref,
    w_qkv_ref, gain_attn_ref, target_col_ref, gain_two_ref, grad_out_ref, *refs,
):
    width, rows = norm_one_ref.shape
    probs_refs, refs = refs[: rows // BALL], refs[rows // BALL :]
    back_ref, *mat_refs, grad_rows_ref = refs
    for ball, probs_ref in enumerate(probs_refs):
        ball_backward(ball, qkv_t_ref, kv_ref, probs_ref, grad_att_ref, grad_rows_ref)
    grad_rows = grad_rows_ref[...]
    grad_normed = mm(w_qkv_ref[...], grad_rows)
    norm_one = norm_one_ref[...]
    gain_one = gain_row(grad_normed * norm_one)
    gain = lane_tile(gain_attn_ref[...], rows)
    grad_rot = grad_middle_ref[...] + norm_backward(grad_normed, norm_one, scales_ref[0:1, :], gain)
    place = one_hot(lane_tile(target_col_ref[...], rows), (back_ref.shape[0], rows), 1)
    back_ref[...] = mm_nt(place, grad_rot.astype(BF16)).astype(BF16)
    normed_one = normed_one_ref[...]
    if not arranged:
        mat_refs[0][...] = mm_nt(normed_one, grad_rows).astype(BF16)
        mat_refs[1][...] = gain_one
        return
    keep_ref, send_ref, blocks_ref = mat_refs
    leaf_size, sample_size = lax.axis_size("leaf"), lax.axis_size("sample")
    step = width // (leaf_size * sample_size)
    for col in range(3):
        grad_qkv = mm_nt(normed_one, grad_rows[col * width : (col + 1) * width])
        place_blocks(blocks_ref, grad_qkv, (1 + col) * step, leaf_size, sample_size)
    place_blocks(blocks_ref, grad_out_ref[...], 0, leaf_size, sample_size)
    row = iota((GAINS, width), 0)
    gains = jnp.where(row == 0, gain_one, jnp.where(row == 1, gain_two_ref[...], 0.0))
    for sample in range(sample_size):
        for leaf in range(leaf_size):
            blocks_ref[sample, leaf, 4 * step :, :] = gains
    part_blocks(blocks_ref, keep_ref, send_ref)


def unpack_kernel(slot_ref, returned_ref, out_ref):
    slots = returned_ref.shape[0]
    slot_col = column_of(slot_ref[...].astype(F32)).astype(jnp.int32)
    place = one_hot(lane_tile(slot_col, slots), (out_ref.shape[0], slots), 1)
    out_ref[...] = mm(place, returned_ref[...]).astype(BF16)


def halve_kernel(axis, bit, keep_ref, got_ref, keep_out_ref, send_out_ref):
    mine = lax.rem(lax.div(lax.axis_index(axis), bit), 2)
    for high in range(keep_out_ref.shape[0]):
        for ref, at in ((keep_out_ref, 2 * high + mine), (send_out_ref, 2 * high + 1 - mine)):
            here = (at, slice(None), slice(0, ref.shape[2])) if len(ref.shape) == 4 else (at,)
            ref[high] = (keep_ref[here] + got_ref[here].astype(F32)).astype(ref.dtype)


def quarter_kernel(skip, keep_mlp_ref, got_mlp_ref, keep_qkv_ref, got_qkv_ref, keep_out_ref, *send_refs):
    mine = lax.rem(lax.div(lax.axis_index("sample"), 2), 2)
    low = lax.rem(lax.axis_index("leaf"), 2)
    places = ((mine, low), (1 - mine, low), (mine, 1 - low), (1 - mine, 1 - low))
    count = keep_mlp_ref.shape[2] - skip
    for ref, (sample, leaf) in zip((keep_out_ref, *send_refs), places):
        for high in range(ref.shape[0]):
            at = (sample, 2 * high + leaf)
            rest = at + (slice(skip, None),)
            ref[high, :count, :] = (keep_mlp_ref[rest] + got_mlp_ref[rest].astype(F32)).astype(ref.dtype)
            ref[high, count:, :] = (keep_qkv_ref[at] + got_qkv_ref[at].astype(F32)).astype(ref.dtype)


def join_kernel(counts, *refs):
    ins, (keep_out_ref, send_out_ref) = list(refs[:-2]), refs[-2:]
    mine = lax.rem(lax.div(lax.axis_index("leaf"), 2), 2)
    start = 0
    for count in counts:
        part, ins = ins[:count], ins[count:]
        rows = pl.ds(start, part[0].shape[1])
        for ref, at in ((keep_out_ref, mine), (send_out_ref, 1 - mine)):
            total = part[0][at]
            for got_ref in part[1:]:
                total = total + got_ref[at].astype(F32)
            ref[rows, :] = total.astype(ref.dtype)
        start += part[0].shape[1]


def finish_kernel(keep_ref, got_ref, low_ref, gains_ref):
    total = keep_ref[...] + got_ref[...].astype(F32)
    gains_ref[...] = total[-GAINS:]
    low_ref[0] = total[:-GAINS].astype(BF16)


def assemble_kernel(scale, offsets, mine_ref, mate_ref, up_ref, down_ref, out_ref, qkv_ref):
    size = 2 * len(offsets)
    width = mine_ref.shape[2]
    up_rows, down_rows, out_rows = up_ref.shape[0], down_ref.shape[0] // size, out_ref.shape[0] // size
    me = lax.axis_index("sample")

    def block(source, count):
        return pl.ds(pl.multiple_of(source * count, count), count)

    for index, offset in enumerate(offsets):
        for mate, ref in enumerate((mine_ref, mate_ref)):
            source = me ^ (offset + mate)
            part = ref[index].astype(F32) * scale
            at = up_rows
            up_ref[:, block(source, width)] = part[:at]
            down_ref[block(source, down_rows), :] = part[at : at + down_rows]
            at += down_rows
            out_ref[block(source, out_rows), :] = part[at : at + out_rows]
            at += out_rows
            for col in range(3):
                qkv_ref[block(source, out_rows), col * width : (col + 1) * width] = part[at : at + out_rows]
                at += out_rows


def permute(value, axis, size, bit):
    return lax.ppermute(value, axis, [(i, i ^ bit) for i in range(size)])


def halve(keep, got, axis, bit, name, micros=0.5, rows=None):
    shape = (keep.shape[0] // 2,) + keep.shape[1:]
    if rows is not None:
        shape = shape[:2] + (rows,) + shape[3:]
    return call(functools.partial(halve_kernel, axis, bit), [(shape, F32), (shape, BF16)], name, micros, keep, got)


def call(kernel, outs, name, micros, *args, scratch=(), hbm_in=False, hbm_out=False, raw_in=0, raw_out=0, blocked=False, limit=16):
    moved = sum(arg.size * arg.dtype.itemsize for arg in args)
    moved += sum(math.prod(shape) * jnp.dtype(dtype).itemsize for shape, dtype in outs)
    vmem = pl.BlockSpec() if blocked else pl.BlockSpec(memory_space=pltpu.VMEM)
    hbm = pl.BlockSpec(memory_space=pltpu.HBM)
    copied_in = len(args) - raw_in if hbm_in else 0
    copied_out = len(outs) - raw_out if hbm_out else 0
    parts = 2

    def body(*refs):
        ins, refs = list(refs[: len(args)]), refs[len(args) :]
        results, refs = list(refs[: len(outs)]), refs[len(outs) :]
        own, refs = refs[: len(scratch)], refs[len(scratch) :]
        in_bufs, refs = refs[:copied_in], refs[copied_in:]
        out_bufs, refs = refs[:copied_out], refs[copied_out:]
        for at, buf in enumerate(in_bufs):
            copy = pltpu.make_async_copy(ins[at], buf, refs[0].at[at])
            copy.start()
            ins[at] = Arriving(buf, [copy])
        for at, buf in enumerate(out_bufs):
            results[at] = Leaving(buf, results[at], refs[-1].at[at])
        kernel(*ins, *results, *own)
        for ref in ins:
            if isinstance(ref, Arriving):
                for copy in ref.copies:
                    copy.wait()
        for ref in results[:copied_out]:
            ref.send()
        for ref in results[:copied_out]:
            for copy in ref.copies:
                copy.wait()

    extra = [pltpu.VMEM(arg.shape, arg.dtype) for arg in args[:copied_in]]
    extra += [pltpu.VMEM(shape, dtype) for shape, dtype in outs[:copied_out]]
    if copied_in:
        extra.append(pltpu.SemaphoreType.DMA((copied_in,)))
    if copied_out:
        extra.append(pltpu.SemaphoreType.DMA((copied_out, parts)))
    return pl.pallas_call(
        body,
        out_shape=[jax.ShapeDtypeStruct(shape, dtype) for shape, dtype in outs],
        in_specs=[hbm if hbm_in else vmem] * (len(args) - raw_in) + [hbm] * raw_in,
        out_specs=[hbm if hbm_out else vmem] * (len(outs) - raw_out) + [hbm] * raw_out,
        scratch_shapes=list(scratch) + extra,
        compiler_params=pltpu.CompilerParams(vmem_limit_bytes=limit * 1024 * 1024),
        cost_estimate=pl.CostEstimate(flops=int(micros * 1.1e9), bytes_accessed=moved, transcendentals=0),
        name=name,
    )(*args)


def exchange(flat, axes, peers):
    moved = lax.all_to_all(
        flat.reshape((peers, -1) + flat.shape[1:]), axes, split_axis=0, concat_axis=0, tiled=True
    )
    return moved.reshape(flat.shape)


def local(points, cotangent, dest_pos, w_qkv, w_out, w_up, w_down, gain_attn, gain_mlp):
    rows, width = points.shape
    hidden_width = w_up.shape[1]
    axes = ("leaf", "sample")
    peers = lax.axis_size(axes)
    leaf_size, sample_size = lax.axis_size("leaf"), lax.axis_size("sample")
    cap = 2 * rows // peers
    slots = peers * cap
    balls = rows // BALL
    direct = cap % 16 == 0
    paired = leaf_size & (leaf_size - 1) == 0 and sample_size & (sample_size - 1) == 0 and min(leaf_size, sample_size) > 1
    arranged = paired and width % (16 * peers) == 0 and hidden_width == sample_size * width and (leaf_size, sample_size) == (4, 4)
    inv_root = 1.0 / math.sqrt(rows * peers)

    msg_rows = 2 * cap + META
    if direct:
        outs = [((peers, msg_rows, 128), BF16)]
    else:
        outs = [((slots, width), BF16), ((peers, 128), F32), ((peers, 128), F32)]
    slot, *message = call(
        functools.partial(pack_points_kernel, peers, cap, direct),
        [((1, rows), jnp.int32)] + outs, "pack_points", 2, dest_pos.reshape(1, rows), points, hbm_in=True, hbm_out=True, limit=60,
    )
    if direct:
        forward_args = [exchange(message[0].reshape(-1, 128), axes, peers).reshape(peers, msg_rows, 128)]
    else:
        packed, high, low = message
        tail = jnp.stack([high, low], axis=1).astype(BF16)
        halves = packed.reshape(peers, cap, 2, 128).transpose(0, 2, 1, 3).reshape(peers, 2 * cap, 128)
        flat = jnp.concatenate([halves, tail], axis=1).reshape(-1, 128)
        arrived = exchange(flat, axes, peers).reshape(peers, 2 * cap + 2, 128)
        halves = arrived[:, : 2 * cap].reshape(peers, 2, cap, 128).transpose(0, 2, 1, 3).reshape(slots, width)
        forward_args = [halves, arrived[:, 2 * cap].astype(F32), arrived[:, 2 * cap + 1].astype(F32)]
    by_permute = direct and paired and peers <= 16
    if by_permute:
        packed_cot = call(
            pack_cot_kernel, [((2, cap, width), BF16)] * (peers // 2), "pack_cot", 1, slot, cotangent,
            scratch=[pltpu.VMEM((peers, cap, width), BF16)],
        )
        pairs = [packed_cot[0]] + [permute(packed_cot[step], axes, peers, 2 * step) for step in range(1, peers // 2)]
        *pairs[1:3], forward_args[0] = lax.optimization_barrier((*pairs[1:3], forward_args[0]))
    else:
        (packed_cot,) = call(pack_cot_kernel, [((slots, width), BF16)], "pack_cot", 1, slot, cotangent)
        arrived_cot = [exchange(packed_cot, axes, peers)]
    target, target_col, rotated = call(
        functools.partial(unpack_points_kernel, cap, peers, direct),
        [((1, slots), jnp.int32), ((slots, 128), jnp.int32), ((width, rows), F32)],
        "unpack_points", 2, *forward_args,
    )
    (
        qkv_t, kv, scales, norm_one, normed_one, attended, norm_two, normed_two, hidden, slope,
        gain_attn_col, gain_mlp_col, *probs,
    ) = call(
        forward_kernel,
        [
            ((3 * width, rows), BF16), ((rows, 2 * width), BF16), ((8, rows), F32),
            ((width, rows), F32), ((width, rows), BF16), ((width, rows), BF16),
            ((width, rows), F32), ((width, rows), BF16),
            ((hidden_width, rows), BF16), ((hidden_width, rows), F32), ((width, 128), F32), ((width, 128), F32),
        ] + [((width // GROUP, BALL, GROUP // HEAD_DIM * BALL), F32)] * balls,
        "forward", 7, rotated, w_qkv, w_out, w_up, gain_attn.reshape(1, width), gain_mlp.reshape(1, width),
    )
    if by_permute:
        scales, *pairs = lax.optimization_barrier((scales, *pairs))
        half = ((peers // 2, cap, width), BF16)
        mine, for_mate = call(regroup_kernel, [half] * 2, "regroup", 0.3, *pairs)
        arrived_cot = [mine, permute(for_mate, axes, peers, 1)]
    mlp_scratch, qkv_scratch = [], []
    if arranged:
        halved = (sample_size // 2, leaf_size)
        mlp_rows = width // leaf_size + hidden_width // peers
        qkv_rows = 4 * width // peers + GAINS
        mlp_mats = [(halved + (mlp_rows, width), F32), (halved + (mlp_rows, width), BF16)]
        qkv_mats = [(halved + (qkv_rows, width), F32), (halved + (qkv_rows, width), BF16)]
        mlp_scratch = [pltpu.VMEM((sample_size, leaf_size, mlp_rows, width), F32)]
        qkv_scratch = [pltpu.VMEM((sample_size, leaf_size, qkv_rows, width), F32)]
    else:
        mlp_mats = [(w_up.shape, BF16), (w_down.shape, BF16)]
        qkv_mats = [(w_qkv.shape, BF16), ((1, width), F32)]
    grad_pre, cot_t, *mlp_grads = call(
        functools.partial(mlp_weights_kernel, arranged, by_permute),
        [((hidden_width, rows), BF16), ((width, rows), F32)] + mlp_mats,
        "mlp_weights", 2.5, target, hidden, slope, normed_two, w_down, *arrived_cot,
        scratch=mlp_scratch + ([pltpu.VMEM((peers, cap, width), BF16)] if by_permute else []),
    )
    gain_two, grad_middle, grad_att, grad_out = call(
        mlp_inputs_kernel,
        [((1, width), F32), ((width, rows), F32), ((width, rows), BF16), ((width, width), F32)],
        "mlp_inputs", 1.5, grad_pre, cot_t, norm_two, scales, attended, w_up, w_out, gain_mlp_col,
    )
    if arranged:
        keep_mlp, send_mlp = mlp_grads
        arrived_mlp = permute(send_mlp, "sample", sample_size, 1)
        up_rows = width // leaf_size
        keep_up, send_up = halve(keep_mlp, arrived_mlp, "sample", 2, "halve_up", rows=up_rows)
        grad_att, send_up = lax.optimization_barrier((grad_att, send_up))
        got_up = permute(send_up, "sample", sample_size, 2)
    back, *qkv_grads = call(
        functools.partial(attention_backward_kernel, arranged),
        [((slots, width), BF16)] + qkv_mats, "attention_backward", 6,
        qkv_t, kv, scales, grad_att, grad_middle, norm_one, normed_one,
        w_qkv, gain_attn_col, target_col, gain_two, grad_out, *probs,
        scratch=qkv_scratch + [pltpu.VMEM((3 * width, rows), BF16)],
    )
    if not arranged:
        returned = exchange(back, axes, peers)
        (grad_points,) = call(unpack_kernel, [((rows, width), BF16)], "unpack", 1, slot, returned, blocked=True)
        up_sum, down_sum, out_sum = reduce_mats([*mlp_grads, grad_out])
        qkv_sum, gain_sum = reduce_mats([qkv_grads[0]], jnp.concatenate([qkv_grads[1], gain_two], axis=0))
        return (
            grad_points, qkv_sum * inv_root, out_sum * inv_root, up_sum * inv_root, down_sum * inv_root,
            gain_sum[0] * inv_root, gain_sum[1] * inv_root,
        )
    keep_qkv, send_qkv = qkv_grads
    got_qkv = permute(send_qkv, "sample", sample_size, 1)
    keep_up, leaving = halve(keep_up[0], got_up[0], "leaf", 1, "leaf_up", 2.0)
    got_qkv, leaving = lax.optimization_barrier((got_qkv, leaving))
    quarter = (leaf_size // 2, mlp_rows - up_rows + qkv_rows, width)
    keep_qkv, send_sample, send_leaf, send_both = call(
        functools.partial(quarter_kernel, up_rows), [(quarter, F32)] + [(quarter, BF16)] * 3, "quarter", 0.5,
        keep_mlp, arrived_mlp, keep_qkv, got_qkv,
    )
    back = lax.optimization_barrier((back, leaving, send_sample))[0]
    returned = exchange(back, axes, peers)
    (grad_points,) = call(unpack_kernel, [((rows, width), BF16)], "unpack", 1, slot, returned, blocked=True)
    joined = (mlp_rows + qkv_rows, width)
    keep, leaving = call(
        functools.partial(join_kernel, (2, 4)), [(joined, F32), (joined, BF16)], "leaf_last", 0.5,
        keep_up, permute(leaving, "leaf", leaf_size, 1), keep_qkv,
        permute(send_sample, "sample", sample_size, 2),
        permute(send_leaf, "leaf", leaf_size, 1),
        permute(send_both, axes, peers, sample_size + 2),
    )
    got = permute(leaving, "leaf", leaf_size, 2)
    low, gains = call(
        finish_kernel, [((1, mlp_rows + qkv_rows - GAINS, width), BF16), ((GAINS, width), F32)], "finish", 3.5, keep, got
    )
    offsets = [0]
    bit = sample_size // 2
    while bit > 1:
        low = jnp.concatenate([low, permute(low, "sample", sample_size, bit)], axis=0)
        offsets += [offset ^ bit for offset in offsets]
        bit //= 2
    mate = permute(low, "sample", sample_size, 1)
    share = width // leaf_size
    gains = lax.dynamic_slice(gains, (0, lax.axis_index("leaf") * share), (2, share)) * inv_root
    gain_one, gain_two = gains[0], gains[1]
    gain_one, gain_two, mate = lax.optimization_barrier((gain_one, gain_two, mate))
    up_sum, down_sum, out_sum, qkv_sum = call(
        functools.partial(assemble_kernel, inv_root, offsets),
        [
            ((share, hidden_width), F32), ((hidden_width // leaf_size, width), F32), ((share, width), F32),
            ((share, 3 * width), F32),
        ],
        "assemble", 1, low, mate, blocked=True,
    )
    return (grad_points, qkv_sum, out_sum, up_sum, down_sum, gain_one, gain_two)


def reduce_mats(mats, gains=None):
    leaf_size = lax.axis_size("leaf")
    sample_size = lax.axis_size("sample")
    me = lax.axis_index("sample")
    pieces = []
    for mat in mats:
        pieces.append(mat.reshape(leaf_size, sample_size, -1, 128).transpose(1, 0, 2, 3))
    if gains is not None:
        gain_block = gains.reshape(2, leaf_size, -1).transpose(1, 0, 2).reshape(1, leaf_size, 1, -1)
        gain_block = jnp.pad(gain_block, ((0, 0), (0, 0), (0, 15), (0, 128 - gain_block.shape[3])))
        pieces.append(jnp.broadcast_to(gain_block, (sample_size,) + gain_block.shape[1:]))
    current = jnp.concatenate(pieces, axis=2).astype(jnp.bfloat16)
    bit = 1
    while bit < sample_size:
        split = current.reshape((current.shape[0] // 2, 2) + current.shape[1:])
        mine = (me // bit) % 2
        keep = lax.dynamic_index_in_dim(split, mine, 1, keepdims=False)
        send = lax.dynamic_index_in_dim(split, 1 - mine, 1, keepdims=False)
        got = lax.ppermute(send, "sample", [(i, i ^ bit) for i in range(sample_size)])
        current = (keep.astype(jnp.float32) + got.astype(jnp.float32)).astype(jnp.bfloat16)
        bit *= 2
    current = lax.all_to_all(current[0], "leaf", split_axis=0, concat_axis=0, tiled=True)
    total = jnp.sum(current.astype(jnp.float32), axis=0)
    low = total.astype(jnp.bfloat16)
    gathered = jnp.zeros((sample_size,) + low.shape, jnp.bfloat16)
    for step in range(sample_size):
        got = low if step == 0 else lax.ppermute(low, "sample", [(i, i ^ step) for i in range(sample_size)])
        gathered = lax.dynamic_update_index_in_dim(gathered, got, me ^ step, 0)
    results = []
    start = 0
    for mat in mats:
        rows = mat.size // (leaf_size * sample_size * 128)
        part = gathered[:, start : start + rows].astype(jnp.float32)
        results.append(part.reshape(mat.shape[0] // leaf_size, mat.shape[1]))
        start += rows
    if gains is not None:
        width = gains.shape[1] // leaf_size
        results.append(total[start, : 2 * width].reshape(2, width))
    return results


def solution(mesh):
    in_specs = (
        P(("groups", "leaf", "sample"), None),
        P(("groups", "leaf", "sample"), None),
        P(("groups", "leaf", "sample")),
        P(),
        P(),
        P(),
        P(),
        P(),
        P(),
    )
    out_specs = (
        P(("groups", "leaf", "sample"), None),
        P(("groups", "leaf"), None),
        P(("groups", "leaf"), None),
        P(("groups", "leaf"), None),
        P(("groups", "leaf"), None),
        P(("groups", "leaf")),
        P(("groups", "leaf")),
    )
    return jax.shard_map(local, mesh=mesh, in_specs=in_specs, out_specs=out_specs, check_vma=False)
```

```python
import functools
import math

import jax
import jax.numpy as jnp
from jax import lax
from jax.experimental import pallas as pl
from jax.experimental.pallas import tpu as pltpu
from jax.sharding import PartitionSpec as P

HEADS = 8
BALL = 256
HEAD_DIM = 32
GROUP = 128
META = 16
GAINS = 8

EPSILON = 1e-06
GELU_COEF = math.sqrt(2.0 / math.pi)
ATT_SCALE = HEAD_DIM ** (-0.5)
BF16 = jnp.bfloat16
F32 = jnp.float32


def mm(a, b):
    return lax.dot_general(a, b, (((1,), (0,)), ((), ())), preferred_element_type=F32)


def mm_nt(a, b):
    return lax.dot_general(a, b, (((1,), (1,)), ((), ())), preferred_element_type=F32)


def mm_tn(a, b):
    return lax.dot_general(a, b, (((0,), (0,)), ((), ())), preferred_element_type=F32)


def iota(shape, dim):
    return lax.broadcasted_iota(jnp.int32, shape, dim)


def one_hot(positions, shape, dim):
    return jnp.where(iota(shape, dim) == positions, 1.0, 0.0).astype(BF16)


def column_of(row):
    return jnp.broadcast_to(row, (128, row.shape[1])).T


def lane_tile(column, width):
    return jnp.concatenate([column] * (width // 128), axis=1)


class Arriving:
    def __init__(self, ref, copies):
        self.ref, self.copies, self.shape = ref, copies, ref.shape

    def __getitem__(self, where):
        for copy in self.copies:
            copy.wait()
        self.copies = []
        return self.ref[where]


class Leaving:
    def __init__(self, ref, out_ref, sems):
        self.ref, self.out_ref, self.sems, self.shape, self.dtype = ref, out_ref, sems, ref.shape, ref.dtype
        self.copies, self.sent = [], 0

    def __getitem__(self, where):
        return self.ref[where]

    def __setitem__(self, where, value):
        self.ref[where] = value

    def send(self, upto=None):
        upto = self.shape[0] if upto is None else upto
        if upto > self.sent:
            part = pl.ds(self.sent, upto - self.sent)
            copy = pltpu.make_async_copy(self.ref.at[part], self.out_ref.at[part], self.sems.at[len(self.copies)])
            copy.start()
            self.copies.append(copy)
            self.sent = upto


def send(ref, upto=None):
    if isinstance(ref, Leaving):
        ref.send(upto)


def pack_points_kernel(peers, cap, direct, dest_ref, points_ref, slot_ref, *out_refs):
    rows = points_ref.shape[0]
    slots = peers * cap
    dest = dest_ref[...]
    shift = rows.bit_length() - 1
    owner = lax.shift_right_logical(dest, shift)
    target = jnp.bitwise_and(dest, rows - 1)
    owned = jnp.where(iota((peers, rows), 0) == owner, 1.0, 0.0)
    upto = jnp.where(iota((rows, rows), 0) <= iota((rows, rows), 1), 1.0, 0.0).astype(BF16)
    counts = mm(owned.astype(BF16), upto)
    rank = (jnp.sum(counts * owned, axis=0, keepdims=True) - 1.0).astype(jnp.int32)
    slot = owner * cap + rank
    slot_ref[...] = slot
    packed = mm(one_hot(slot, (slots, rows), 0), points_ref[...]).astype(BF16)
    within = one_hot(rank, (cap, rows), 0)
    within = jnp.concatenate([within] * (128 // cap), axis=0)
    high = (lax.shift_right_logical(target, 4) + 1).astype(F32)
    low = jnp.bitwise_and(target, 15).astype(F32)
    high_rows = mm_nt((owned * high).astype(BF16), within)
    low_rows = mm_nt((owned * low).astype(BF16), within)
    if direct:
        (msg_ref,) = out_refs
        msg_ref[:, :cap, :] = packed[:, :128].reshape(peers, cap, 128)
        msg_ref[:, cap : 2 * cap, :] = packed[:, 128:].reshape(peers, cap, 128)
        first = iota((META, 128), 0) == 0
        for peer in range(peers):
            block = jnp.where(first, high_rows[peer : peer + 1], low_rows[peer : peer + 1])
            msg_ref[peer, 2 * cap :, :] = block.astype(BF16)
    else:
        packed_ref, high_ref, low_ref = out_refs
        packed_ref[...] = packed
        high_ref[...] = high_rows
        low_ref[...] = low_rows


def partner(step):
    return (lax.axis_index("leaf") * lax.axis_size("sample") + lax.axis_index("sample")) ^ step


def pack_cot_kernel(slot_ref, cot_ref, *refs):
    rows = cot_ref.shape[0]
    if len(refs) == 1:
        (packed_ref,) = refs
        packed_ref[...] = mm(one_hot(slot_ref[...], (packed_ref.shape[0], rows), 0), cot_ref[...]).astype(BF16)
        return
    *block_refs, packed_ref = refs
    peers, cap, width = packed_ref.shape
    packed = mm(one_hot(slot_ref[...], (peers * cap, rows), 0), cot_ref[...]).astype(BF16)
    packed_ref[...] = packed.reshape(peers, cap, width)
    for step, ref in enumerate(block_refs):
        for mate in range(2):
            ref[mate] = packed_ref[partner(2 * step + mate)]


def regroup_kernel(*refs):
    *pair_refs, mine_ref, mate_ref = refs
    for step, ref in enumerate(pair_refs):
        mine_ref[step] = ref[0]
        mate_ref[step] = ref[1]


def group_heads(rows):
    heads = range(GROUP // HEAD_DIM)
    return jnp.concatenate([head_rows(rows[h * HEAD_DIM : (h + 1) * HEAD_DIM], h) for h in heads], axis=1)


def head_rows(rows, head):
    width = rows.shape[1]
    at = (head * HEAD_DIM) % GROUP
    parts = []
    if at:
        parts.append(jnp.zeros((at, width), rows.dtype))
    parts.append(rows)
    if at + HEAD_DIM < GROUP:
        parts.append(jnp.zeros((GROUP - at - HEAD_DIM, width), rows.dtype))
    return jnp.concatenate(parts, axis=0)


def unpack_points_kernel(cap, peers, direct, *refs):
    if not direct:
        recv_ref, high_ref, low_ref = refs[:3]
        recv = recv_ref[...]
        high_rows, low_rows = high_ref[...], low_ref[...]
    else:
        msg_ref = refs[0]
        left = msg_ref[:, :cap, :].reshape(peers * cap, 128)
        right = msg_ref[:, cap : 2 * cap, :].reshape(peers * cap, 128)
        recv = jnp.concatenate([left, right], axis=1)
        tails = [msg_ref[peer, 2 * cap :, :].astype(F32) for peer in range(peers)]
        high_rows = jnp.concatenate([tail[0:1] for tail in tails], axis=0)
        low_rows = jnp.concatenate([tail[1:2] for tail in tails], axis=0)
    target_ref, target_col_ref, rotated_ref = refs[-3:]
    rows = rotated_ref.shape[1]
    slots = peers * cap
    targets = (high_rows - 1.0) * 16.0 + low_rows
    per_row = 128 // cap
    own_lane = iota((per_row, 128), 1) // cap == iota((per_row, 128), 0)
    pieces = []
    for group in range(slots // 128):
        block = targets[group * per_row : (group + 1) * per_row]
        pieces.append(jnp.sum(jnp.where(own_lane, block, 0.0), axis=0, keepdims=True))
    target = jnp.concatenate(pieces, axis=1)
    target_ref[...] = target.astype(jnp.int32)
    target_col_ref[...] = column_of(target).astype(jnp.int32)
    rotated_ref[...] = mm(one_hot(target.astype(jnp.int32), (rows, slots), 0), recv).T


def forward_kernel(
    rotated_ref, w_qkv_ref, w_out_ref, w_up_ref, gain_attn_ref, gain_mlp_ref,
    qkv_t_ref, kv_ref, scales_ref, norm_one_ref, normed_one_ref, attended_ref, norm_two_ref, normed_two_ref,
    hidden_ref, slope_ref, gain_attn_col_ref, gain_mlp_col_ref, *probs_refs,
):
    rot_t = rotated_ref[...]
    width, rows = rot_t.shape
    gain_attn_col = column_of(gain_attn_ref[...])
    gain_attn_col_ref[...] = gain_attn_col
    gain_mlp_col = column_of(gain_mlp_ref[...])
    gain_mlp_col_ref[...] = gain_mlp_col
    scale_one = lax.rsqrt(jnp.mean(rot_t * rot_t, axis=0, keepdims=True) + EPSILON)
    norm_one = rot_t * scale_one
    norm_one_ref[...] = norm_one
    normed_one = (norm_one * lane_tile(gain_attn_col, rows)).astype(BF16)
    normed_one_ref[...] = normed_one
    qkv_t = mm_tn(w_qkv_ref[...], normed_one).astype(BF16)
    qkv_t_ref[...] = qkv_t
    kv_ref[...] = qkv_t[width:].astype(F32).T.astype(BF16)

    for ball in range(rows // BALL):
        at = ball * BALL
        cols = slice(at, at + BALL)
        for group in range(0, width, GROUP):
            queries = group_heads(qkv_t_ref[group : group + GROUP, cols])
            scores = mm(kv_ref[cols, group : group + GROUP], queries) * ATT_SCALE
            top = jnp.max(scores, axis=0, keepdims=True)
            weights = jnp.exp(scores - top)
            probs = weights * (1.0 / jnp.sum(weights, axis=0, keepdims=True))
            probs_refs[ball][group // GROUP] = probs
            probs_low = probs.astype(BF16)
            for head in range(GROUP // HEAD_DIM):
                own = slice(group + head * HEAD_DIM, group + (head + 1) * HEAD_DIM)
                values = qkv_t_ref[2 * width + own.start : 2 * width + own.stop, cols]
                attended_ref[own, cols] = mm(values, probs_low[:, head * BALL : (head + 1) * BALL]).astype(BF16)

    middle = rot_t + mm_tn(w_out_ref[...], attended_ref[...])
    scale_two = lax.rsqrt(jnp.mean(middle * middle, axis=0, keepdims=True) + EPSILON)
    norm_two = middle * scale_two
    norm_two_ref[...] = norm_two
    normed_two = (norm_two * lane_tile(gain_mlp_col, rows)).astype(BF16)
    normed_two_ref[...] = normed_two
    scales_ref[...] = jnp.where(iota(scales_ref.shape, 0) == 0, scale_one, scale_two)
    step = 256
    for at in range(0, hidden_ref.shape[0], step):
        pre_act = mm_tn(w_up_ref[:, at : at + step], normed_two)
        square = pre_act * pre_act
        tanh_val = jnp.tanh(GELU_COEF * (pre_act + 0.044715 * pre_act * square))
        half = 0.5 * (1.0 + tanh_val)
        hidden_ref[at : at + step, :] = (pre_act * half).astype(BF16)
        slope_ref[at : at + step, :] = half + 0.5 * pre_act * (1.0 - tanh_val * tanh_val) * (
            GELU_COEF * (1.0 + 3.0 * 0.044715 * square)
        )


def norm_backward(grad_normed, norm, scale, gain):
    inner = grad_normed * gain
    return scale * (inner - norm * jnp.mean(inner * norm, axis=0, keepdims=True))


def gain_row(product):
    width = product.shape[1]
    partial = product[:, :128]
    for at in range(128, width, 128):
        partial = partial + product[:, at : at + 128]
    return jnp.sum(partial.T, axis=0, keepdims=True)


def place_blocks(blocks_ref, values, first_row, leaf_size, sample_size):
    step = values.shape[0] // (leaf_size * sample_size)
    for block in range(leaf_size * sample_size):
        leaf, sample = divmod(block, sample_size)
        blocks_ref[sample, leaf, first_row : first_row + step, :] = values[block * step : (block + 1) * step]


def part_blocks(blocks_ref, keep_ref, send_ref):
    low = lax.rem(lax.axis_index("sample"), 2)
    for high in range(keep_ref.shape[0]):
        keep_ref[high] = blocks_ref[2 * high + low]
        send_ref[high] = blocks_ref[2 * high + 1 - low].astype(BF16)


def mlp_weights_kernel(
    arranged, direct, target_ref, hidden_ref, slope_ref, normed_two_ref, w_down_ref, *refs
):
    width, rows = normed_two_ref.shape
    if direct:
        mine_ref, mate_ref, *refs, landing_ref = refs
        for step in range(mine_ref.shape[0]):
            landing_ref[partner(2 * step)] = mine_ref[step]
            landing_ref[partner(2 * step + 1)] = mate_ref[step]
        recv_ref = landing_ref
    else:
        recv_ref, *refs = refs
    grad_pre_ref, cot_t_ref, *mat_refs = refs
    recv = recv_ref[...].reshape(-1, width)
    cot_f = mm(one_hot(target_ref[...], (rows, recv.shape[0]), 0), recv)
    cot = cot_f.astype(BF16)
    cot_t = cot_f.T
    cot_t_ref[...] = cot_t
    cot_t_low = cot_t.astype(BF16)
    normed_two = normed_two_ref[...]
    step = 256
    if arranged:
        keep_ref, send_ref, blocks_ref = mat_refs
        leaf_size, sample_size = lax.axis_size("leaf"), lax.axis_size("sample")
        up_rows = width // leaf_size
        down_rows = hidden_ref.shape[0] // (leaf_size * sample_size)
    else:
        grad_up_ref, grad_down_ref = mat_refs
    for at in range(0, hidden_ref.shape[0], step):
        grad_down = mm(hidden_ref[at : at + step, :], cot)
        grad_pre = (mm(w_down_ref[at : at + step, :], cot_t_low) * slope_ref[at : at + step, :]).astype(BF16)
        grad_pre_ref[at : at + step, :] = grad_pre
        grad_up = mm_nt(normed_two, grad_pre)
        if arranged:
            for leaf in range(leaf_size):
                blocks_ref[at // step, leaf, :up_rows, :] = grad_up[leaf * up_rows : (leaf + 1) * up_rows]
            for block in range(step // down_rows):
                leaf, sample = divmod(at // down_rows + block, sample_size)
                piece = grad_down[block * down_rows : (block + 1) * down_rows]
                blocks_ref[sample, leaf, up_rows:, :] = piece
        else:
            grad_down_ref[at : at + step, :] = grad_down.astype(BF16)
            grad_up_ref[:, at : at + step] = grad_up.astype(BF16)
    if arranged:
        part_blocks(blocks_ref, keep_ref, send_ref)


def mlp_inputs_kernel(
    grad_pre_ref, cot_t_ref, norm_two_ref, scales_ref, attended_ref, w_up_ref, w_out_ref, gain_mlp_ref,
    grad_gain_ref, grad_middle_ref, grad_att_ref, grad_out_ref,
):
    grad_normed = mm(w_up_ref[...], grad_pre_ref[...])
    norm_two = norm_two_ref[...]
    grad_gain_ref[...] = gain_row(grad_normed * norm_two)
    gain = lane_tile(gain_mlp_ref[...], norm_two.shape[1])
    grad_middle = cot_t_ref[...] + norm_backward(grad_normed, norm_two, scales_ref[1:2, :], gain)
    grad_middle_ref[...] = grad_middle
    grad_middle_low = grad_middle.astype(BF16)
    grad_att_ref[...] = mm(w_out_ref[...], grad_middle_low).astype(BF16)
    grad_out_ref[...] = mm_nt(attended_ref[...], grad_middle_low)


def ball_backward(ball, qkv_t_ref, kv_ref, probs_ref, grad_att_ref, grad_rows_ref):
    width = qkv_t_ref.shape[0] // 3
    cols = slice(ball * BALL, (ball + 1) * BALL)
    for group in range(0, width, GROUP):
        upstream = grad_att_ref[group : group + GROUP, cols]
        probs = probs_ref[group // GROUP]
        grad_probs = mm(kv_ref[cols, width + group : width + group + GROUP], group_heads(upstream))
        delta = jnp.sum(grad_probs * probs, axis=0, keepdims=True)
        grad_scores = (probs * (grad_probs - delta)).astype(BF16)
        probs_low = probs.astype(BF16)
        for head in range(GROUP // HEAD_DIM):
            first = group + head * HEAD_DIM
            own, own_key, own_value = (slice(at + first, at + first + HEAD_DIM) for at in (0, width, 2 * width))
            part = slice(head * BALL, (head + 1) * BALL)
            scores_of = grad_scores[:, part]
            grad_rows_ref[own, cols] = (mm(qkv_t_ref[own_key, cols], scores_of) * ATT_SCALE).astype(BF16)
            grad_rows_ref[own_key, cols] = (mm_nt(qkv_t_ref[own, cols], scores_of) * ATT_SCALE).astype(BF16)
            grad_rows_ref[own_value, cols] = mm_nt(grad_att_ref[own, cols], probs_low[:, part]).astype(BF16)


def attention_backward_kernel(
    arranged,
    qkv_t_ref, kv_ref, scales_ref, grad_att_ref, grad_middle_ref, norm_one_ref, normed_one_ref,
    w_qkv_ref, gain_attn_ref, target_col_ref, gain_two_ref, grad_out_ref, *refs,
):
    width, rows = norm_one_ref.shape
    probs_refs, refs = refs[: rows // BALL], refs[rows // BALL :]
    back_ref, *mat_refs, grad_rows_ref = refs
    for ball, probs_ref in enumerate(probs_refs):
        ball_backward(ball, qkv_t_ref, kv_ref, probs_ref, grad_att_ref, grad_rows_ref)
    grad_rows = grad_rows_ref[...]
    grad_normed = mm(w_qkv_ref[...], grad_rows)
    norm_one = norm_one_ref[...]
    gain_one = gain_row(grad_normed * norm_one)
    gain = lane_tile(gain_attn_ref[...], rows)
    grad_rot = grad_middle_ref[...] + norm_backward(grad_normed, norm_one, scales_ref[0:1, :], gain)
    place = one_hot(lane_tile(target_col_ref[...], rows), (back_ref.shape[0], rows), 1)
    back_ref[...] = mm_nt(place, grad_rot.astype(BF16)).astype(BF16)
    normed_one = normed_one_ref[...]
    if not arranged:
        mat_refs[0][...] = mm_nt(normed_one, grad_rows).astype(BF16)
        mat_refs[1][...] = gain_one
        return
    keep_ref, send_ref, blocks_ref = mat_refs
    leaf_size, sample_size = lax.axis_size("leaf"), lax.axis_size("sample")
    step = width // (leaf_size * sample_size)
    for col in range(3):
        grad_qkv = mm_nt(normed_one, grad_rows[col * width : (col + 1) * width])
        place_blocks(blocks_ref, grad_qkv, (1 + col) * step, leaf_size, sample_size)
    place_blocks(blocks_ref, grad_out_ref[...], 0, leaf_size, sample_size)
    row = iota((GAINS, width), 0)
    gains = jnp.where(row == 0, gain_one, jnp.where(row == 1, gain_two_ref[...], 0.0))
    for sample in range(sample_size):
        for leaf in range(leaf_size):
            blocks_ref[sample, leaf, 4 * step :, :] = gains
    part_blocks(blocks_ref, keep_ref, send_ref)


def unpack_kernel(slot_ref, returned_ref, out_ref):
    slots = returned_ref.shape[0]
    slot_col = column_of(slot_ref[...].astype(F32)).astype(jnp.int32)
    place = one_hot(lane_tile(slot_col, slots), (out_ref.shape[0], slots), 1)
    out_ref[...] = mm(place, returned_ref[...]).astype(BF16)


def halve_kernel(axis, bit, keep_ref, got_ref, keep_out_ref, send_out_ref):
    mine = lax.rem(lax.div(lax.axis_index(axis), bit), 2)
    for high in range(keep_out_ref.shape[0]):
        for ref, at in ((keep_out_ref, 2 * high + mine), (send_out_ref, 2 * high + 1 - mine)):
            ref[high] = (keep_ref[at] + got_ref[at].astype(F32)).astype(ref.dtype)


def quarter_kernel(keep_ref, got_ref, keep_out_ref, *send_refs):
    mine = lax.rem(lax.div(lax.axis_index("sample"), 2), 2)
    low = lax.rem(lax.axis_index("leaf"), 2)
    places = ((mine, low), (1 - mine, low), (mine, 1 - low), (1 - mine, 1 - low))
    for ref, (sample, leaf) in zip((keep_out_ref, *send_refs), places):
        for high in range(ref.shape[0]):
            total = keep_ref[sample, 2 * high + leaf] + got_ref[sample, 2 * high + leaf].astype(F32)
            ref[high] = total.astype(ref.dtype)


def join_kernel(counts, *refs):
    ins, (keep_out_ref, send_out_ref) = list(refs[:-2]), refs[-2:]
    mine = lax.rem(lax.div(lax.axis_index("leaf"), 2), 2)
    start = 0
    for count in counts:
        part, ins = ins[:count], ins[count:]
        rows = pl.ds(start, part[0].shape[1])
        for ref, at in ((keep_out_ref, mine), (send_out_ref, 1 - mine)):
            total = part[0][at]
            for got_ref in part[1:]:
                total = total + got_ref[at].astype(F32)
            ref[rows, :] = total.astype(ref.dtype)
        start += part[0].shape[1]


def finish_kernel(keep_ref, got_ref, low_ref, gains_ref):
    total = keep_ref[...] + got_ref[...].astype(F32)
    gains_ref[...] = total[-GAINS:]
    low_ref[0] = total[:-GAINS].astype(BF16)


def assemble_kernel(scale, offsets, mine_ref, mate_ref, up_ref, down_ref, out_ref, qkv_ref):
    size = 2 * len(offsets)
    width = mine_ref.shape[2]
    up_rows, down_rows, out_rows = up_ref.shape[0], down_ref.shape[0] // size, out_ref.shape[0] // size
    me = lax.axis_index("sample")

    def block(source, count):
        return pl.ds(pl.multiple_of(source * count, count), count)

    for index, offset in enumerate(offsets):
        for mate, ref in enumerate((mine_ref, mate_ref)):
            source = me ^ (offset + mate)
            part = ref[index].astype(F32) * scale
            at = up_rows
            up_ref[:, block(source, width)] = part[:at]
            down_ref[block(source, down_rows), :] = part[at : at + down_rows]
            at += down_rows
            out_ref[block(source, out_rows), :] = part[at : at + out_rows]
            at += out_rows
            for col in range(3):
                qkv_ref[block(source, out_rows), col * width : (col + 1) * width] = part[at : at + out_rows]
                at += out_rows


def permute(value, axis, size, bit):
    return lax.ppermute(value, axis, [(i, i ^ bit) for i in range(size)])


def halve(keep, got, axis, bit, name, micros=0.5):
    shape = (keep.shape[0] // 2,) + keep.shape[1:]
    return call(functools.partial(halve_kernel, axis, bit), [(shape, F32), (shape, BF16)], name, micros, keep, got)


def call(kernel, outs, name, micros, *args, scratch=(), hbm_in=False, hbm_out=False, raw_in=0, raw_out=0, blocked=False, limit=16):
    moved = sum(arg.size * arg.dtype.itemsize for arg in args)
    moved += sum(math.prod(shape) * jnp.dtype(dtype).itemsize for shape, dtype in outs)
    vmem = pl.BlockSpec() if blocked else pl.BlockSpec(memory_space=pltpu.VMEM)
    hbm = pl.BlockSpec(memory_space=pltpu.HBM)
    copied_in = len(args) - raw_in if hbm_in else 0
    copied_out = len(outs) - raw_out if hbm_out else 0
    parts = 2

    def body(*refs):
        ins, refs = list(refs[: len(args)]), refs[len(args) :]
        results, refs = list(refs[: len(outs)]), refs[len(outs) :]
        own, refs = refs[: len(scratch)], refs[len(scratch) :]
        in_bufs, refs = refs[:copied_in], refs[copied_in:]
        out_bufs, refs = refs[:copied_out], refs[copied_out:]
        for at, buf in enumerate(in_bufs):
            copy = pltpu.make_async_copy(ins[at], buf, refs[0].at[at])
            copy.start()
            ins[at] = Arriving(buf, [copy])
        for at, buf in enumerate(out_bufs):
            results[at] = Leaving(buf, results[at], refs[-1].at[at])
        kernel(*ins, *results, *own)
        for ref in ins:
            if isinstance(ref, Arriving):
                for copy in ref.copies:
                    copy.wait()
        for ref in results[:copied_out]:
            ref.send()
        for ref in results[:copied_out]:
            for copy in ref.copies:
                copy.wait()

    extra = [pltpu.VMEM(arg.shape, arg.dtype) for arg in args[:copied_in]]
    extra += [pltpu.VMEM(shape, dtype) for shape, dtype in outs[:copied_out]]
    if copied_in:
        extra.append(pltpu.SemaphoreType.DMA((copied_in,)))
    if copied_out:
        extra.append(pltpu.SemaphoreType.DMA((copied_out, parts)))
    return pl.pallas_call(
        body,
        out_shape=[jax.ShapeDtypeStruct(shape, dtype) for shape, dtype in outs],
        in_specs=[hbm if hbm_in else vmem] * (len(args) - raw_in) + [hbm] * raw_in,
        out_specs=[hbm if hbm_out else vmem] * (len(outs) - raw_out) + [hbm] * raw_out,
        scratch_shapes=list(scratch) + extra,
        compiler_params=pltpu.CompilerParams(vmem_limit_bytes=limit * 1024 * 1024),
        cost_estimate=pl.CostEstimate(flops=int(micros * 1.1e9), bytes_accessed=moved, transcendentals=0),
        name=name,
    )(*args)


def exchange(flat, axes, peers):
    moved = lax.all_to_all(
        flat.reshape((peers, -1) + flat.shape[1:]), axes, split_axis=0, concat_axis=0, tiled=True
    )
    return moved.reshape(flat.shape)


def local(points, cotangent, dest_pos, w_qkv, w_out, w_up, w_down, gain_attn, gain_mlp):
    rows, width = points.shape
    hidden_width = w_up.shape[1]
    axes = ("leaf", "sample")
    peers = lax.axis_size(axes)
    leaf_size, sample_size = lax.axis_size("leaf"), lax.axis_size("sample")
    cap = 2 * rows // peers
    slots = peers * cap
    balls = rows // BALL
    direct = cap % 16 == 0
    paired = leaf_size & (leaf_size - 1) == 0 and sample_size & (sample_size - 1) == 0 and min(leaf_size, sample_size) > 1
    arranged = paired and width % (16 * peers) == 0 and hidden_width == sample_size * width and (leaf_size, sample_size) == (4, 4)
    inv_root = 1.0 / math.sqrt(rows * peers)

    msg_rows = 2 * cap + META
    if direct:
        outs = [((peers, msg_rows, 128), BF16)]
    else:
        outs = [((slots, width), BF16), ((peers, 128), F32), ((peers, 128), F32)]
    slot, *message = call(
        functools.partial(pack_points_kernel, peers, cap, direct),
        [((1, rows), jnp.int32)] + outs, "pack_points", 2, dest_pos.reshape(1, rows), points, hbm_in=True, hbm_out=True, limit=60,
    )
    if direct:
        forward_args = [exchange(message[0].reshape(-1, 128), axes, peers).reshape(peers, msg_rows, 128)]
    else:
        packed, high, low = message
        tail = jnp.stack([high, low], axis=1).astype(BF16)
        halves = packed.reshape(peers, cap, 2, 128).transpose(0, 2, 1, 3).reshape(peers, 2 * cap, 128)
        flat = jnp.concatenate([halves, tail], axis=1).reshape(-1, 128)
        arrived = exchange(flat, axes, peers).reshape(peers, 2 * cap + 2, 128)
        halves = arrived[:, : 2 * cap].reshape(peers, 2, cap, 128).transpose(0, 2, 1, 3).reshape(slots, width)
        forward_args = [halves, arrived[:, 2 * cap].astype(F32), arrived[:, 2 * cap + 1].astype(F32)]
    by_permute = direct and paired and peers <= 16
    if by_permute:
        packed_cot = call(
            pack_cot_kernel, [((2, cap, width), BF16)] * (peers // 2), "pack_cot", 1, slot, cotangent,
            scratch=[pltpu.VMEM((peers, cap, width), BF16)],
        )
        far = [permute(packed_cot[step], axes, peers, 2 * step) for step in range(3, peers // 2)]
    else:
        (packed_cot,) = call(pack_cot_kernel, [((slots, width), BF16)], "pack_cot", 1, slot, cotangent)
        arrived_cot = [exchange(packed_cot, axes, peers)]
    target, target_col, rotated = call(
        functools.partial(unpack_points_kernel, cap, peers, direct),
        [((1, slots), jnp.int32), ((slots, 128), jnp.int32), ((width, rows), F32)],
        "unpack_points", 2, *forward_args,
    )
    (
        qkv_t, kv, scales, norm_one, normed_one, attended, norm_two, normed_two, hidden, slope,
        gain_attn_col, gain_mlp_col, *probs,
    ) = call(
        forward_kernel,
        [
            ((3 * width, rows), BF16), ((rows, 2 * width), BF16), ((8, rows), F32),
            ((width, rows), F32), ((width, rows), BF16), ((width, rows), BF16),
            ((width, rows), F32), ((width, rows), BF16),
            ((hidden_width, rows), BF16), ((hidden_width, rows), F32), ((width, 128), F32), ((width, 128), F32),
        ] + [((width // GROUP, BALL, GROUP // HEAD_DIM * BALL), F32)] * balls,
        "forward", 7, rotated, w_qkv, w_out, w_up, gain_attn.reshape(1, width), gain_mlp.reshape(1, width),
    )
    if by_permute:
        near = lax.optimization_barrier((scales, *packed_cot[1:3]))[1:]
        scales, *far = lax.optimization_barrier((scales, *far))
        near = [permute(block, axes, peers, 2 * step) for step, block in enumerate(near, 1)]
        pairs = [packed_cot[0], *near, *far]
        half = ((peers // 2, cap, width), BF16)
        mine, for_mate = call(regroup_kernel, [half] * 2, "regroup", 0.3, *pairs)
        arrived_cot = [mine, permute(for_mate, axes, peers, 1)]
    mlp_scratch, qkv_scratch = [], []
    if arranged:
        halved = (sample_size // 2, leaf_size)
        mlp_rows = width // leaf_size + hidden_width // peers
        qkv_rows = 4 * width // peers + GAINS
        mlp_mats = [(halved + (mlp_rows, width), F32), (halved + (mlp_rows, width), BF16)]
        qkv_mats = [(halved + (qkv_rows, width), F32), (halved + (qkv_rows, width), BF16)]
        mlp_scratch = [pltpu.VMEM((sample_size, leaf_size, mlp_rows, width), F32)]
        qkv_scratch = [pltpu.VMEM((sample_size, leaf_size, qkv_rows, width), F32)]
    else:
        mlp_mats = [(w_up.shape, BF16), (w_down.shape, BF16)]
        qkv_mats = [(w_qkv.shape, BF16), ((1, width), F32)]
    grad_pre, cot_t, *mlp_grads = call(
        functools.partial(mlp_weights_kernel, arranged, by_permute),
        [((hidden_width, rows), BF16), ((width, rows), F32)] + mlp_mats,
        "mlp_weights", 2.5, target, hidden, slope, normed_two, w_down, *arrived_cot,
        scratch=mlp_scratch + ([pltpu.VMEM((peers, cap, width), BF16)] if by_permute else []),
    )
    gain_two, grad_middle, grad_att, grad_out = call(
        mlp_inputs_kernel,
        [((1, width), F32), ((width, rows), F32), ((width, rows), BF16), ((width, width), F32)],
        "mlp_inputs", 1.5, grad_pre, cot_t, norm_two, scales, attended, w_up, w_out, gain_mlp_col,
    )
    if arranged:
        keep_mlp, send_mlp = mlp_grads
        got_mlp = permute(send_mlp, "sample", sample_size, 1)
        bit = 2
        while bit < sample_size:
            keep_mlp, send_mlp = halve(keep_mlp, got_mlp, "sample", bit, "halve_mlp")
            grad_att, send_mlp = lax.optimization_barrier((grad_att, send_mlp))
            got_mlp = permute(send_mlp, "sample", sample_size, bit)
            bit *= 2
    back, *qkv_grads = call(
        functools.partial(attention_backward_kernel, arranged),
        [((slots, width), BF16)] + qkv_mats, "attention_backward", 6,
        qkv_t, kv, scales, grad_att, grad_middle, norm_one, normed_one,
        w_qkv, gain_attn_col, target_col, gain_two, grad_out, *probs,
        scratch=qkv_scratch + [pltpu.VMEM((3 * width, rows), BF16)],
    )
    if not arranged:
        returned = exchange(back, axes, peers)
        (grad_points,) = call(unpack_kernel, [((rows, width), BF16)], "unpack", 1, slot, returned, blocked=True)
        up_sum, down_sum, out_sum = reduce_mats([*mlp_grads, grad_out])
        qkv_sum, gain_sum = reduce_mats([qkv_grads[0]], jnp.concatenate([qkv_grads[1], gain_two], axis=0))
        return (
            grad_points, qkv_sum * inv_root, out_sum * inv_root, up_sum * inv_root, down_sum * inv_root,
            gain_sum[0] * inv_root, gain_sum[1] * inv_root,
        )
    keep_qkv, send_qkv = qkv_grads
    got_qkv = permute(send_qkv, "sample", sample_size, 1)
    keep_mlp, leaving = halve(keep_mlp[0], got_mlp[0], "leaf", 1, "leaf_mlp", 1.0)
    got_qkv, leaving = lax.optimization_barrier((got_qkv, leaving))
    quarter = (leaf_size // 2, qkv_rows, width)
    keep_qkv, send_sample, send_leaf, send_both = call(
        quarter_kernel, [(quarter, F32)] + [(quarter, BF16)] * 3, "quarter_qkv", 0.5, keep_qkv, got_qkv
    )
    back = lax.optimization_barrier((back, leaving, send_sample))[0]
    returned = exchange(back, axes, peers)
    (grad_points,) = call(unpack_kernel, [((rows, width), BF16)], "unpack", 1, slot, returned, blocked=True)
    joined = (mlp_rows + qkv_rows, width)
    keep, leaving = call(
        functools.partial(join_kernel, (2, 4)), [(joined, F32), (joined, BF16)], "leaf_last", 0.5,
        keep_mlp, permute(leaving, "leaf", leaf_size, 1), keep_qkv,
        permute(send_sample, "sample", sample_size, 2),
        permute(send_leaf, "leaf", leaf_size, 1),
        permute(send_both, axes, peers, sample_size + 2),
    )
    got = permute(leaving, "leaf", leaf_size, 2)
    low, gains = call(
        finish_kernel, [((1, mlp_rows + qkv_rows - GAINS, width), BF16), ((GAINS, width), F32)], "finish", 3.5, keep, got
    )
    offsets = [0]
    bit = sample_size // 2
    while bit > 1:
        low = jnp.concatenate([low, permute(low, "sample", sample_size, bit)], axis=0)
        offsets += [offset ^ bit for offset in offsets]
        bit //= 2
    mate = permute(low, "sample", sample_size, 1)
    share = width // leaf_size
    gains = lax.dynamic_slice(gains, (0, lax.axis_index("leaf") * share), (2, share)) * inv_root
    gain_one, gain_two = gains[0], gains[1]
    gain_one, gain_two, mate = lax.optimization_barrier((gain_one, gain_two, mate))
    up_sum, down_sum, out_sum, qkv_sum = call(
        functools.partial(assemble_kernel, inv_root, offsets),
        [
            ((share, hidden_width), F32), ((hidden_width // leaf_size, width), F32), ((share, width), F32),
            ((share, 3 * width), F32),
        ],
        "assemble", 1, low, mate, blocked=True,
    )
    return (grad_points, qkv_sum, out_sum, up_sum, down_sum, gain_one, gain_two)


def reduce_mats(mats, gains=None):
    leaf_size = lax.axis_size("leaf")
    sample_size = lax.axis_size("sample")
    me = lax.axis_index("sample")
    pieces = []
    for mat in mats:
        pieces.append(mat.reshape(leaf_size, sample_size, -1, 128).transpose(1, 0, 2, 3))
    if gains is not None:
        gain_block = gains.reshape(2, leaf_size, -1).transpose(1, 0, 2).reshape(1, leaf_size, 1, -1)
        gain_block = jnp.pad(gain_block, ((0, 0), (0, 0), (0, 15), (0, 128 - gain_block.shape[3])))
        pieces.append(jnp.broadcast_to(gain_block, (sample_size,) + gain_block.shape[1:]))
    current = jnp.concatenate(pieces, axis=2).astype(jnp.bfloat16)
    bit = 1
    while bit < sample_size:
        split = current.reshape((current.shape[0] // 2, 2) + current.shape[1:])
        mine = (me // bit) % 2
        keep = lax.dynamic_index_in_dim(split, mine, 1, keepdims=False)
        send = lax.dynamic_index_in_dim(split, 1 - mine, 1, keepdims=False)
        got = lax.ppermute(send, "sample", [(i, i ^ bit) for i in range(sample_size)])
        current = (keep.astype(jnp.float32) + got.astype(jnp.float32)).astype(jnp.bfloat16)
        bit *= 2
    current = lax.all_to_all(current[0], "leaf", split_axis=0, concat_axis=0, tiled=True)
    total = jnp.sum(current.astype(jnp.float32), axis=0)
    low = total.astype(jnp.bfloat16)
    gathered = jnp.zeros((sample_size,) + low.shape, jnp.bfloat16)
    for step in range(sample_size):
        got = low if step == 0 else lax.ppermute(low, "sample", [(i, i ^ step) for i in range(sample_size)])
        gathered = lax.dynamic_update_index_in_dim(gathered, got, me ^ step, 0)
    results = []
    start = 0
    for mat in mats:
        rows = mat.size // (leaf_size * sample_size * 128)
        part = gathered[:, start : start + rows].astype(jnp.float32)
        results.append(part.reshape(mat.shape[0] // leaf_size, mat.shape[1]))
        start += rows
    if gains is not None:
        width = gains.shape[1] // leaf_size
        results.append(total[start, : 2 * width].reshape(2, width))
    return results


def solution(mesh):
    in_specs = (
        P(("groups", "leaf", "sample"), None),
        P(("groups", "leaf", "sample"), None),
        P(("groups", "leaf", "sample")),
        P(),
        P(),
        P(),
        P(),
        P(),
        P(),
    )
    out_specs = (
        P(("groups", "leaf", "sample"), None),
        P(("groups", "leaf"), None),
        P(("groups", "leaf"), None),
        P(("groups", "leaf"), None),
        P(("groups", "leaf"), None),
        P(("groups", "leaf")),
        P(("groups", "leaf")),
    )
    return jax.shard_map(local, mesh=mesh, in_specs=in_specs, out_specs=out_specs, check_vma=False)
```

```python
import functools
import math

import jax
import jax.numpy as jnp
from jax import lax
from jax.experimental import pallas as pl
from jax.experimental.pallas import tpu as pltpu
from jax.sharding import PartitionSpec as P

HEADS = 8
BALL = 256
HEAD_DIM = 32
GROUP = 128
META = 16
GAINS = 8

EPSILON = 1e-06
GELU_COEF = math.sqrt(2.0 / math.pi)
ATT_SCALE = HEAD_DIM ** (-0.5)
BF16 = jnp.bfloat16
F32 = jnp.float32


def mm(a, b):
    return lax.dot_general(a, b, (((1,), (0,)), ((), ())), preferred_element_type=F32)


def mm_nt(a, b):
    return lax.dot_general(a, b, (((1,), (1,)), ((), ())), preferred_element_type=F32)


def mm_tn(a, b):
    return lax.dot_general(a, b, (((0,), (0,)), ((), ())), preferred_element_type=F32)


def iota(shape, dim):
    return lax.broadcasted_iota(jnp.int32, shape, dim)


def one_hot(positions, shape, dim):
    return jnp.where(iota(shape, dim) == positions, 1.0, 0.0).astype(BF16)


def column_of(row):
    return jnp.broadcast_to(row, (128, row.shape[1])).T


def lane_tile(column, width):
    return jnp.concatenate([column] * (width // 128), axis=1)


class Arriving:
    def __init__(self, ref, copies):
        self.ref, self.copies, self.shape = ref, copies, ref.shape

    def __getitem__(self, where):
        for copy in self.copies:
            copy.wait()
        self.copies = []
        return self.ref[where]


class Leaving:
    def __init__(self, ref, out_ref, sems):
        self.ref, self.out_ref, self.sems, self.shape, self.dtype = ref, out_ref, sems, ref.shape, ref.dtype
        self.copies, self.sent = [], 0

    def __getitem__(self, where):
        return self.ref[where]

    def __setitem__(self, where, value):
        self.ref[where] = value

    def send(self, upto=None):
        upto = self.shape[0] if upto is None else upto
        if upto > self.sent:
            part = pl.ds(self.sent, upto - self.sent)
            copy = pltpu.make_async_copy(self.ref.at[part], self.out_ref.at[part], self.sems.at[len(self.copies)])
            copy.start()
            self.copies.append(copy)
            self.sent = upto


def send(ref, upto=None):
    if isinstance(ref, Leaving):
        ref.send(upto)


def pack_points_kernel(peers, cap, direct, dest_ref, points_ref, slot_ref, *out_refs):
    rows = points_ref.shape[0]
    slots = peers * cap
    dest = dest_ref[...]
    shift = rows.bit_length() - 1
    owner = lax.shift_right_logical(dest, shift)
    target = jnp.bitwise_and(dest, rows - 1)
    owned = jnp.where(iota((peers, rows), 0) == owner, 1.0, 0.0)
    upto = jnp.where(iota((rows, rows), 0) <= iota((rows, rows), 1), 1.0, 0.0).astype(BF16)
    counts = mm(owned.astype(BF16), upto)
    rank = (jnp.sum(counts * owned, axis=0, keepdims=True) - 1.0).astype(jnp.int32)
    slot = owner * cap + rank
    slot_ref[...] = slot
    within = one_hot(rank, (cap, rows), 0)
    within = jnp.concatenate([within] * (128 // cap), axis=0)
    high = (lax.shift_right_logical(target, 4) + 1).astype(F32)
    low = jnp.bitwise_and(target, 15).astype(F32)
    high_rows = mm_nt((owned * high).astype(BF16), within)
    low_rows = mm_nt((owned * low).astype(BF16), within)
    if direct:
        (msg_ref,) = out_refs
        first = iota((META, 128), 0) == 0
        half = peers // 2
        for start in (0, half):
            packed = mm(one_hot(slot - start * cap, (half * cap, rows), 0), points_ref[...]).astype(BF16)
            msg_ref[start : start + half, :cap, :] = packed[:, :128].reshape(half, cap, 128)
            msg_ref[start : start + half, cap : 2 * cap, :] = packed[:, 128:].reshape(half, cap, 128)
            for peer in range(start, start + half):
                block = jnp.where(first, high_rows[peer : peer + 1], low_rows[peer : peer + 1])
                msg_ref[peer, 2 * cap :, :] = block.astype(BF16)
            send(msg_ref, start + half)
    else:
        packed_ref, high_ref, low_ref = out_refs
        packed_ref[...] = mm(one_hot(slot, (slots, rows), 0), points_ref[...]).astype(BF16)
        high_ref[...] = high_rows
        low_ref[...] = low_rows


def partner(step):
    return (lax.axis_index("leaf") * lax.axis_size("sample") + lax.axis_index("sample")) ^ step


def pack_cot_kernel(slot_ref, cot_ref, *refs):
    rows = cot_ref.shape[0]
    if len(refs) == 1:
        (packed_ref,) = refs
        packed_ref[...] = mm(one_hot(slot_ref[...], (packed_ref.shape[0], rows), 0), cot_ref[...]).astype(BF16)
        return
    *block_refs, packed_ref = refs
    peers, cap, width = packed_ref.shape
    packed = mm(one_hot(slot_ref[...], (peers * cap, rows), 0), cot_ref[...]).astype(BF16)
    packed_ref[...] = packed.reshape(peers, cap, width)
    for step, ref in enumerate(block_refs):
        for mate in range(2):
            ref[mate] = packed_ref[partner(2 * step + mate)]


def regroup_kernel(*refs):
    *pair_refs, mine_ref, mate_ref = refs
    for step, ref in enumerate(pair_refs):
        mine_ref[step] = ref[0]
        mate_ref[step] = ref[1]


def group_heads(rows):
    heads = range(GROUP // HEAD_DIM)
    return jnp.concatenate([head_rows(rows[h * HEAD_DIM : (h + 1) * HEAD_DIM], h) for h in heads], axis=1)


def head_rows(rows, head):
    width = rows.shape[1]
    at = (head * HEAD_DIM) % GROUP
    parts = []
    if at:
        parts.append(jnp.zeros((at, width), rows.dtype))
    parts.append(rows)
    if at + HEAD_DIM < GROUP:
        parts.append(jnp.zeros((GROUP - at - HEAD_DIM, width), rows.dtype))
    return jnp.concatenate(parts, axis=0)


def unpack_points_kernel(cap, peers, direct, *refs):
    if not direct:
        recv_ref, high_ref, low_ref = refs[:3]
        recv = recv_ref[...]
        high_rows, low_rows = high_ref[...], low_ref[...]
    else:
        msg_ref = refs[0]
        left = msg_ref[:, :cap, :].reshape(peers * cap, 128)
        right = msg_ref[:, cap : 2 * cap, :].reshape(peers * cap, 128)
        recv = jnp.concatenate([left, right], axis=1)
        tails = [msg_ref[peer, 2 * cap :, :].astype(F32) for peer in range(peers)]
        high_rows = jnp.concatenate([tail[0:1] for tail in tails], axis=0)
        low_rows = jnp.concatenate([tail[1:2] for tail in tails], axis=0)
    gather_ref, place_ref, rotated_ref = refs[-3:]
    rows = rotated_ref.shape[1]
    slots = peers * cap
    targets = (high_rows - 1.0) * 16.0 + low_rows
    per_row = 128 // cap
    own_lane = iota((per_row, 128), 1) // cap == iota((per_row, 128), 0)
    pieces = []
    for group in range(slots // 128):
        block = targets[group * per_row : (group + 1) * per_row]
        pieces.append(jnp.sum(jnp.where(own_lane, block, 0.0), axis=0, keepdims=True))
    target = jnp.concatenate(pieces, axis=1)
    gather = one_hot(target.astype(jnp.int32), (rows, slots), 0)
    gather_ref[...] = gather
    rotated_ref[...] = mm(gather, recv).T
    place_ref[...] = one_hot(lane_tile(column_of(target).astype(jnp.int32), rows), (slots, rows), 1)


def forward_kernel(
    rotated_ref, w_qkv_ref, w_out_ref, w_up_ref, gain_attn_ref, gain_mlp_ref,
    qkv_t_ref, kv_ref, scales_ref, norm_one_ref, normed_one_ref, attended_ref, norm_two_ref, normed_two_ref,
    hidden_ref, slope_ref, gain_attn_col_ref, gain_mlp_col_ref, *probs_refs,
):
    rot_t = rotated_ref[...]
    width, rows = rot_t.shape
    gain_attn_col = column_of(gain_attn_ref[...])
    gain_attn_col_ref[...] = gain_attn_col
    gain_mlp_col = column_of(gain_mlp_ref[...])
    gain_mlp_col_ref[...] = gain_mlp_col
    scale_one = lax.rsqrt(jnp.mean(rot_t * rot_t, axis=0, keepdims=True) + EPSILON)
    norm_one = rot_t * scale_one
    norm_one_ref[...] = norm_one
    normed_one = (norm_one * lane_tile(gain_attn_col, rows)).astype(BF16)
    normed_one_ref[...] = normed_one
    qkv_t = mm_tn(w_qkv_ref[...], normed_one).astype(BF16)
    qkv_t_ref[...] = qkv_t
    kv_ref[...] = qkv_t[width:].astype(F32).T.astype(BF16)

    for ball in range(rows // BALL):
        at = ball * BALL
        cols = slice(at, at + BALL)
        for group in range(0, width, GROUP):
            queries = group_heads(qkv_t_ref[group : group + GROUP, cols])
            scores = mm(kv_ref[cols, group : group + GROUP], queries) * ATT_SCALE
            top = jnp.max(scores, axis=0, keepdims=True)
            weights = jnp.exp(scores - top)
            probs = weights * (1.0 / jnp.sum(weights, axis=0, keepdims=True))
            probs_refs[ball][group // GROUP] = probs
            probs_low = probs.astype(BF16)
            for head in range(GROUP // HEAD_DIM):
                own = slice(group + head * HEAD_DIM, group + (head + 1) * HEAD_DIM)
                values = qkv_t_ref[2 * width + own.start : 2 * width + own.stop, cols]
                attended_ref[own, cols] = mm(values, probs_low[:, head * BALL : (head + 1) * BALL]).astype(BF16)

    middle = rot_t + mm_tn(w_out_ref[...], attended_ref[...])
    scale_two = lax.rsqrt(jnp.mean(middle * middle, axis=0, keepdims=True) + EPSILON)
    norm_two = middle * scale_two
    norm_two_ref[...] = norm_two
    normed_two = (norm_two * lane_tile(gain_mlp_col, rows)).astype(BF16)
    normed_two_ref[...] = normed_two
    scales_ref[...] = jnp.where(iota(scales_ref.shape, 0) == 0, scale_one, scale_two)
    step = 256
    for at in range(0, hidden_ref.shape[0], step):
        pre_act = mm_tn(w_up_ref[:, at : at + step], normed_two)
        square = pre_act * pre_act
        tanh_val = jnp.tanh(GELU_COEF * (pre_act + 0.044715 * pre_act * square))
        half = 0.5 * (1.0 + tanh_val)
        hidden_ref[at : at + step, :] = (pre_act * half).astype(BF16)
        slope_ref[at : at + step, :] = half + 0.5 * pre_act * (1.0 - tanh_val * tanh_val) * (
            GELU_COEF * (1.0 + 3.0 * 0.044715 * square)
        )


def norm_backward(grad_normed, norm, scale, gain):
    inner = grad_normed * gain
    return scale * (inner - norm * jnp.mean(inner * norm, axis=0, keepdims=True))


def gain_row(product):
    width = product.shape[1]
    partial = product[:, :128]
    for at in range(128, width, 128):
        partial = partial + product[:, at : at + 128]
    return jnp.sum(partial.T, axis=0, keepdims=True)


def place_blocks(blocks_ref, values, first_row, leaf_size, sample_size):
    step = values.shape[0] // (leaf_size * sample_size)
    for block in range(leaf_size * sample_size):
        leaf, sample = divmod(block, sample_size)
        blocks_ref[sample, leaf, first_row : first_row + step, :] = values[block * step : (block + 1) * step]


def part_blocks(blocks_ref, keep_ref, send_ref):
    low = lax.rem(lax.axis_index("sample"), 2)
    for high in range(keep_ref.shape[0]):
        keep_ref[high] = blocks_ref[2 * high + low]
        send_ref[high] = blocks_ref[2 * high + 1 - low].astype(BF16)


def mlp_weights_kernel(
    arranged, direct, gather_ref, hidden_ref, slope_ref, normed_two_ref, w_down_ref, *refs
):
    width, rows = normed_two_ref.shape
    if direct:
        mine_ref, mate_ref, *refs, landing_ref = refs
        for step in range(mine_ref.shape[0]):
            landing_ref[partner(2 * step)] = mine_ref[step]
            landing_ref[partner(2 * step + 1)] = mate_ref[step]
        recv_ref = landing_ref
    else:
        recv_ref, *refs = refs
    grad_pre_ref, cot_t_ref, *mat_refs = refs
    recv = recv_ref[...].reshape(-1, width)
    cot_f = mm(gather_ref[...], recv)
    cot = cot_f.astype(BF16)
    cot_t = cot_f.T
    cot_t_ref[...] = cot_t
    cot_t_low = cot_t.astype(BF16)
    normed_two = normed_two_ref[...]
    step = 256
    if arranged:
        keep_ref, send_ref, blocks_ref = mat_refs
        leaf_size, sample_size = lax.axis_size("leaf"), lax.axis_size("sample")
        up_rows = width // leaf_size
        down_rows = hidden_ref.shape[0] // (leaf_size * sample_size)
    else:
        grad_up_ref, grad_down_ref = mat_refs
    for at in range(0, hidden_ref.shape[0], step):
        grad_down = mm(hidden_ref[at : at + step, :], cot)
        grad_pre = (mm(w_down_ref[at : at + step, :], cot_t_low) * slope_ref[at : at + step, :]).astype(BF16)
        grad_pre_ref[at : at + step, :] = grad_pre
        grad_up = mm_nt(normed_two, grad_pre)
        if arranged:
            for leaf in range(leaf_size):
                blocks_ref[at // step, leaf, :up_rows, :] = grad_up[leaf * up_rows : (leaf + 1) * up_rows]
            for block in range(step // down_rows):
                leaf, sample = divmod(at // down_rows + block, sample_size)
                piece = grad_down[block * down_rows : (block + 1) * down_rows]
                blocks_ref[sample, leaf, up_rows:, :] = piece
        else:
            grad_down_ref[at : at + step, :] = grad_down.astype(BF16)
            grad_up_ref[:, at : at + step] = grad_up.astype(BF16)
    if arranged:
        part_blocks(blocks_ref, keep_ref, send_ref)


def mlp_inputs_kernel(
    grad_pre_ref, cot_t_ref, norm_two_ref, scales_ref, attended_ref, w_up_ref, w_out_ref, gain_mlp_ref,
    grad_gain_ref, grad_middle_ref, grad_att_ref, grad_out_ref,
):
    grad_normed = mm(w_up_ref[...], grad_pre_ref[...])
    norm_two = norm_two_ref[...]
    grad_gain_ref[...] = gain_row(grad_normed * norm_two)
    gain = lane_tile(gain_mlp_ref[...], norm_two.shape[1])
    grad_middle = cot_t_ref[...] + norm_backward(grad_normed, norm_two, scales_ref[1:2, :], gain)
    grad_middle_ref[...] = grad_middle
    grad_middle_low = grad_middle.astype(BF16)
    grad_att_ref[...] = mm(w_out_ref[...], grad_middle_low).astype(BF16)
    grad_out_ref[...] = mm_nt(attended_ref[...], grad_middle_low)


def ball_backward(ball, qkv_t_ref, kv_ref, probs_ref, grad_att_ref, grad_rows_ref):
    width = qkv_t_ref.shape[0] // 3
    cols = slice(ball * BALL, (ball + 1) * BALL)
    for group in range(0, width, GROUP):
        upstream = grad_att_ref[group : group + GROUP, cols]
        probs = probs_ref[group // GROUP]
        grad_probs = mm(kv_ref[cols, width + group : width + group + GROUP], group_heads(upstream))
        delta = jnp.sum(grad_probs * probs, axis=0, keepdims=True)
        grad_scores = (probs * (grad_probs - delta)).astype(BF16)
        probs_low = probs.astype(BF16)
        for head in range(GROUP // HEAD_DIM):
            first = group + head * HEAD_DIM
            own, own_key, own_value = (slice(at + first, at + first + HEAD_DIM) for at in (0, width, 2 * width))
            part = slice(head * BALL, (head + 1) * BALL)
            scores_of = grad_scores[:, part]
            grad_rows_ref[own, cols] = (mm(qkv_t_ref[own_key, cols], scores_of) * ATT_SCALE).astype(BF16)
            grad_rows_ref[own_key, cols] = (mm_nt(qkv_t_ref[own, cols], scores_of) * ATT_SCALE).astype(BF16)
            grad_rows_ref[own_value, cols] = mm_nt(grad_att_ref[own, cols], probs_low[:, part]).astype(BF16)


def attention_backward_kernel(
    arranged,
    qkv_t_ref, kv_ref, scales_ref, grad_att_ref, grad_middle_ref, norm_one_ref, normed_one_ref,
    w_qkv_ref, gain_attn_ref, place_ref, gain_two_ref, grad_out_ref, *refs,
):
    width, rows = norm_one_ref.shape
    probs_refs, refs = refs[: rows // BALL], refs[rows // BALL :]
    back_ref, *mat_refs, grad_rows_ref = refs
    for ball, probs_ref in enumerate(probs_refs):
        ball_backward(ball, qkv_t_ref, kv_ref, probs_ref, grad_att_ref, grad_rows_ref)
    grad_rows = grad_rows_ref[...]
    grad_normed = mm(w_qkv_ref[...], grad_rows)
    norm_one = norm_one_ref[...]
    gain_one = gain_row(grad_normed * norm_one)
    gain = lane_tile(gain_attn_ref[...], rows)
    grad_rot = grad_middle_ref[...] + norm_backward(grad_normed, norm_one, scales_ref[0:1, :], gain)
    back_ref[...] = mm_nt(place_ref[...], grad_rot.astype(BF16)).astype(BF16)
    normed_one = normed_one_ref[...]
    if not arranged:
        mat_refs[0][...] = mm_nt(normed_one, grad_rows).astype(BF16)
        mat_refs[1][...] = gain_one
        return
    keep_ref, send_ref, blocks_ref = mat_refs
    leaf_size, sample_size = lax.axis_size("leaf"), lax.axis_size("sample")
    step = width // (leaf_size * sample_size)
    for col in range(3):
        grad_qkv = mm_nt(normed_one, grad_rows[col * width : (col + 1) * width])
        place_blocks(blocks_ref, grad_qkv, (1 + col) * step, leaf_size, sample_size)
    place_blocks(blocks_ref, grad_out_ref[...], 0, leaf_size, sample_size)
    row = iota((GAINS, width), 0)
    gains = jnp.where(row == 0, gain_one, jnp.where(row == 1, gain_two_ref[...], 0.0))
    for sample in range(sample_size):
        for leaf in range(leaf_size):
            blocks_ref[sample, leaf, 4 * step :, :] = gains
    part_blocks(blocks_ref, keep_ref, send_ref)


def unpack_kernel(slot_ref, returned_ref, out_ref):
    slots = returned_ref.shape[0]
    slot_col = column_of(slot_ref[...].astype(F32)).astype(jnp.int32)
    place = one_hot(lane_tile(slot_col, slots), (out_ref.shape[0], slots), 1)
    out_ref[...] = mm(place, returned_ref[...]).astype(BF16)


def halve_kernel(axis, bit, keep_ref, got_ref, keep_out_ref, send_out_ref):
    mine = lax.rem(lax.div(lax.axis_index(axis), bit), 2)
    for high in range(keep_out_ref.shape[0]):
        for ref, at in ((keep_out_ref, 2 * high + mine), (send_out_ref, 2 * high + 1 - mine)):
            ref[high] = (keep_ref[at] + got_ref[at].astype(F32)).astype(ref.dtype)


def quarter_kernel(keep_ref, got_ref, keep_out_ref, *send_refs):
    mine = lax.rem(lax.div(lax.axis_index("sample"), 2), 2)
    low = lax.rem(lax.axis_index("leaf"), 2)
    places = ((mine, low), (1 - mine, low), (mine, 1 - low), (1 - mine, 1 - low))
    for ref, (sample, leaf) in zip((keep_out_ref, *send_refs), places):
        for high in range(ref.shape[0]):
            total = keep_ref[sample, 2 * high + leaf] + got_ref[sample, 2 * high + leaf].astype(F32)
            ref[high] = total.astype(ref.dtype)


def join_kernel(counts, *refs):
    ins, (keep_out_ref, send_out_ref) = list(refs[:-2]), refs[-2:]
    mine = lax.rem(lax.div(lax.axis_index("leaf"), 2), 2)
    start = 0
    for count in counts:
        part, ins = ins[:count], ins[count:]
        rows = pl.ds(start, part[0].shape[1])
        for ref, at in ((keep_out_ref, mine), (send_out_ref, 1 - mine)):
            total = part[0][at]
            for got_ref in part[1:]:
                total = total + got_ref[at].astype(F32)
            ref[rows, :] = total.astype(ref.dtype)
        start += part[0].shape[1]


def finish_kernel(keep_ref, got_ref, low_ref, gains_ref):
    total = keep_ref[...] + got_ref[...].astype(F32)
    gains_ref[...] = total[-GAINS:]
    low_ref[0] = total[:-GAINS].astype(BF16)


def assemble_kernel(scale, offsets, mine_ref, mate_ref, up_ref, down_ref, out_ref, qkv_ref):
    size = 2 * len(offsets)
    width = mine_ref.shape[2]
    up_rows, down_rows, out_rows = up_ref.shape[0], down_ref.shape[0] // size, out_ref.shape[0] // size
    me = lax.axis_index("sample")

    def block(source, count):
        return pl.ds(pl.multiple_of(source * count, count), count)

    for index, offset in enumerate(offsets):
        for mate, ref in enumerate((mine_ref, mate_ref)):
            source = me ^ (offset + mate)
            part = ref[index].astype(F32) * scale
            at = up_rows
            up_ref[:, block(source, width)] = part[:at]
            down_ref[block(source, down_rows), :] = part[at : at + down_rows]
            at += down_rows
            out_ref[block(source, out_rows), :] = part[at : at + out_rows]
            at += out_rows
            for col in range(3):
                qkv_ref[block(source, out_rows), col * width : (col + 1) * width] = part[at : at + out_rows]
                at += out_rows


def permute(value, axis, size, bit):
    return lax.ppermute(value, axis, [(i, i ^ bit) for i in range(size)])


def halve(keep, got, axis, bit, name, micros=0.5):
    shape = (keep.shape[0] // 2,) + keep.shape[1:]
    return call(functools.partial(halve_kernel, axis, bit), [(shape, F32), (shape, BF16)], name, micros, keep, got)


def call(kernel, outs, name, micros, *args, scratch=(), hbm_in=False, hbm_out=False, raw_in=0, raw_out=0, blocked=False, limit=16):
    moved = sum(arg.size * arg.dtype.itemsize for arg in args)
    moved += sum(math.prod(shape) * jnp.dtype(dtype).itemsize for shape, dtype in outs)
    vmem = pl.BlockSpec() if blocked else pl.BlockSpec(memory_space=pltpu.VMEM)
    hbm = pl.BlockSpec(memory_space=pltpu.HBM)
    copied_in = len(args) - raw_in if hbm_in else 0
    copied_out = len(outs) - raw_out if hbm_out else 0
    parts = 2

    def body(*refs):
        ins, refs = list(refs[: len(args)]), refs[len(args) :]
        results, refs = list(refs[: len(outs)]), refs[len(outs) :]
        own, refs = refs[: len(scratch)], refs[len(scratch) :]
        in_bufs, refs = refs[:copied_in], refs[copied_in:]
        out_bufs, refs = refs[:copied_out], refs[copied_out:]
        for at, buf in enumerate(in_bufs):
            copy = pltpu.make_async_copy(ins[at], buf, refs[0].at[at])
            copy.start()
            ins[at] = Arriving(buf, [copy])
        for at, buf in enumerate(out_bufs):
            results[at] = Leaving(buf, results[at], refs[-1].at[at])
        kernel(*ins, *results, *own)
        for ref in ins:
            if isinstance(ref, Arriving):
                for copy in ref.copies:
                    copy.wait()
        for ref in results[:copied_out]:
            ref.send()
        for ref in results[:copied_out]:
            for copy in ref.copies:
                copy.wait()

    extra = [pltpu.VMEM(arg.shape, arg.dtype) for arg in args[:copied_in]]
    extra += [pltpu.VMEM(shape, dtype) for shape, dtype in outs[:copied_out]]
    if copied_in:
        extra.append(pltpu.SemaphoreType.DMA((copied_in,)))
    if copied_out:
        extra.append(pltpu.SemaphoreType.DMA((copied_out, parts)))
    return pl.pallas_call(
        body,
        out_shape=[jax.ShapeDtypeStruct(shape, dtype) for shape, dtype in outs],
        in_specs=[hbm if hbm_in else vmem] * (len(args) - raw_in) + [hbm] * raw_in,
        out_specs=[hbm if hbm_out else vmem] * (len(outs) - raw_out) + [hbm] * raw_out,
        scratch_shapes=list(scratch) + extra,
        compiler_params=pltpu.CompilerParams(vmem_limit_bytes=limit * 1024 * 1024),
        cost_estimate=pl.CostEstimate(flops=int(micros * 1.1e9), bytes_accessed=moved, transcendentals=0),
        name=name,
    )(*args)


def exchange(flat, axes, peers):
    moved = lax.all_to_all(
        flat.reshape((peers, -1) + flat.shape[1:]), axes, split_axis=0, concat_axis=0, tiled=True
    )
    return moved.reshape(flat.shape)


def local(points, cotangent, dest_pos, w_qkv, w_out, w_up, w_down, gain_attn, gain_mlp):
    rows, width = points.shape
    hidden_width = w_up.shape[1]
    axes = ("leaf", "sample")
    peers = lax.axis_size(axes)
    leaf_size, sample_size = lax.axis_size("leaf"), lax.axis_size("sample")
    cap = 2 * rows // peers
    slots = peers * cap
    balls = rows // BALL
    direct = cap % 16 == 0
    paired = leaf_size & (leaf_size - 1) == 0 and sample_size & (sample_size - 1) == 0 and min(leaf_size, sample_size) > 1
    arranged = paired and width % (16 * peers) == 0 and hidden_width == sample_size * width and (leaf_size, sample_size) == (4, 4)
    inv_root = 1.0 / math.sqrt(rows * peers)

    msg_rows = 2 * cap + META
    if direct:
        outs = [((peers, msg_rows, 128), BF16)]
    else:
        outs = [((slots, width), BF16), ((peers, 128), F32), ((peers, 128), F32)]
    slot, *message = call(
        functools.partial(pack_points_kernel, peers, cap, direct),
        [((1, rows), jnp.int32)] + outs, "pack_points", 2, dest_pos.reshape(1, rows), points, hbm_in=True, hbm_out=True, limit=60,
    )
    if direct:
        forward_args = [exchange(message[0].reshape(-1, 128), axes, peers).reshape(peers, msg_rows, 128)]
    else:
        packed, high, low = message
        tail = jnp.stack([high, low], axis=1).astype(BF16)
        halves = packed.reshape(peers, cap, 2, 128).transpose(0, 2, 1, 3).reshape(peers, 2 * cap, 128)
        flat = jnp.concatenate([halves, tail], axis=1).reshape(-1, 128)
        arrived = exchange(flat, axes, peers).reshape(peers, 2 * cap + 2, 128)
        halves = arrived[:, : 2 * cap].reshape(peers, 2, cap, 128).transpose(0, 2, 1, 3).reshape(slots, width)
        forward_args = [halves, arrived[:, 2 * cap].astype(F32), arrived[:, 2 * cap + 1].astype(F32)]
    by_permute = direct and paired and peers <= 16
    if by_permute:
        packed_cot = call(
            pack_cot_kernel, [((2, cap, width), BF16)] * (peers // 2), "pack_cot", 1, slot, cotangent,
            scratch=[pltpu.VMEM((peers, cap, width), BF16)],
        )
        pairs = [packed_cot[0]] + [permute(packed_cot[step], axes, peers, 2 * step) for step in range(1, peers // 2)]
        *pairs[1:3], forward_args[0] = lax.optimization_barrier((*pairs[1:3], forward_args[0]))
    else:
        (packed_cot,) = call(pack_cot_kernel, [((slots, width), BF16)], "pack_cot", 1, slot, cotangent)
        arrived_cot = [exchange(packed_cot, axes, peers)]
    gather, place, rotated = call(
        functools.partial(unpack_points_kernel, cap, peers, direct),
        [((rows, slots), BF16), ((slots, rows), BF16), ((width, rows), F32)],
        "unpack_points", 2, *forward_args,
    )
    (
        qkv_t, kv, scales, norm_one, normed_one, attended, norm_two, normed_two, hidden, slope,
        gain_attn_col, gain_mlp_col, *probs,
    ) = call(
        forward_kernel,
        [
            ((3 * width, rows), BF16), ((rows, 2 * width), BF16), ((8, rows), F32),
            ((width, rows), F32), ((width, rows), BF16), ((width, rows), BF16),
            ((width, rows), F32), ((width, rows), BF16),
            ((hidden_width, rows), BF16), ((hidden_width, rows), F32), ((width, 128), F32), ((width, 128), F32),
        ] + [((width // GROUP, BALL, GROUP // HEAD_DIM * BALL), F32)] * balls,
        "forward", 7, rotated, w_qkv, w_out, w_up, gain_attn.reshape(1, width), gain_mlp.reshape(1, width),
    )
    if by_permute:
        scales, *pairs = lax.optimization_barrier((scales, *pairs))
        half = ((peers // 2, cap, width), BF16)
        mine, for_mate = call(regroup_kernel, [half] * 2, "regroup", 0.3, *pairs)
        arrived_cot = [mine, permute(for_mate, axes, peers, 1)]
    mlp_scratch, qkv_scratch = [], []
    if arranged:
        halved = (sample_size // 2, leaf_size)
        mlp_rows = width // leaf_size + hidden_width // peers
        qkv_rows = 4 * width // peers + GAINS
        mlp_mats = [(halved + (mlp_rows, width), F32), (halved + (mlp_rows, width), BF16)]
        qkv_mats = [(halved + (qkv_rows, width), F32), (halved + (qkv_rows, width), BF16)]
        mlp_scratch = [pltpu.VMEM((sample_size, leaf_size, mlp_rows, width), F32)]
        qkv_scratch = [pltpu.VMEM((sample_size, leaf_size, qkv_rows, width), F32)]
    else:
        mlp_mats = [(w_up.shape, BF16), (w_down.shape, BF16)]
        qkv_mats = [(w_qkv.shape, BF16), ((1, width), F32)]
    grad_pre, cot_t, *mlp_grads = call(
        functools.partial(mlp_weights_kernel, arranged, by_permute),
        [((hidden_width, rows), BF16), ((width, rows), F32)] + mlp_mats,
        "mlp_weights", 2.5, gather, hidden, slope, normed_two, w_down, *arrived_cot,
        scratch=mlp_scratch + ([pltpu.VMEM((peers, cap, width), BF16)] if by_permute else []),
    )
    gain_two, grad_middle, grad_att, grad_out = call(
        mlp_inputs_kernel,
        [((1, width), F32), ((width, rows), F32), ((width, rows), BF16), ((width, width), F32)],
        "mlp_inputs", 1.5, grad_pre, cot_t, norm_two, scales, attended, w_up, w_out, gain_mlp_col,
    )
    if arranged:
        keep_mlp, send_mlp = mlp_grads
        got_mlp = permute(send_mlp, "sample", sample_size, 1)
        bit = 2
        while bit < sample_size:
            keep_mlp, send_mlp = halve(keep_mlp, got_mlp, "sample", bit, "halve_mlp")
            grad_att, send_mlp = lax.optimization_barrier((grad_att, send_mlp))
            got_mlp = permute(send_mlp, "sample", sample_size, bit)
            bit *= 2
    back, *qkv_grads = call(
        functools.partial(attention_backward_kernel, arranged),
        [((slots, width), BF16)] + qkv_mats, "attention_backward", 6,
        qkv_t, kv, scales, grad_att, grad_middle, norm_one, normed_one,
        w_qkv, gain_attn_col, place, gain_two, grad_out, *probs,
        scratch=qkv_scratch + [pltpu.VMEM((3 * width, rows), BF16)],
    )
    if not arranged:
        returned = exchange(back, axes, peers)
        (grad_points,) = call(unpack_kernel, [((rows, width), BF16)], "unpack", 1, slot, returned, blocked=True)
        up_sum, down_sum, out_sum = reduce_mats([*mlp_grads, grad_out])
        qkv_sum, gain_sum = reduce_mats([qkv_grads[0]], jnp.concatenate([qkv_grads[1], gain_two], axis=0))
        return (
            grad_points, qkv_sum * inv_root, out_sum * inv_root, up_sum * inv_root, down_sum * inv_root,
            gain_sum[0] * inv_root, gain_sum[1] * inv_root,
        )
    keep_qkv, send_qkv = qkv_grads
    got_qkv = permute(send_qkv, "sample", sample_size, 1)
    keep_mlp, leaving = halve(keep_mlp[0], got_mlp[0], "leaf", 1, "leaf_mlp", 1.0)
    got_qkv, leaving = lax.optimization_barrier((got_qkv, leaving))
    quarter = (leaf_size // 2, qkv_rows, width)
    keep_qkv, send_sample, send_leaf, send_both = call(
        quarter_kernel, [(quarter, F32)] + [(quarter, BF16)] * 3, "quarter_qkv", 0.5, keep_qkv, got_qkv
    )
    back = lax.optimization_barrier((back, leaving, send_sample))[0]
    returned = exchange(back, axes, peers)
    (grad_points,) = call(unpack_kernel, [((rows, width), BF16)], "unpack", 1, slot, returned, blocked=True)
    joined = (mlp_rows + qkv_rows, width)
    keep, leaving = call(
        functools.partial(join_kernel, (2, 4)), [(joined, F32), (joined, BF16)], "leaf_last", 0.5,
        keep_mlp, permute(leaving, "leaf", leaf_size, 1), keep_qkv,
        permute(send_sample, "sample", sample_size, 2),
        permute(send_leaf, "leaf", leaf_size, 1),
        permute(send_both, axes, peers, sample_size + 2),
    )
    got = permute(leaving, "leaf", leaf_size, 2)
    low, gains = call(
        finish_kernel, [((1, mlp_rows + qkv_rows - GAINS, width), BF16), ((GAINS, width), F32)], "finish", 3.5, keep, got
    )
    offsets = [0]
    bit = sample_size // 2
    while bit > 1:
        low = jnp.concatenate([low, permute(low, "sample", sample_size, bit)], axis=0)
        offsets += [offset ^ bit for offset in offsets]
        bit //= 2
    mate = permute(low, "sample", sample_size, 1)
    share = width // leaf_size
    gains = lax.dynamic_slice(gains, (0, lax.axis_index("leaf") * share), (2, share)) * inv_root
    gain_one, gain_two = gains[0], gains[1]
    gain_one, gain_two, mate = lax.optimization_barrier((gain_one, gain_two, mate))
    up_sum, down_sum, out_sum, qkv_sum = call(
        functools.partial(assemble_kernel, inv_root, offsets),
        [
            ((share, hidden_width), F32), ((hidden_width // leaf_size, width), F32), ((share, width), F32),
            ((share, 3 * width), F32),
        ],
        "assemble", 1, low, mate, blocked=True,
    )
    return (grad_points, qkv_sum, out_sum, up_sum, down_sum, gain_one, gain_two)


def reduce_mats(mats, gains=None):
    leaf_size = lax.axis_size("leaf")
    sample_size = lax.axis_size("sample")
    me = lax.axis_index("sample")
    pieces = []
    for mat in mats:
        pieces.append(mat.reshape(leaf_size, sample_size, -1, 128).transpose(1, 0, 2, 3))
    if gains is not None:
        gain_block = gains.reshape(2, leaf_size, -1).transpose(1, 0, 2).reshape(1, leaf_size, 1, -1)
        gain_block = jnp.pad(gain_block, ((0, 0), (0, 0), (0, 15), (0, 128 - gain_block.shape[3])))
        pieces.append(jnp.broadcast_to(gain_block, (sample_size,) + gain_block.shape[1:]))
    current = jnp.concatenate(pieces, axis=2).astype(jnp.bfloat16)
    bit = 1
    while bit < sample_size:
        split = current.reshape((current.shape[0] // 2, 2) + current.shape[1:])
        mine = (me // bit) % 2
        keep = lax.dynamic_index_in_dim(split, mine, 1, keepdims=False)
        send = lax.dynamic_index_in_dim(split, 1 - mine, 1, keepdims=False)
        got = lax.ppermute(send, "sample", [(i, i ^ bit) for i in range(sample_size)])
        current = (keep.astype(jnp.float32) + got.astype(jnp.float32)).astype(jnp.bfloat16)
        bit *= 2
    current = lax.all_to_all(current[0], "leaf", split_axis=0, concat_axis=0, tiled=True)
    total = jnp.sum(current.astype(jnp.float32), axis=0)
    low = total.astype(jnp.bfloat16)
    gathered = jnp.zeros((sample_size,) + low.shape, jnp.bfloat16)
    for step in range(sample_size):
        got = low if step == 0 else lax.ppermute(low, "sample", [(i, i ^ step) for i in range(sample_size)])
        gathered = lax.dynamic_update_index_in_dim(gathered, got, me ^ step, 0)
    results = []
    start = 0
    for mat in mats:
        rows = mat.size // (leaf_size * sample_size * 128)
        part = gathered[:, start : start + rows].astype(jnp.float32)
        results.append(part.reshape(mat.shape[0] // leaf_size, mat.shape[1]))
        start += rows
    if gains is not None:
        width = gains.shape[1] // leaf_size
        results.append(total[start, : 2 * width].reshape(2, width))
    return results


def solution(mesh):
    in_specs = (
        P(("groups", "leaf", "sample"), None),
        P(("groups", "leaf", "sample"), None),
        P(("groups", "leaf", "sample")),
        P(),
        P(),
        P(),
        P(),
        P(),
        P(),
    )
    out_specs = (
        P(("groups", "leaf", "sample"), None),
        P(("groups", "leaf"), None),
        P(("groups", "leaf"), None),
        P(("groups", "leaf"), None),
        P(("groups", "leaf"), None),
        P(("groups", "leaf")),
        P(("groups", "leaf")),
    )
    return jax.shard_map(local, mesh=mesh, in_specs=in_specs, out_specs=out_specs, check_vma=False)
```
